32 devices in a mesh: batch: 8 (over y, x, core), tensor: 4 (over z).
Axes of the slice: x: 2, y: 2, z: 4, core: 2. Of those that a mesh axis runs over, the one named last changes fastest.
Arguments:
- tokens: bfloat16 [8192, 1024], P('batch'), may hold values from -6 to 6
- segment_ids: int32 [8, 1024], P('batch'), may hold values from 0 to 3, never falling along the last dimension, each value on 1 to 512 neighbouring positions
- attention_gain: float32 [1024], replicated, may hold values from 0.5 to 1.5
- attention_shift: float32 [1024], replicated, may hold values from -1.25 to 1.25
- joint_weight: bfloat16 [3, 1024, 1024], P(None, None, 'tensor'), may hold values from -0.1875 to 0.1875
- joint_bias: float32 [3, 1024], P(None, 'tensor'), may hold values from -1.75 to 1.75
- output_weight: bfloat16 [1024, 1024], P('tensor'), may hold values from -0.75 to 0.75
- output_bias: float32 [1024], replicated, may hold values from -1.75 to 1.75
- mixer_gain: float32 [1024], replicated, may hold values from 0.5 to 1.5
- mixer_shift: float32 [1024], replicated, may hold values from -1.25 to 1.25
- up_weight: bfloat16 [1024, 4096], P(None, 'tensor'), may hold values from -0.1875 to 0.1875
- up_bias: float32 [4096], P('tensor'), may hold values from -1.75 to 1.75
- down_weight: bfloat16 [4096, 1024], P('tensor'), may hold values from -0.125 to 0.125
- down_bias: float32 [1024], replicated, may hold values from -1.75 to 1.75
- prefix_table: float32 [10, 1024], replicated, may hold values from -6 to 6
- inner_weight: bfloat16 [1024, 512], replicated, may hold values from -0.1875 to 0.1875
- inner_bias: float32 [512], replicated, may hold values from -1.75 to 1.75
- outer_weight: bfloat16 [512, 2, 1024], P(None, None, 'tensor'), may hold values from -0.5 to 0.5
- outer_bias: float32 [2, 1024], P(None, 'tensor'), may hold values from -1.75 to 1.75
- cotangent: bfloat16 [8192, 1024], P('batch'), may hold values from -6 to 6
Outputs:
- block_output: bfloat16 [8192, 1024], P('batch', 'tensor')
- tokens_gradient: bfloat16 [8192, 1024], P('batch', 'tensor')
- attention_gain_gradient: float32 [1024], P('tensor')
- attention_shift_gradient: float32 [1024], P('tensor')
- joint_weight_gradient: float32 [3, 1024, 1024], P(None, 'batch', 'tensor')
- joint_bias_gradient: float32 [3, 1024], P(None, 'tensor')
- output_weight_gradient: float32 [1024, 1024], P('tensor', 'batch')
- output_bias_gradient: float32 [1024], P('tensor')
- mixer_gain_gradient: float32 [1024], P('tensor')
- mixer_shift_gradient: float32 [1024], P('tensor')
- up_weight_gradient: float32 [1024, 4096], P('batch', 'tensor')
- up_bias_gradient: float32 [4096], P('tensor')
- down_weight_gradient: float32 [4096, 1024], P('tensor', 'batch')
- down_bias_gradient: float32 [1024], P('tensor')
- prefix_table_gradient: float32 [10, 1024], replicated
- inner_weight_gradient: float32 [1024, 512], replicated
- inner_bias_gradient: float32 [512], replicated
- outer_weight_gradient: float32 [512, 2, 1024], P('batch', None, 'tensor')
- outer_bias_gradient: float32 [2, 1024], P(None, 'tensor')
The draws below stay inside these ranges and needn't reach their ends.
Inputs may be any that keep to these rules, and one draw needn't show every extreme that they name: `segment_ids`: along each packed row the ids never fall, and no segment holds more than half of 1024 tokens.
All inputs are finite; a program needn't handle non-finite values.
Results may differ from the reference program's by a relative error of at most 0.013.
Values sent between devices are 32-bit elements; how exact they have to be, the bound alone decides.
No kernel may reach another device: no remote copies, remote signals or barrier semaphores. Data moves between devices by JAX's collectives and lax.ppermute only.
A program may use at most 192 MiB of HBM per device.

```python
import functools
import math
import jax
import jax.numpy as jnp
import numpy as np
from jax import lax

D = 1024
H = 16
HD = 64
FF = 4096
PREFIX = 10
RHID = 512
SEQ = 1024
ROWS = 8
TOKENS = 8192


def block_levels(own_key, extent, cuts, smallest, top_value):
    gain = 1.0
    for dim, shards_of in cuts:
        heights = jax.random.uniform(jax.random.fold_in(jax.random.fold_in(own_key, 6), dim), (shards_of,), jnp.float32, smallest / len(cuts), top_value / len(cuts))
        gain = gain * jnp.repeat(jnp.exp(heights), extent[dim] // shards_of).reshape((-1,) + (1,) * (len(extent) - 1 - dim))
    return gain


def length_profile(amount, total, bound, skew):
    loads = [(1 << 20) // math.isqrt(grade ** skew) + 1 for grade in range(2, amount + 1)]
    rest, given = total - bound - (amount - 1), [1] * (amount - 1)
    while rest > 0:
        candidates = [i for i in range(amount - 1) if given[i] < bound]
        whole, budget = sum([loads[i] for i in candidates]), rest
        for i in candidates:
            extra = min(bound - given[i], max(1, budget * loads[i] // whole), rest)
            given[i] = given[i] + extra
            rest = rest - extra
    return np.array([bound] + given)


def uneven_parts(own_key, amount, total, limit, slope):
    if amount == 2:
        one = jax.random.randint(own_key, (), max(1, total - limit), min(limit, total - 1) + 1)
        return jnp.stack([one, total - one])
    sizes = jnp.asarray(length_profile(amount, total, limit, slope), jnp.int32)
    pairs = (amount - 1) // 2
    donor, taker = sizes[1:1 + 2 * pairs:2], sizes[2:2 + 2 * pairs:2]
    margin = jnp.minimum(donor - 1, limit - taker)
    shifted = jax.random.randint(jax.random.fold_in(own_key, 1), (pairs,), 0, 1 << 20) % (margin + 1)
    sizes = sizes.at[1:1 + 2 * pairs:2].set(donor - shifted).at[2:2 + 2 * pairs:2].set(taker + shifted)
    return sizes[jax.random.permutation(jax.random.fold_in(own_key, 2), amount)]


def centred(stream_key, dims, scale, reach, split=(), held_as=jnp.bfloat16):
    values = jax.random.normal(stream_key, dims, jnp.float32) * scale
    if len(split) > 0:
        values = block_levels(stream_key, dims, split, -0.22, 0.18) * values
    return jnp.clip(values, min=-reach, max=reach).astype(held_as)


def setup_inputs(seed: int = 0) -> dict:
    seeds = jax.random.split(jax.random.key(seed), 21)
    tokens = centred(seeds[0], (TOKENS, D), 1.0, 6.0, ((0, 8),))
    segment_ids = jax.vmap(lambda own: jnp.searchsorted(jnp.cumsum(uneven_parts(own, 4, SEQ, SEQ // 2, 0)), jnp.arange(SEQ), side="right"))(jax.random.split(seeds[1], ROWS)).reshape((ROWS, SEQ)).astype(jnp.int32)
    attention_gain = jnp.clip(1.0 + 0.1 * jax.random.normal(seeds[2], (D,), jnp.float32), 0.5, 1.5)
    attention_shift = centred(seeds[3], (D,), 0.2, 1.25, (), jnp.float32)
    joint_weight = centred(seeds[4], (3, D, D), D ** -0.5, 0.1875, ((2, 4),))
    joint_bias = centred(seeds[5], (3, D), 0.3, 1.75, ((1, 4),), jnp.float32)
    output_weight = centred(seeds[6], (D, D), (D // 16) ** -0.5, 0.75, ((0, 4),))
    output_bias = centred(seeds[7], (D,), 0.3, 1.75, (), jnp.float32)
    mixer_gain = jnp.clip(1.0 + 0.1 * jax.random.normal(seeds[8], (D,), jnp.float32), 0.5, 1.5)
    mixer_shift = centred(seeds[9], (D,), 0.2, 1.25, (), jnp.float32)
    up_weight = centred(seeds[10], (D, FF), D ** -0.5, 0.1875, ((1, 4),))
    up_bias = centred(seeds[11], (FF,), 0.3, 1.75, ((0, 4),), jnp.float32)
    down_weight = centred(seeds[12], (FF, D), (FF // 2) ** -0.5, 0.125, ((0, 4),))
    down_bias = centred(seeds[13], (D,), 0.3, 1.75, (), jnp.float32)
    prefix_table = centred(seeds[14], (PREFIX, D), 1.0, 6.0, (), jnp.float32)
    inner_weight = centred(seeds[15], (D, RHID), D ** -0.5, 0.1875)
    inner_bias = centred(seeds[16], (RHID,), 0.3, 1.75, (), jnp.float32)
    outer_weight = centred(seeds[17], (RHID, 2, D), (RHID // 4) ** -0.5, 0.5, ((2, 4),))
    outer_bias = centred(seeds[18], (2, D), 0.3, 1.75, ((1, 4),), jnp.float32)
    cotangent = centred(seeds[19], (TOKENS, D), 1.0, 6.0, ((0, 8),))
    return dict(tokens=tokens, segment_ids=segment_ids, attention_gain=attention_gain, attention_shift=attention_shift, joint_weight=joint_weight, joint_bias=joint_bias, output_weight=output_weight, output_bias=output_bias, mixer_gain=mixer_gain, mixer_shift=mixer_shift, up_weight=up_weight, up_bias=up_bias, down_weight=down_weight, down_bias=down_bias, prefix_table=prefix_table, inner_weight=inner_weight, inner_bias=inner_bias, outer_weight=outer_weight, outer_bias=outer_bias, cotangent=cotangent)


EPSILON = 1e-05
PRECISE = lax.Precision.HIGHEST
NEGATIVE = -1e+30

@jax.custom_vjp
def low(v):
    return lax.optimization_barrier(v.astype(jnp.bfloat16)).astype(jnp.float32)

@jax.custom_vjp
def low_back(v):
    return v

def low_keep(v):
    return (low(v), None)

def low_pass(kept, grad):
    return (grad,)

def back_keep(v):
    return (v, None)

def back_low(kept, grad):
    return (low(grad),)
low.defvjp(low_keep, low_pass)
low_back.defvjp(back_keep, back_low)

def normalize(values):
    centered = values - lax.optimization_barrier(jnp.mean(values, axis=-1, keepdims=True))
    return centered * lax.rsqrt(lax.optimization_barrier(jnp.mean(centered * centered, axis=-1, keepdims=True)) + EPSILON)

def split_heads(flat_rows):
    return flat_rows.reshape(flat_rows.shape[0], H, HD).transpose(1, 0, 2)

def block_forward(segment_ids, tokens, attention_gain, attention_shift, joint_weight, joint_bias, output_weight, output_bias, mixer_gain, mixer_shift, up_weight, up_bias, down_weight, down_bias, prefix_table, inner_weight, inner_bias, outer_weight, outer_bias):
    hidden_prefix = jnp.tanh(jnp.dot(prefix_table, inner_weight, precision=PRECISE) + inner_bias)
    prefix_pairs = jnp.einsum('pr,rke->pke', hidden_prefix, outer_weight, precision=PRECISE) + outer_bias
    prefix_pairs = low(prefix_pairs)
    prefix_keys = split_heads(prefix_pairs[:, 0])
    prefix_values = split_heads(prefix_pairs[:, 1])
    position = lax.broadcasted_iota(jnp.int32, (SEQ, SEQ), 0)
    causal = lax.broadcasted_iota(jnp.int32, (SEQ, SEQ), 1) <= position
    prefix_open = jnp.ones((SEQ, PREFIX), dtype=bool)

    def one_row(row_items):
        row_tokens, row_segments = row_items
        attention_in = low(normalize(row_tokens) * attention_gain + attention_shift)
        joint_proj = jnp.einsum('td,kde->tke', attention_in, joint_weight, precision=PRECISE) + joint_bias
        queries = low(low_back(joint_proj[:, 0] * HD ** (-0.5)))
        key_part = low(low_back(joint_proj[:, 1]))
        value_part = low(low_back(joint_proj[:, 2]))
        all_keys = jnp.concatenate([prefix_keys, split_heads(key_part)], axis=1)
        all_values = jnp.concatenate([prefix_values, split_heads(value_part)], axis=1)
        scores = low_back(jnp.einsum('hqd,hkd->hqk', split_heads(queries), all_keys, precision=PRECISE))
        same_doc = (row_segments[:, None] == row_segments[None, :]) & causal
        allowed = jnp.concatenate([prefix_open, same_doc], axis=1)
        scores = jnp.where(allowed[None], scores, NEGATIVE)
        weights = low(jax.nn.softmax(scores, axis=-1))
        attended = jnp.einsum('hqk,hkd->hqd', weights, all_values, precision=PRECISE)
        attended = low(low_back(attended.transpose(1, 0, 2).reshape(SEQ, D)))
        residual = row_tokens + low_back(jnp.dot(attended, output_weight, precision=PRECISE)) + output_bias
        mixer_in = low(normalize(residual) * mixer_gain + mixer_shift)
        pre_act = low_back(jnp.dot(mixer_in, up_weight, precision=PRECISE) + up_bias)
        activated = low(jax.nn.gelu(pre_act, approximate=True))
        return residual + jnp.dot(activated, down_weight, precision=PRECISE) + down_bias
    row_tokens = tokens.reshape(ROWS, SEQ, D)
    outputs = lax.map(jax.checkpoint(one_row), (row_tokens, segment_ids))
    return outputs.reshape(ROWS * SEQ, D)

def reference(tokens, segment_ids, attention_gain, attention_shift, joint_weight, joint_bias, output_weight, output_bias, mixer_gain, mixer_shift, up_weight, up_bias, down_weight, down_bias, prefix_table, inner_weight, inner_bias, outer_weight, outer_bias, cotangent):
    floats = [array.astype(jnp.float32) for array in (tokens, attention_gain, attention_shift, joint_weight, joint_bias, output_weight, output_bias, mixer_gain, mixer_shift, up_weight, up_bias, down_weight, down_bias, prefix_table, inner_weight, inner_bias, outer_weight, outer_bias)]
    forward = functools.partial(block_forward, segment_ids)
    output, pullback = jax.vjp(forward, *floats)
    gradients = pullback(cotangent.astype(jnp.float32))
    return (output.astype(jnp.bfloat16), gradients[0].astype(jnp.bfloat16), gradients[1], gradients[2], gradients[3], gradients[4], gradients[5], gradients[6], gradients[7], gradients[8], gradients[9], gradients[10], gradients[11], gradients[12], gradients[13], gradients[14], gradients[15], gradients[16], gradients[17])
```

```python
import functools

import jax
import jax.numpy as jnp
from jax import lax
from jax.experimental import pallas as pl
from jax.experimental.pallas import tpu as pltpu
from jax.sharding import PartitionSpec as P

HD = 64
GROUP = 4
WIDE = GROUP * HD
QB = 256
PAD = 16
TB = 256
EPSILON = 1e-05
PRECISE = lax.Precision.HIGHEST
NEGATIVE = -1e30
VMEM = 56 * 2**20
F32, BF16 = jnp.float32, jnp.bfloat16
NN = (((1,), (0,)), ((), ()))
NT = (((1,), (1,)), ((), ()))
TN = (((0,), (0,)), ((), ()))
TT = (((0,), (1,)), ((), ()))
shape_of = jax.ShapeDtypeStruct


def dot(a, b, dims=NN):
    return lax.dot_general(a, b, dims, preferred_element_type=F32)


def params(**kw):
    return pltpu.CompilerParams(vmem_limit_bytes=VMEM, **kw)


def normalize(values):
    centered = values - jnp.mean(values, axis=-1, keepdims=True)
    inverse = lax.rsqrt(jnp.mean(centered * centered, axis=-1, keepdims=True) + EPSILON)
    return centered * inverse, inverse


def heads_kernel(turn, member_ref, joint_ref, out_ref, own_ref, send_ref):
    for c in range(3):
        own_ref[c] = joint_ref[c].T
    own_ref[3] = out_ref[...]
    rows = own_ref.shape[1] // 8
    for p in range(2):
        member = member_ref[0] ^ (turn * p)
        start = pl.multiple_of(member * rows, rows)
        for c in range(4):
            send_ref[p, c * rows : (c + 1) * rows, :] = own_ref[c, pl.ds(start, rows), :].astype(F32)


def head_pieces(member, joint_weight, output_weight):
    _, width, local = joint_weight.shape
    vm = pl.BlockSpec(memory_space=pltpu.VMEM)
    return pl.pallas_call(
        functools.partial(heads_kernel, 6),
        out_shape=[shape_of((4, local, width), BF16), shape_of((2, local // 2, width), F32)],
        in_specs=[pl.BlockSpec(memory_space=pltpu.SMEM), vm, vm],
        out_specs=[vm, vm],
        compiler_params=params(),
        name="head_pieces",
    )(member, joint_weight, output_weight)


def hidden_kernel(member_ref, up_ref, down_ref, send_ref):
    rows = down_ref.shape[0]
    send_ref[0, 0:rows, :] = up_ref[...].T.astype(F32)
    send_ref[0, rows : 2 * rows, :] = down_ref[...].astype(F32)


def hidden_pieces(member, up_weight, down_weight):
    width, local = up_weight.shape
    rows = local // 8
    return pl.pallas_call(
        hidden_kernel,
        out_shape=shape_of((2, 2 * rows, width), F32),
        grid_spec=pltpu.PrefetchScalarGridSpec(
            num_scalar_prefetch=1,
            grid=(2,),
            in_specs=[
                pl.BlockSpec((width, rows), lambda p, m: (0, m[0] ^ (6 * p))),
                pl.BlockSpec((rows, width), lambda p, m: (m[0] ^ (6 * p), 0)),
            ],
            out_specs=pl.BlockSpec((1, 2 * rows, width), lambda p, m: (p, 0, 0)),
        ),
        compiler_params=params(),
        name="hidden_pieces",
    )(member, up_weight, down_weight)


def head_of_lane(rows):
    return lax.broadcasted_iota(jnp.int32, (rows, WIDE), 1) // HD


def first_key(i, length):
    return max(0, (i * QB - length // 2 + 1) // QB) * QB


def mask_tile(seg_col, seg_row, first, last, start):
    keys = lax.broadcasted_iota(jnp.int32, (last - first, QB), 0) + first
    asks = lax.broadcasted_iota(jnp.int32, (last - first, QB), 1) + start
    allowed = (seg_col == seg_row) & (keys <= asks)
    return jnp.where(allowed, 0.0, NEGATIVE)


def attend_kernel(merge, prefix_count, *refs):
    if merge:
        x_ref, mine_ref, theirs_ref, bias_ref, pk_ref, pv_ref, segc_ref, segr_ref, acc_ref = refs[:9]
        w_ref, q_ref, k_ref, v_ref, att_ref, lse_ref, out_ref, mask_ref, vt_ref = refs[9:]
        half = HD // 2
        for g in range(GROUP):
            for c in range(4):
                piece = slice(g * 4 * half + c * half, g * 4 * half + (c + 1) * half)
                w_ref[c, g * HD : g * HD + half, :] = mine_ref[piece, :].astype(BF16)
                w_ref[c, g * HD + half : (g + 1) * HD, :] = theirs_ref[piece, :].astype(BF16)
    else:
        tok_ref, gain_ref, shift_ref, w_ref, bias_ref, pk_ref, pv_ref, segc_ref, segr_ref, acc_ref = refs[:10]
        x_ref, q_ref, k_ref, v_ref, att_ref, lse_ref, out_ref, mask_ref, vt_ref = refs[10:]
        for t in range(0, tok_ref.shape[0], TB):
            normed, _ = normalize(tok_ref[t : t + TB, :].astype(F32))
            x_ref[t : t + TB, :] = (normed * gain_ref[...] + shift_ref[...]).astype(BF16)
    length = x_ref.shape[0]
    x = x_ref[...]
    q_ref[...] = ((dot(x, w_ref[0], NT) + bias_ref[0:1, :]) * HD ** (-0.5)).astype(BF16)
    k_ref[...] = (dot(x, w_ref[1], NT) + bias_ref[1:2, :]).astype(BF16)
    v_ref[...] = (dot(x, w_ref[2], NT) + bias_ref[2:3, :]).astype(BF16)
    vt_ref[...] = v_ref[...].T
    pvt = pv_ref[...].astype(BF16).T
    pk = pk_ref[...].astype(BF16)
    live = lax.broadcasted_iota(jnp.int32, (PAD, QB), 0) < prefix_count
    heads = head_of_lane(QB)
    for i in range(length // QB):
        first, last, rows = first_key(i, length), (i + 1) * QB, slice(i * QB, (i + 1) * QB)
        mask_ref[first:last, :] = mask_tile(segc_ref[first:last, :], segr_ref[:, rows], first, last, i * QB)
        for h in range(GROUP):
            span = slice(h * HD, (h + 1) * HD)
            asked = jnp.where(heads == h, q_ref[rows, :], jnp.zeros((), BF16))
            s = dot(k_ref[first:last, :], asked, NT) + mask_ref[first:last, :]
            sp = jnp.where(live, dot(pk, asked, NT), NEGATIVE)
            top = jnp.maximum(jnp.max(s, axis=0, keepdims=True), jnp.max(sp, axis=0, keepdims=True))
            e, ep = jnp.exp(s - top), jnp.exp(sp - top)
            total = jnp.sum(e, axis=0, keepdims=True) + jnp.sum(ep, axis=0, keepdims=True)
            o = dot(vt_ref[span, first:last], e.astype(BF16)) + dot(pvt[span, :], ep.astype(BF16))
            att_ref[span, rows] = (o / total).astype(BF16)
            lse_ref[h : h + 1, rows] = top + jnp.log(total)
    if merge:
        out_ref[...] = acc_ref[...] + dot(att_ref[...], w_ref[3], TN)
    else:
        for t in range(0, length, TB):
            base = tok_ref[t : t + TB, :].astype(F32) + acc_ref[...]
            out_ref[t : t + TB, :] = base + dot(att_ref[:, t : t + TB], w_ref[3], TN)


def attend_outs(length, width):
    return [shape_of((length, WIDE), BF16)] * 3 + [
        shape_of((WIDE, length), BF16),
        shape_of((GROUP, length), F32),
        shape_of((length, width), F32),
    ]


def attend(merge, prefix_count, length, width, args):
    first = shape_of((4, WIDE, width), BF16) if merge else shape_of((length, width), BF16)
    return pl.pallas_call(
        functools.partial(attend_kernel, merge, prefix_count),
        out_shape=[first] + attend_outs(length, width),
        scratch_shapes=[pltpu.VMEM((length, QB), F32), pltpu.VMEM((WIDE, length), BF16)],
        compiler_params=params(),
        name="attend_others" if merge else "attend_own",
    )(*args)


def back_kernel(own, prefix_count, own_start, *refs):
    w_ref, q_ref, k_ref, v_ref, att_ref, lse_ref, pk_ref, pv_ref, segc_ref, segr_ref, gr_ref = refs[:11]
    if own:
        gj_ref, gp_ref, out_ref, mask_ref, kt_ref, p_ref, ds_ref, do_ref, dot_ref, dqt_ref, dk_ref, dv_ref, qm_ref, gm_ref = refs[11:]
    else:
        acc_ref, out_ref, mask_ref, kt_ref, p_ref, ds_ref, do_ref, dot_ref, dqt_ref, dk_ref, dv_ref, qm_ref, gm_ref, gj_ref = refs[11:]
    length = q_ref.shape[0]
    do_ref[...] = dot(gr_ref[...], w_ref[3], NT).astype(BF16)
    dot_ref[...] = do_ref[...].T
    kt_ref[...] = k_ref[...].T
    pk, pv = pk_ref[...].astype(BF16), pv_ref[...].astype(BF16)
    pkt = pk.T
    live = lax.broadcasted_iota(jnp.int32, (PAD, QB), 0) < prefix_count
    heads = head_of_lane(QB)
    dk_ref[...] = jnp.zeros_like(dk_ref)
    dv_ref[...] = jnp.zeros_like(dv_ref)
    zero = jnp.zeros((), BF16)
    gpk = jnp.zeros((PAD, WIDE), F32)
    gpv = jnp.zeros((PAD, WIDE), F32)
    for i in range(length // QB):
        first, last, rows = first_key(i, length), (i + 1) * QB, slice(i * QB, (i + 1) * QB)
        mask_ref[first:last, :] = mask_tile(segc_ref[first:last, :], segr_ref[:, rows], first, last, i * QB)
        for h in range(GROUP):
            span, lanes = slice(h * HD, (h + 1) * HD), slice(h * QB, (h + 1) * QB)
            asked = jnp.where(heads == h, q_ref[rows, :], zero)
            grad = jnp.where(heads == h, do_ref[rows, :], zero)
            qm_ref[lanes, :] = asked
            gm_ref[lanes, :] = grad
            lse = lse_ref[h : h + 1, rows]
            delta = jnp.sum(dot_ref[span, rows].astype(F32) * att_ref[span, rows].astype(F32), axis=0, keepdims=True)
            p = jnp.exp(dot(k_ref[first:last, :], asked, NT) + mask_ref[first:last, :] - lse)
            p_ref[first:last, lanes] = p.astype(BF16)
            ds = (p * (dot(v_ref[first:last, :], grad, NT) - delta)).astype(BF16)
            ds_ref[first:last, lanes] = ds
            pp = jnp.exp(jnp.where(live, dot(pk, asked, NT), NEGATIVE) - lse)
            dsp = (pp * (dot(pv, grad, NT) - delta)).astype(BF16)
            dqt_ref[span, rows] = dot(kt_ref[span, first:last], ds) + dot(pkt[span, :], dsp)
            if own:
                gpk = gpk + dot(dsp, asked)
                gpv = gpv + dot(pp.astype(BF16), grad)
        dk_ref[first:last, :] += dot(ds_ref[first:last, :], qm_ref[...])
        dv_ref[first:last, :] += dot(p_ref[first:last, :], gm_ref[...])
    gj_ref[:, 0:WIDE] = dqt_ref[...].astype(BF16).T * jnp.asarray(HD ** (-0.5), BF16)
    gj_ref[:, WIDE : 2 * WIDE] = dk_ref[...].astype(BF16)
    gj_ref[:, 2 * WIDE : 3 * WIDE] = dv_ref[...].astype(BF16)
    part = dot(gj_ref[...], w_ref[0:3].reshape(3 * WIDE, w_ref.shape[2]))
    if own:
        gp_ref[0] = gpk
        gp_ref[1] = gpv
        out_ref[...] = part
    else:
        out_ref[...] = acc_ref[...] + part


def attend_back(own, prefix_count, args):
    length, width = args[10].shape
    outs = [shape_of((length, width), F32)]
    scratch = [
        pltpu.VMEM((length, QB), F32),
        pltpu.VMEM((WIDE, length), BF16),
        pltpu.VMEM((length, GROUP * QB), BF16),
        pltpu.VMEM((length, GROUP * QB), BF16),
        pltpu.VMEM((length, WIDE), BF16),
        pltpu.VMEM((WIDE, length), BF16),
        pltpu.VMEM((WIDE, length), F32),
        pltpu.VMEM((length, WIDE), F32),
        pltpu.VMEM((length, WIDE), F32),
        pltpu.VMEM((GROUP * QB, WIDE), BF16),
        pltpu.VMEM((GROUP * QB, WIDE), BF16),
    ]
    if own:
        outs = [shape_of((length, 3 * WIDE), BF16), shape_of((2, PAD, WIDE), F32)] + outs
    else:
        scratch = scratch + [pltpu.VMEM((length, 3 * WIDE), BF16)]
    return pl.pallas_call(
        functools.partial(back_kernel, own, prefix_count, 0),
        out_shape=outs,
        scratch_shapes=scratch,
        compiler_params=params(),
        name="back_own" if own else "back_others",
    )(*args)


def gelu_pair(v):
    c = 0.7978845608028654
    t = jnp.tanh(c * (v + 0.044715 * (v * v * v)))
    half = 0.5 * (1.0 + t)
    return v * half, half + 0.5 * v * (1.0 - t * t) * (c + (3.0 * 0.044715 * c) * (v * v))


def mix_own_kernel(z_ref, res_ref, cot_ref, gain_ref, shift_ref, up_ref, bias_ref, down_ref, dbias_ref,
                   mid_ref, act_ref, gp_ref, share_ref, gm_ref, bsum_ref):
    start = pl.multiple_of(z_ref[0] * share_ref.shape[1], share_ref.shape[1])
    own = pl.ds(start, share_ref.shape[1])
    normed, _ = normalize(res_ref[...])
    mid = (normed * gain_ref[...] + shift_ref[...]).astype(BF16)
    mid_ref[...] = mid
    act, slope = gelu_pair(dot(mid, up_ref[...]) + bias_ref[...])
    act = act.astype(BF16)
    act_ref[...] = act
    gp = (dot(cot_ref[...], down_ref[...], NT) * slope).astype(BF16)
    gp_ref[...] = gp
    share_ref[...] = res_ref[:, own] + dbias_ref[:, own] + dot(act, down_ref[:, own])
    gm_ref[...] = dot(gp, up_ref[...], NT)

    @pl.when(pl.program_id(0) == 0)
    def _():
        bsum_ref[...] = jnp.zeros_like(bsum_ref)

    bsum_ref[...] += jnp.sum(gp.astype(F32), axis=0, keepdims=True)


def mix_own(z, residual, cotangent, gain, shift, up, up_bias, down, down_bias, own_width):
    length, width = residual.shape
    hidden = up.shape[1]
    rows = lambda w: pl.BlockSpec((TB, w), lambda t: (t, 0))
    whole = lambda a: pl.BlockSpec(a.shape, lambda t: (0, 0), pipeline_mode=pl.Buffered(1))
    return pl.pallas_call(
        mix_own_kernel,
        grid=(length // TB,),
        in_specs=[
            pl.BlockSpec(memory_space=pltpu.SMEM),
            rows(width),
            rows(width),
            whole(gain),
            whole(shift),
            whole(up),
            whole(up_bias),
            whole(down),
            whole(down_bias),
        ],
        out_specs=[rows(width), rows(hidden), rows(hidden), rows(own_width), rows(width), pl.BlockSpec((1, hidden), lambda t: (0, 0))],
        out_shape=[
            shape_of((length, width), BF16),
            shape_of((length, hidden), BF16),
            shape_of((length, hidden), BF16),
            shape_of((length, own_width), F32),
            shape_of((length, width), F32),
            shape_of((1, hidden), F32),
        ],
        compiler_params=params(),
        name="mix_own",
    )(z, residual, cotangent, gain, shift, up, up_bias, down, down_bias)


def mix_kernel(pieces, z_ref, mid_ref, cot_ref, mine_ref, theirs_ref, bias_ref, share_in, gm_in, share_ref, gm_ref, up_ref, down_ref, part_ref):
    rows = mine_ref.shape[0] // pieces // 2
    start = pl.multiple_of(z_ref[0] * share_ref.shape[1], share_ref.shape[1])
    own = pl.ds(start, share_ref.shape[1])

    @pl.when(pl.program_id(0) == 0)
    def _():
        for g in range(pieces):
            for side, ref in enumerate((mine_ref, theirs_ref)):
                to = slice((2 * g + side) * rows, (2 * g + side + 1) * rows)
                up_ref[to, :] = ref[2 * g * rows : (2 * g + 1) * rows, :].astype(BF16)
                down_ref[to, :] = ref[(2 * g + 1) * rows : (2 * g + 2) * rows, :].astype(BF16)
        part_ref[...] = down_ref[:, own]

    mid = mid_ref[...]
    act, slope = gelu_pair(dot(mid, up_ref[...], NT) + bias_ref[...])
    gp = (dot(cot_ref[...], down_ref[...], NT) * slope).astype(BF16)
    share_ref[...] = (share_in[...] + dot(act.astype(BF16), part_ref[...])).astype(share_ref.dtype)
    gm_ref[...] = gm_in[...] + dot(gp, up_ref[...])


def mix(z, mid, cotangent, mine, theirs, bias, share, gm, last):
    length, width = mid.shape
    pieces = 4
    hidden = mine.shape[0]
    own_width = share.shape[1]
    rows = lambda w: pl.BlockSpec((TB, w), lambda t: (t, 0))
    whole = lambda a: pl.BlockSpec(a.shape, lambda t: (0, 0), pipeline_mode=pl.Buffered(1))
    return pl.pallas_call(
        functools.partial(mix_kernel, pieces),
        grid=(length // TB,),
        in_specs=[
            pl.BlockSpec(memory_space=pltpu.SMEM),
            rows(width),
            rows(width),
            whole(mine),
            whole(theirs),
            whole(bias),
            rows(own_width),
            rows(width),
        ],
        out_specs=[rows(own_width), rows(width)],
        out_shape=[shape_of((length, own_width), BF16 if last else F32), shape_of((length, width), F32)],
        scratch_shapes=[pltpu.VMEM((hidden, width), BF16), pltpu.VMEM((hidden, width), BF16), pltpu.VMEM((hidden, own_width), BF16)],
        compiler_params=params(),
        name="mix_others",
    )(z, mid, cotangent, mine, theirs, bias, share, gm)


def residual_kernel(z_ref, res_ref, cot_ref, gm_ref, gain_ref, low_ref, part_ref, sums_ref):
    start = pl.multiple_of(z_ref[0] * part_ref.shape[1], part_ref.shape[1])
    normed, inverse = normalize(res_ref[...])
    gm = gm_ref[...]
    cot = cot_ref[...].astype(F32)
    scaled = gm * gain_ref[...]
    grad = cot + inverse * (
        scaled - jnp.mean(scaled, axis=-1, keepdims=True) - normed * jnp.mean(scaled * normed, axis=-1, keepdims=True)
    )
    low_ref[...] = grad.astype(BF16)

    @pl.when(pl.program_id(0) == 0)
    def _():
        sums_ref[...] = jnp.zeros_like(sums_ref)

    sums_ref[0:1, :] += jnp.sum(gm * normed, axis=0, keepdims=True)
    sums_ref[1:2, :] += jnp.sum(gm, axis=0, keepdims=True)
    sums_ref[2:3, :] += jnp.sum(grad, axis=0, keepdims=True)
    sums_ref[3:4, :] += jnp.sum(cot, axis=0, keepdims=True)
    grid_own(part_ref, grad, z_ref[0])


def grid_own(part_ref, values, index):
    width = part_ref.shape[1]
    for k in range(values.shape[1] // width):

        @pl.when(index == k)
        def _():
            part_ref[...] = values[:, k * width : (k + 1) * width].astype(part_ref.dtype)


def residual_back(z, residual, cotangent, gm, gain, own_width):
    length, width = residual.shape
    rows = lambda w: pl.BlockSpec((TB, w), lambda t: (t, 0))
    return pl.pallas_call(
        residual_kernel,
        grid=(length // TB,),
        in_specs=[
            pl.BlockSpec(memory_space=pltpu.SMEM),
            rows(width),
            rows(width),
            rows(width),
            pl.BlockSpec((1, width), lambda t: (0, 0)),
        ],
        out_specs=[rows(width), rows(own_width), pl.BlockSpec((8, width), lambda t: (0, 0))],
        out_shape=[shape_of((length, width), BF16), shape_of((length, own_width), F32), shape_of((8, width), F32)],
        compiler_params=params(),
        name="residual_back",
    )(z, residual, cotangent, gm, gain)


def final_kernel(z_ref, tok_ref, part_ref, ga_ref, gain_ref, out_ref, sums_ref):
    normed, inverse = normalize(tok_ref[...].astype(F32))
    ga = ga_ref[...]
    scaled = ga * gain_ref[...]
    grad = inverse * (
        scaled - jnp.mean(scaled, axis=-1, keepdims=True) - normed * jnp.mean(scaled * normed, axis=-1, keepdims=True)
    )
    width = out_ref.shape[1]

    @pl.when(pl.program_id(0) == 0)
    def _():
        sums_ref[...] = jnp.zeros_like(sums_ref)

    for k in range(grad.shape[1] // width):

        @pl.when(z_ref[0] == k)
        def _():
            own = slice(k * width, (k + 1) * width)
            out_ref[...] = (part_ref[...] + grad[:, own]).astype(BF16)
            sums_ref[0:1, :] += jnp.sum(ga[:, own] * normed[:, own], axis=0, keepdims=True)
            sums_ref[1:2, :] += jnp.sum(ga[:, own], axis=0, keepdims=True)


def final_back(z, tokens, part, ga, gain):
    length, width = tokens.shape
    own_width = part.shape[1]
    rows = lambda w: pl.BlockSpec((TB, w), lambda t: (t, 0))
    return pl.pallas_call(
        final_kernel,
        grid=(length // TB,),
        in_specs=[
            pl.BlockSpec(memory_space=pltpu.SMEM),
            rows(width),
            rows(own_width),
            rows(width),
            pl.BlockSpec((1, width), lambda t: (0, 0)),
        ],
        out_specs=[rows(own_width), pl.BlockSpec((8, own_width), lambda t: (0, 0))],
        out_shape=[shape_of((length, own_width), BF16), shape_of((8, own_width), F32)],
        compiler_params=params(),
        name="final_back",
    )(z, tokens, part, ga, gain)


def hidden_grad_kernel(mid_ref, cot_ref, gp_ref, act_ref, out_ref):
    parts, per = out_ref.shape[0], out_ref.shape[1] // 2
    for at, left, right in ((0, mid_ref, gp_ref), (per, cot_ref, act_ref)):
        grad = dot(left[...], right[...], TN)
        for a in range(parts):
            out_ref[a, at : at + per, :] = grad[a * per : (a + 1) * per]


def hidden_grad(mid, cotangent, gp, act, parts):
    length, width = mid.shape
    hidden = gp.shape[1]
    rows = 128
    per = width // parts
    column = pl.BlockSpec((length, rows), lambda j: (0, j))
    whole = pl.BlockSpec((length, hidden), lambda j: (0, 0), pipeline_mode=pl.Buffered(1))
    return pl.pallas_call(
        hidden_grad_kernel,
        grid=(width // rows,),
        in_specs=[column, column, whole, whole],
        out_specs=pl.BlockSpec((rows // per, 2 * per, hidden), lambda j: (j, 0, 0)),
        out_shape=shape_of((parts, 2 * per, hidden), F32),
        compiler_params=params(),
        name="hidden_grad",
    )(mid, cotangent, gp, act)


def head_grad_kernel(x_ref, low_ref, gj_ref, att_ref, out_ref, bsum_ref):
    wide = gj_ref.shape[1]
    out_ref[0, :, 0:wide] = dot(x_ref[...], gj_ref[...], TN)
    out_ref[0, :, wide:] = dot(low_ref[...], att_ref[...], TT)

    @pl.when(pl.program_id(0) == 0)
    def _():
        bsum_ref[...] = jnp.sum(gj_ref[...].astype(F32), axis=0, keepdims=True)


def head_grad(x, low, gj, att):
    length, width = x.shape
    wide, local = gj.shape[1], att.shape[0]
    rows = 128
    column = pl.BlockSpec((length, rows), lambda j: (0, j))
    whole = lambda a: pl.BlockSpec(a.shape, lambda j: (0, 0), pipeline_mode=pl.Buffered(1))
    return pl.pallas_call(
        head_grad_kernel,
        grid=(width // rows,),
        in_specs=[column, column, whole(gj), whole(att)],
        out_specs=[pl.BlockSpec((1, rows, wide + local), lambda j: (j, 0, 0)), pl.BlockSpec((1, wide), lambda j: (0, 0))],
        out_shape=[shape_of((width // rows, rows, wide + local), F32), shape_of((1, wide), F32)],
        compiler_params=params(),
        name="head_grad",
    )(x, low, gj, att)


def shards(
    tokens, segment_ids, attention_gain, attention_shift, joint_weight, joint_bias, output_weight, output_bias,
    mixer_gain, mixer_shift, up_weight, up_bias, down_weight, down_bias, prefix_table, inner_weight, inner_bias,
    outer_weight, outer_bias, cotangent,
):
    length, width = tokens.shape
    local = joint_weight.shape[2]
    hidden = up_weight.shape[1]
    prefix_count = prefix_table.shape[0]
    batch_size, tensor_size = lax.axis_size("batch"), lax.axis_size("tensor")
    z = lax.axis_index("tensor").astype(jnp.int32)
    member = (lax.axis_index("batch") % 8).astype(jnp.int32)
    z_arr, member_arr = z.reshape(1), member.reshape(1)

    def own_columns(values):
        return lax.dynamic_slice_in_dim(values, z * local, local, values.ndim - 1)

    def along(values, k):
        return lax.ppermute(values, "tensor", [(i, i ^ k) for i in range(tensor_size)])

    def across(values, k):
        return lax.ppermute(values, "batch", [(i, i ^ k) for i in range(batch_size)])

    row = lambda v: v.reshape(1, -1)
    own_heads, send_heads = head_pieces(member_arr, joint_weight, output_weight)
    send_hidden = hidden_pieces(member_arr, up_weight, down_weight)

    hidden_prefix = jnp.tanh(jnp.dot(prefix_table, inner_weight.astype(F32), precision=PRECISE) + inner_bias)
    outer_float = outer_weight.astype(F32)
    prefix_pairs = jnp.einsum("pr,rke->kpe", hidden_prefix, outer_float, precision=PRECISE) + outer_bias[:, None, :]
    prefix_padded = jnp.pad(prefix_pairs, ((0, 0), (0, PAD - prefix_count), (0, 0)))

    small = jnp.concatenate([prefix_padded.reshape(2 * PAD, local), joint_bias, up_bias.reshape(8, hidden // 256, 32).transpose(1, 0, 2).reshape(-1, local), jnp.zeros((1, local), F32)], axis=0)

    def reorder(values):
        parts = values.reshape(values.shape[0], 8, local // 8)
        for bit in (1, 2, 4):
            turned = parts.reshape(values.shape[0], 4 // bit, 2, bit, local // 8)[:, :, ::-1].reshape(parts.shape)
            parts = jnp.where((member & bit) > 0, turned, parts)
        return parts.reshape(values.shape)

    smalls = [reorder(along(small, k)) for k in (1, 2, 3)]

    def plane(first, diagonal, turn):
        x1, y1 = across(first, 2), across(first, 4)
        if diagonal is None:
            diagonal = across(x1, 4) if turn == 2 else across(y1, 2)
        mine = jnp.concatenate([first, x1, y1, diagonal], axis=0)
        return mine, across(mine, 1)

    def slots(send):
        return [
            plane(along(send[0], 1), along(send[1], 1), 1),
            plane(along(send[0], 2), None, 2),
            plane(along(send[0], 3), None, 3),
        ]

    seg_row = segment_ids
    seg_col = segment_ids.reshape(length, 1)
    others = slots(send_heads)
    x, *saved, residual = attend(
        False, prefix_count, length, width,
        (tokens, row(attention_gain), row(attention_shift), own_heads, joint_bias, prefix_padded[0], prefix_padded[1], seg_col, seg_row, row(output_bias)),
    )
    groups = [(own_heads, saved, prefix_padded[0], prefix_padded[1])]
    for (mine, theirs), extra in zip(others, smalls):
        pk, pv, bias = extra[0:PAD], extra[PAD : 2 * PAD], extra[2 * PAD : 2 * PAD + 3]
        w, *saved, residual = attend(True, prefix_count, length, width, (x, mine, theirs, bias, pk, pv, seg_col, seg_row, residual))
        groups.append((w, saved, pk, pv))

    mid, act, gp, share, gm, up_bias_sum = mix_own(
        z_arr, residual, cotangent, row(mixer_gain), row(mixer_shift), up_weight, row(up_bias), down_weight, row(down_bias), local
    )
    hidden_sum = lax.psum_scatter(hidden_grad(mid, cotangent, gp, act, batch_size), "batch", scatter_dimension=0, tiled=False)
    for k, ((mine, theirs), extra) in enumerate(zip(slots(send_hidden), smalls)):
        bias = extra[2 * PAD + 3 : 2 * PAD + 3 + hidden // 256].reshape(hidden // 256, 8, 32).transpose(1, 0, 2).reshape(1, hidden)
        share, gm = mix(z_arr, mid, cotangent, mine, theirs, bias, share, gm, k == 2)
    low, part, sums = residual_back(z_arr, residual, cotangent, gm, row(mixer_gain), local)

    w, saved, pk, pv = groups[0]
    gj, gprefix, ga = attend_back(True, prefix_count, (w, *saved, pk, pv, seg_col, seg_row, low))
    head_parts, joint_bias_sum = head_grad(x, low, gj, saved[3])
    head_sum = lax.psum_scatter(head_parts.reshape(batch_size, -1, 3 * local + local), "batch", scatter_dimension=0, tiled=False)
    gprefix = gprefix[:, :prefix_count]
    grad_hidden_part = jnp.einsum("kpe,rke->pr", gprefix, outer_float, precision=PRECISE)
    for w, saved, pk, pv in groups[1:]:
        (ga,) = attend_back(False, prefix_count, (w, *saved, pk, pv, seg_col, seg_row, low, ga))
    tokens_gradient, gain_sums = final_back(z_arr, tokens, part, ga, row(attention_gain))

    mixed = own_columns(sums[0:4])
    totals = lax.psum((joint_bias_sum, up_bias_sum, mixed, gain_sums[0:2], gprefix), "batch")
    grad_hidden_prefix = lax.psum(grad_hidden_part, ("batch", "tensor"))
    joint_bias_total, up_bias_total, mixed_total, gain_total, grad_prefix = totals
    outer_rows = outer_weight.shape[0] // batch_size
    hidden_own = lax.dynamic_slice_in_dim(hidden_prefix, lax.axis_index("batch") * outer_rows, outer_rows, 1)
    outer_total = jnp.einsum("pr,kpe->rke", hidden_own, grad_prefix, precision=PRECISE)
    outer_bias_total = jnp.sum(grad_prefix, axis=1)
    grad_inner = grad_hidden_prefix * (1.0 - hidden_prefix * hidden_prefix)
    inner_total = jnp.einsum("pd,pr->dr", prefix_table, grad_inner, precision=PRECISE)
    inner_bias_total = jnp.sum(grad_inner, axis=0)
    table_total = jnp.einsum("pr,dr->pd", grad_inner, inner_weight.astype(F32), precision=PRECISE)

    per = width // batch_size
    up_total, down_total = hidden_sum[:per], hidden_sum[per:].T
    head_sum = head_sum.reshape(per, 4 * local)
    joint_total = head_sum[:, : 3 * local].reshape(per, 3, local).transpose(1, 0, 2)
    output_total = head_sum[:, 3 * local :].T
    return (
        share,
        tokens_gradient,
        gain_total[0],
        gain_total[1],
        joint_total,
        joint_bias_total.reshape(3, local),
        output_total,
        mixed_total[2],
        mixed_total[0],
        mixed_total[1],
        up_total,
        up_bias_total.reshape(hidden),
        down_total,
        mixed_total[3],
        table_total,
        inner_total,
        inner_bias_total,
        outer_total,
        outer_bias_total,
    )


def solution(mesh):
    placed = (
        P("batch", None),
        P("batch", None),
        P(),
        P(),
        P(None, None, "tensor"),
        P(None, "tensor"),
        P("tensor", None),
        P(),
        P(),
        P(),
        P(None, "tensor"),
        P("tensor"),
        P("tensor", None),
        P(),
        P(),
        P(),
        P(),
        P(None, None, "tensor"),
        P(None, "tensor"),
        P("batch", None),
    )
    return jax.shard_map(
        shards,
        mesh=mesh,
        in_specs=placed,
        out_specs=(
            P("batch", "tensor"),
            P("batch", "tensor"),
            P("tensor"),
            P("tensor"),
            P(None, "batch", "tensor"),
            P(None, "tensor"),
            P("tensor", "batch"),
            P("tensor"),
            P("tensor"),
            P("tensor"),
            P("batch", "tensor"),
            P("tensor"),
            P("tensor", "batch"),
            P("tensor"),
            P(),
            P(),
            P(),
            P("batch", None, "tensor"),
            P(None, "tensor"),
        ),
        check_vma=False,
    )
```

```python
import functools

import jax
import jax.numpy as jnp
from jax import lax
from jax.experimental import pallas as pl
from jax.experimental.pallas import tpu as pltpu
from jax.sharding import PartitionSpec as P

HD = 64
GROUP = 4
WIDE = GROUP * HD
QB = 256
PAD = 16
TB = 256
EPSILON = 1e-05
PRECISE = lax.Precision.HIGHEST
NEGATIVE = -1e30
VMEM = 56 * 2**20
F32, BF16 = jnp.float32, jnp.bfloat16
NN = (((1,), (0,)), ((), ()))
NT = (((1,), (1,)), ((), ()))
TN = (((0,), (0,)), ((), ()))
TT = (((0,), (1,)), ((), ()))
shape_of = jax.ShapeDtypeStruct


def dot(a, b, dims=NN):
    return lax.dot_general(a, b, dims, preferred_element_type=F32)


def params(**kw):
    return pltpu.CompilerParams(vmem_limit_bytes=VMEM, **kw)


def normalize(values):
    centered = values - jnp.mean(values, axis=-1, keepdims=True)
    inverse = lax.rsqrt(jnp.mean(centered * centered, axis=-1, keepdims=True) + EPSILON)
    return centered * inverse, inverse


def heads_kernel(turn, member_ref, joint_ref, out_ref, own_ref, send_ref):
    for c in range(3):
        own_ref[c] = joint_ref[c].T
    own_ref[3] = out_ref[...]
    rows = own_ref.shape[1] // 8
    for p in range(2):
        member = member_ref[0] ^ (turn * p)
        start = pl.multiple_of(member * rows, rows)
        for c in range(4):
            send_ref[p, c * rows : (c + 1) * rows, :] = own_ref[c, pl.ds(start, rows), :].astype(F32)


def head_pieces(member, joint_weight, output_weight):
    _, width, local = joint_weight.shape
    vm = pl.BlockSpec(memory_space=pltpu.VMEM)
    return pl.pallas_call(
        functools.partial(heads_kernel, 6),
        out_shape=[shape_of((4, local, width), BF16), shape_of((2, local // 2, width), F32)],
        in_specs=[pl.BlockSpec(memory_space=pltpu.SMEM), vm, vm],
        out_specs=[vm, vm],
        compiler_params=params(),
        name="head_pieces",
    )(member, joint_weight, output_weight)


def hidden_kernel(member_ref, up_ref, down_ref, send_ref):
    rows = down_ref.shape[0]
    send_ref[0, 0:rows, :] = up_ref[...].T.astype(F32)
    send_ref[0, rows : 2 * rows, :] = down_ref[...].astype(F32)


def hidden_pieces(member, up_weight, down_weight):
    width, local = up_weight.shape
    rows = local // 8
    return pl.pallas_call(
        hidden_kernel,
        out_shape=shape_of((2, 2 * rows, width), F32),
        grid_spec=pltpu.PrefetchScalarGridSpec(
            num_scalar_prefetch=1,
            grid=(2,),
            in_specs=[
                pl.BlockSpec((width, rows), lambda p, m: (0, m[0] ^ (6 * p))),
                pl.BlockSpec((rows, width), lambda p, m: (m[0] ^ (6 * p), 0)),
            ],
            out_specs=pl.BlockSpec((1, 2 * rows, width), lambda p, m: (p, 0, 0)),
        ),
        compiler_params=params(),
        name="hidden_pieces",
    )(member, up_weight, down_weight)


def head_of_lane(rows):
    return lax.broadcasted_iota(jnp.int32, (rows, WIDE), 1) // HD


def first_key(i, length):
    return max(0, (i * QB - length // 2 + 1) // QB) * QB


def mask_tile(seg_col, seg_row, first, last, start):
    keys = lax.broadcasted_iota(jnp.int32, (last - first, QB), 0) + first
    asks = lax.broadcasted_iota(jnp.int32, (last - first, QB), 1) + start
    allowed = (seg_col == seg_row) & (keys <= asks)
    return jnp.where(allowed, 0.0, NEGATIVE)


def reorder(values, member, dim=1):
    block = values.shape[dim] // 8
    place = lax.broadcasted_iota(jnp.int32, values.shape, dim) // block
    for bit in (1, 2, 4):
        up = pltpu.roll(values, block * bit, dim)
        down = pltpu.roll(values, values.shape[dim] - block * bit, dim)
        turned = jnp.where((place & bit) != 0, up, down)
        values = jnp.where((member & bit) != 0, turned, values)
    return values


def column_of(seg_row):
    wide = jnp.broadcast_to(seg_row.astype(F32), (128, seg_row.shape[1]))
    return wide.T[:, 0:1].astype(jnp.int32)


def extras(member_ref, small_ref, merge):
    small = small_ref[0:40, :]
    if merge:
        small = reorder(small, member_ref[0])
    return small[0:PAD].astype(BF16), small[PAD : 2 * PAD].astype(BF16), small[2 * PAD : 2 * PAD + 8]


def attend_kernel(merge, prefix_count, member_ref, *refs):
    if merge:
        x_ref, mine_ref, theirs_ref, small_ref, segr_ref, acc_ref = refs[:6]
        w_ref, q_ref, k_ref, v_ref, att_ref, lse_ref, out_ref, mask_ref, vt_ref = refs[6:]
        half = HD // 2
        for g in range(GROUP):
            for c in range(4):
                piece = slice(g * 4 * half + c * half, g * 4 * half + (c + 1) * half)
                w_ref[c, g * HD : g * HD + half, :] = mine_ref[piece, :].astype(BF16)
                w_ref[c, g * HD + half : (g + 1) * HD, :] = theirs_ref[piece, :].astype(BF16)
    else:
        tok_ref, gain_ref, shift_ref, w_ref, small_ref, segr_ref, acc_ref = refs[:7]
        x_ref, q_ref, k_ref, v_ref, att_ref, lse_ref, out_ref, mask_ref, vt_ref = refs[7:]
        for t in range(0, tok_ref.shape[0], TB):
            normed, _ = normalize(tok_ref[t : t + TB, :].astype(F32))
            x_ref[t : t + TB, :] = (normed * gain_ref[...] + shift_ref[...]).astype(BF16)
    pk, pv, bias = extras(member_ref, small_ref, merge)
    seg_col = column_of(segr_ref[...])
    length = x_ref.shape[0]
    x = x_ref[...]
    q_ref[...] = ((dot(x, w_ref[0], NT) + bias[0:1]) * HD ** (-0.5)).astype(BF16)
    k_ref[...] = (dot(x, w_ref[1], NT) + bias[1:2]).astype(BF16)
    v_ref[...] = (dot(x, w_ref[2], NT) + bias[2:3]).astype(BF16)
    vt_ref[...] = v_ref[...].T
    pvt = pv.T
    live = lax.broadcasted_iota(jnp.int32, (PAD, QB), 0) < prefix_count
    heads = head_of_lane(QB)
    for i in range(length // QB):
        first, last, rows = first_key(i, length), (i + 1) * QB, slice(i * QB, (i + 1) * QB)
        mask_ref[first:last, :] = mask_tile(seg_col[first:last], segr_ref[:, rows], first, last, i * QB)
        for h in range(GROUP):
            span = slice(h * HD, (h + 1) * HD)
            asked = jnp.where(heads == h, q_ref[rows, :], jnp.zeros((), BF16))
            s = dot(k_ref[first:last, :], asked, NT) + mask_ref[first:last, :]
            sp = jnp.where(live, dot(pk, asked, NT), NEGATIVE)
            top = jnp.maximum(jnp.max(s, axis=0, keepdims=True), jnp.max(sp, axis=0, keepdims=True))
            e, ep = jnp.exp(s - top), jnp.exp(sp - top)
            total = jnp.sum(e, axis=0, keepdims=True) + jnp.sum(ep, axis=0, keepdims=True)
            o = dot(vt_ref[span, first:last], e.astype(BF16)) + dot(pvt[span, :], ep.astype(BF16))
            att_ref[span, rows] = (o / total).astype(BF16)
            lse_ref[h : h + 1, rows] = top + jnp.log(total)
    if merge:
        out_ref[...] = acc_ref[...] + dot(att_ref[...], w_ref[3], TN)
    else:
        for t in range(0, length, TB):
            base = tok_ref[t : t + TB, :].astype(F32) + acc_ref[...]
            out_ref[t : t + TB, :] = base + dot(att_ref[:, t : t + TB], w_ref[3], TN)


def attend_outs(length, width):
    return [shape_of((length, WIDE), BF16)] * 3 + [
        shape_of((WIDE, length), BF16),
        shape_of((GROUP, length), F32),
        shape_of((length, width), F32),
    ]


def attend(merge, prefix_count, length, width, *args):
    first = shape_of((4, WIDE, width), BF16) if merge else shape_of((length, width), BF16)
    vm = pl.BlockSpec(memory_space=pltpu.VMEM)
    return pl.pallas_call(
        functools.partial(attend_kernel, merge, prefix_count),
        out_shape=[first] + attend_outs(length, width),
        in_specs=[pl.BlockSpec(memory_space=pltpu.SMEM)] + [vm] * (len(args) - 1),
        scratch_shapes=[pltpu.VMEM((length, QB), F32), pltpu.VMEM((WIDE, length), BF16)],
        compiler_params=params(),
        name="attend_others" if merge else "attend_own",
    )(*args)


def back_kernel(own, prefix_count, member_ref, *refs):
    w_ref, q_ref, k_ref, v_ref, att_ref, lse_ref, small_ref, segr_ref, gr_ref = refs[:9]
    if own:
        gj_ref, gp_ref, out_ref, mask_ref, kt_ref, p_ref, ds_ref, do_ref, dot_ref, dqt_ref, dk_ref, dv_ref, qm_ref, gm_ref = refs[9:]
    else:
        acc_ref, out_ref, mask_ref, kt_ref, p_ref, ds_ref, do_ref, dot_ref, dqt_ref, dk_ref, dv_ref, qm_ref, gm_ref, gj_ref = refs[9:]
    length = q_ref.shape[0]
    do_ref[...] = dot(gr_ref[...], w_ref[3], NT).astype(BF16)
    dot_ref[...] = do_ref[...].T
    kt_ref[...] = k_ref[...].T
    pk, pv, _ = extras(member_ref, small_ref, not own)
    seg_col = column_of(segr_ref[...])
    pkt = pk.T
    live = lax.broadcasted_iota(jnp.int32, (PAD, QB), 0) < prefix_count
    heads = head_of_lane(QB)
    dk_ref[...] = jnp.zeros_like(dk_ref)
    dv_ref[...] = jnp.zeros_like(dv_ref)
    zero = jnp.zeros((), BF16)
    gpk = jnp.zeros((PAD, WIDE), F32)
    gpv = jnp.zeros((PAD, WIDE), F32)
    for i in range(length // QB):
        first, last, rows = first_key(i, length), (i + 1) * QB, slice(i * QB, (i + 1) * QB)
        mask_ref[first:last, :] = mask_tile(seg_col[first:last], segr_ref[:, rows], first, last, i * QB)
        for h in range(GROUP):
            span, lanes = slice(h * HD, (h + 1) * HD), slice(h * QB, (h + 1) * QB)
            asked = jnp.where(heads == h, q_ref[rows, :], zero)
            grad = jnp.where(heads == h, do_ref[rows, :], zero)
            qm_ref[lanes, :] = asked
            gm_ref[lanes, :] = grad
            lse = lse_ref[h : h + 1, rows]
            delta = jnp.sum(dot_ref[span, rows].astype(F32) * att_ref[span, rows].astype(F32), axis=0, keepdims=True)
            p = jnp.exp(dot(k_ref[first:last, :], asked, NT) + mask_ref[first:last, :] - lse)
            p_ref[first:last, lanes] = p.astype(BF16)
            ds = (p * (dot(v_ref[first:last, :], grad, NT) - delta)).astype(BF16)
            ds_ref[first:last, lanes] = ds
            pp = jnp.exp(jnp.where(live, dot(pk, asked, NT), NEGATIVE) - lse)
            dsp = (pp * (dot(pv, grad, NT) - delta)).astype(BF16)
            dqt_ref[span, rows] = dot(kt_ref[span, first:last], ds) + dot(pkt[span, :], dsp)
            if own:
                gpk = gpk + dot(dsp, asked)
                gpv = gpv + dot(pp.astype(BF16), grad)
        dk_ref[first:last, :] += dot(ds_ref[first:last, :], qm_ref[...])
        dv_ref[first:last, :] += dot(p_ref[first:last, :], gm_ref[...])
    gj_ref[:, 0:WIDE] = dqt_ref[...].astype(BF16).T * jnp.asarray(HD ** (-0.5), BF16)
    gj_ref[:, WIDE : 2 * WIDE] = dk_ref[...].astype(BF16)
    gj_ref[:, 2 * WIDE : 3 * WIDE] = dv_ref[...].astype(BF16)
    part = dot(gj_ref[...], w_ref[0:3].reshape(3 * WIDE, w_ref.shape[2]))
    if own:
        gp_ref[0] = gpk
        gp_ref[1] = gpv
        out_ref[...] = part
    else:
        out_ref[...] = acc_ref[...] + part


def attend_back(own, prefix_count, *args):
    length, width = args[9].shape
    outs = [shape_of((length, width), F32)]
    scratch = [
        pltpu.VMEM((length, QB), F32),
        pltpu.VMEM((WIDE, length), BF16),
        pltpu.VMEM((length, GROUP * QB), BF16),
        pltpu.VMEM((length, GROUP * QB), BF16),
        pltpu.VMEM((length, WIDE), BF16),
        pltpu.VMEM((WIDE, length), BF16),
        pltpu.VMEM((WIDE, length), F32),
        pltpu.VMEM((length, WIDE), F32),
        pltpu.VMEM((length, WIDE), F32),
        pltpu.VMEM((GROUP * QB, WIDE), BF16),
        pltpu.VMEM((GROUP * QB, WIDE), BF16),
    ]
    if own:
        outs = [shape_of((length, 3 * WIDE), BF16), shape_of((2, PAD, WIDE), F32)] + outs
    else:
        scratch = scratch + [pltpu.VMEM((length, 3 * WIDE), BF16)]
    return pl.pallas_call(
        functools.partial(back_kernel, own, prefix_count),
        out_shape=outs,
        in_specs=[pl.BlockSpec(memory_space=pltpu.SMEM)] + [pl.BlockSpec(memory_space=pltpu.VMEM)] * (len(args) - 1),
        scratch_shapes=scratch,
        compiler_params=params(),
        name="back_own" if own else "back_others",
    )(*args)


def gelu_pair(v):
    c = 0.7978845608028654
    t = jnp.tanh(c * (v + 0.044715 * (v * v * v)))
    half = 0.5 * (1.0 + t)
    return v * half, half + 0.5 * v * (1.0 - t * t) * (c + (3.0 * 0.044715 * c) * (v * v))


def mix_own_kernel(z_ref, res_ref, cot_ref, gain_ref, shift_ref, up_ref, bias_ref, down_ref, dbias_ref,
                   mid_ref, act_ref, gp_ref, share_ref, gm_ref, bsum_ref):
    start = pl.multiple_of(z_ref[0] * share_ref.shape[1], share_ref.shape[1])
    own = pl.ds(start, share_ref.shape[1])
    normed, _ = normalize(res_ref[...])
    mid = (normed * gain_ref[...] + shift_ref[...]).astype(BF16)
    mid_ref[...] = mid
    act, slope = gelu_pair(dot(mid, up_ref[...]) + bias_ref[...])
    act = act.astype(BF16)
    act_ref[...] = act
    gp = (dot(cot_ref[...], down_ref[...], NT) * slope).astype(BF16)
    gp_ref[...] = gp
    share_ref[...] = res_ref[:, own] + dbias_ref[:, own] + dot(act, down_ref[:, own])
    gm_ref[...] = dot(gp, up_ref[...], NT)

    @pl.when(pl.program_id(0) == 0)
    def _():
        bsum_ref[...] = jnp.zeros_like(bsum_ref)

    bsum_ref[...] += jnp.sum(gp.astype(F32), axis=0, keepdims=True)


def mix_own(own_width, z, residual, cotangent, gain, shift, up, up_bias, down, down_bias):
    length, width = residual.shape
    hidden = up.shape[1]
    rows = lambda w: pl.BlockSpec((TB, w), lambda t: (t, 0))
    whole = lambda a: pl.BlockSpec(a.shape, lambda t: (0, 0), pipeline_mode=pl.Buffered(1))
    return pl.pallas_call(
        mix_own_kernel,
        grid=(length // TB,),
        in_specs=[
            pl.BlockSpec(memory_space=pltpu.SMEM),
            rows(width),
            rows(width),
            whole(gain),
            whole(shift),
            whole(up),
            whole(up_bias),
            whole(down),
            whole(down_bias),
        ],
        out_specs=[rows(width), rows(hidden), rows(hidden), rows(own_width), rows(width), pl.BlockSpec((1, hidden), lambda t: (0, 0))],
        out_shape=[
            shape_of((length, width), BF16),
            shape_of((length, hidden), BF16),
            shape_of((length, hidden), BF16),
            shape_of((length, own_width), F32),
            shape_of((length, width), F32),
            shape_of((1, hidden), F32),
        ],
        compiler_params=params(),
        name="mix_own",
    )(z, residual, cotangent, gain, shift, up, up_bias, down, down_bias)


def mix_kernel(pieces, begin, z_ref, mid_ref, cot_ref, mine_ref, theirs_ref, small_ref, share_in, gm_in, share_ref, gm_ref, up_ref, down_ref, part_ref):
    rows = mine_ref.shape[0] // pieces // 2
    start = pl.multiple_of(z_ref[0] * share_ref.shape[1], share_ref.shape[1])
    own = pl.ds(start, share_ref.shape[1])

    @pl.when(pl.program_id(0) == 0)
    def _():
        for g in range(pieces):
            for side, ref in enumerate((mine_ref, theirs_ref)):
                to = slice((2 * g + side) * rows, (2 * g + side + 1) * rows)
                up_ref[to, :] = ref[2 * g * rows : (2 * g + 1) * rows, :].astype(BF16)
                down_ref[to, :] = ref[(2 * g + 1) * rows : (2 * g + 2) * rows, :].astype(BF16)
        part_ref[...] = down_ref[:, own]

    mid = mid_ref[...]
    biases = reorder(small_ref[40:48, 0:rows], z_ref[1], 0)
    bias = jnp.concatenate([biases[2 * begin + j : 2 * begin + j + 1] for j in range(2 * pieces)], axis=1)
    act, slope = gelu_pair(dot(mid, up_ref[...], NT) + bias)
    gp = (dot(cot_ref[...], down_ref[...], NT) * slope).astype(BF16)
    share_ref[...] = (share_in[...] + dot(act.astype(BF16), part_ref[...])).astype(share_ref.dtype)
    gm_ref[...] = gm_in[...] + dot(gp, up_ref[...])


def mix(z, mid, cotangent, mine, theirs, bias, share, gm, begin, last):
    length, width = mid.shape
    pieces = mine.shape[0] // 256
    hidden = mine.shape[0]
    own_width = share.shape[1]
    rows = lambda w: pl.BlockSpec((TB, w), lambda t: (t, 0))
    whole = lambda a: pl.BlockSpec(a.shape, lambda t: (0, 0), pipeline_mode=pl.Buffered(1))
    return pl.pallas_call(
        functools.partial(mix_kernel, pieces, begin),
        grid=(length // TB,),
        in_specs=[
            pl.BlockSpec(memory_space=pltpu.SMEM),
            rows(width),
            rows(width),
            whole(mine),
            whole(theirs),
            whole(bias),
            rows(own_width),
            rows(width),
        ],
        out_specs=[rows(own_width), rows(width)],
        out_shape=[shape_of((length, own_width), BF16 if last else F32), shape_of((length, width), F32)],
        scratch_shapes=[pltpu.VMEM((hidden, width), BF16), pltpu.VMEM((hidden, width), BF16), pltpu.VMEM((hidden, own_width), BF16)],
        compiler_params=params(),
        name="mix_others",
    )(z, mid, cotangent, mine, theirs, bias, share, gm)


def residual_kernel(z_ref, res_ref, cot_ref, gm_ref, gain_ref, low_ref, part_ref, sums_ref):
    start = pl.multiple_of(z_ref[0] * part_ref.shape[1], part_ref.shape[1])
    normed, inverse = normalize(res_ref[...])
    gm = gm_ref[...]
    cot = cot_ref[...].astype(F32)
    scaled = gm * gain_ref[...]
    grad = cot + inverse * (
        scaled - jnp.mean(scaled, axis=-1, keepdims=True) - normed * jnp.mean(scaled * normed, axis=-1, keepdims=True)
    )
    low_ref[...] = grad.astype(BF16)

    @pl.when(pl.program_id(0) == 0)
    def _():
        sums_ref[...] = jnp.zeros_like(sums_ref)

    sums_ref[0:1, :] += jnp.sum(gm * normed, axis=0, keepdims=True)
    sums_ref[1:2, :] += jnp.sum(gm, axis=0, keepdims=True)
    sums_ref[2:3, :] += jnp.sum(grad, axis=0, keepdims=True)
    sums_ref[3:4, :] += jnp.sum(cot, axis=0, keepdims=True)
    grid_own(part_ref, grad, z_ref[0])


def grid_own(part_ref, values, index):
    width = part_ref.shape[1]
    for k in range(values.shape[1] // width):

        @pl.when(index == k)
        def _():
            part_ref[...] = values[:, k * width : (k + 1) * width].astype(part_ref.dtype)


def residual_back(z, residual, cotangent, gm, gain, own_width):
    length, width = residual.shape
    rows = lambda w: pl.BlockSpec((TB, w), lambda t: (t, 0))
    return pl.pallas_call(
        residual_kernel,
        grid=(length // TB,),
        in_specs=[
            pl.BlockSpec(memory_space=pltpu.SMEM),
            rows(width),
            rows(width),
            rows(width),
            pl.BlockSpec((1, width), lambda t: (0, 0)),
        ],
        out_specs=[rows(width), rows(own_width), pl.BlockSpec((8, width), lambda t: (0, 0))],
        out_shape=[shape_of((length, width), BF16), shape_of((length, own_width), F32), shape_of((8, width), F32)],
        compiler_params=params(),
        name="residual_back",
    )(z, residual, cotangent, gm, gain)


def final_kernel(z_ref, tok_ref, part_ref, ga_ref, gain_ref, out_ref, sums_ref):
    normed, inverse = normalize(tok_ref[...].astype(F32))
    ga = ga_ref[...]
    scaled = ga * gain_ref[...]
    grad = inverse * (
        scaled - jnp.mean(scaled, axis=-1, keepdims=True) - normed * jnp.mean(scaled * normed, axis=-1, keepdims=True)
    )
    width = out_ref.shape[1]

    @pl.when(pl.program_id(0) == 0)
    def _():
        sums_ref[...] = jnp.zeros_like(sums_ref)

    for k in range(grad.shape[1] // width):

        @pl.when(z_ref[0] == k)
        def _():
            own = slice(k * width, (k + 1) * width)
            out_ref[...] = (part_ref[...] + grad[:, own]).astype(BF16)
            sums_ref[0:1, :] += jnp.sum(ga[:, own] * normed[:, own], axis=0, keepdims=True)
            sums_ref[1:2, :] += jnp.sum(ga[:, own], axis=0, keepdims=True)


def final_back(z, tokens, part, ga, gain):
    length, width = tokens.shape
    own_width = part.shape[1]
    rows = lambda w: pl.BlockSpec((TB, w), lambda t: (t, 0))
    return pl.pallas_call(
        final_kernel,
        grid=(length // TB,),
        in_specs=[
            pl.BlockSpec(memory_space=pltpu.SMEM),
            rows(width),
            rows(own_width),
            rows(width),
            pl.BlockSpec((1, width), lambda t: (0, 0)),
        ],
        out_specs=[rows(own_width), pl.BlockSpec((8, own_width), lambda t: (0, 0))],
        out_shape=[shape_of((length, own_width), BF16), shape_of((8, own_width), F32)],
        compiler_params=params(),
        name="final_back",
    )(z, tokens, part, ga, gain)


def hidden_grad_kernel(mid_ref, cot_ref, gp_ref, act_ref, out_ref):
    parts, per = out_ref.shape[0], out_ref.shape[1] // 2
    for at, left, right in ((0, mid_ref, gp_ref), (per, cot_ref, act_ref)):
        grad = dot(left[...], right[...], TN)
        for a in range(parts):
            out_ref[a, at : at + per, :] = grad[a * per : (a + 1) * per]


def hidden_grad(parts, mid, cotangent, gp, act):
    length, width = mid.shape
    hidden = gp.shape[1]
    rows = 128
    per = width // parts
    column = pl.BlockSpec((length, rows), lambda j: (0, j))
    whole = pl.BlockSpec((length, hidden), lambda j: (0, 0), pipeline_mode=pl.Buffered(1))
    return pl.pallas_call(
        hidden_grad_kernel,
        grid=(width // rows,),
        in_specs=[column, column, whole, whole],
        out_specs=pl.BlockSpec((rows // per, 2 * per, hidden), lambda j: (j, 0, 0)),
        out_shape=shape_of((parts, 2 * per, hidden), F32),
        compiler_params=params(),
        name="hidden_grad",
    )(mid, cotangent, gp, act)


def head_grad_kernel(x_ref, low_ref, gj_ref, att_ref, out_ref, bsum_ref):
    wide = gj_ref.shape[1]
    out_ref[0, :, 0:wide] = dot(x_ref[...], gj_ref[...], TN)
    out_ref[0, :, wide:] = dot(low_ref[...], att_ref[...], TT)

    @pl.when(pl.program_id(0) == 0)
    def _():
        bsum_ref[...] = jnp.sum(gj_ref[...].astype(F32), axis=0, keepdims=True)


def head_grad(x, low, gj, att):
    length, width = x.shape
    wide, local = gj.shape[1], att.shape[0]
    rows = 128
    column = pl.BlockSpec((length, rows), lambda j: (0, j))
    whole = lambda a: pl.BlockSpec(a.shape, lambda j: (0, 0), pipeline_mode=pl.Buffered(1))
    return pl.pallas_call(
        head_grad_kernel,
        grid=(width // rows,),
        in_specs=[column, column, whole(gj), whole(att)],
        out_specs=[pl.BlockSpec((1, rows, wide + local), lambda j: (j, 0, 0)), pl.BlockSpec((1, wide), lambda j: (0, 0))],
        out_shape=[shape_of((width // rows, rows, wide + local), F32), shape_of((1, wide), F32)],
        compiler_params=params(),
        name="head_grad",
    )(x, low, gj, att)


def shards(
    tokens, segment_ids, attention_gain, attention_shift, joint_weight, joint_bias, output_weight, output_bias,
    mixer_gain, mixer_shift, up_weight, up_bias, down_weight, down_bias, prefix_table, inner_weight, inner_bias,
    outer_weight, outer_bias, cotangent,
):
    length, width = tokens.shape
    local = joint_weight.shape[2]
    hidden = up_weight.shape[1]
    prefix_count = prefix_table.shape[0]
    batch_size, tensor_size = lax.axis_size("batch"), lax.axis_size("tensor")
    z = lax.axis_index("tensor").astype(jnp.int32)
    member = (lax.axis_index("batch") % 8).astype(jnp.int32)
    member_arr, places = member.reshape(1), jnp.stack([z, member])

    def own_columns(values):
        return lax.dynamic_slice_in_dim(values, z * local, local, values.ndim - 1)

    def along(values, k):
        return lax.ppermute(values, "tensor", [(i, i ^ k) for i in range(tensor_size)])

    def across(values, k):
        return lax.ppermute(values, "batch", [(i, i ^ k) for i in range(batch_size)])

    now = [member_arr]

    def after(values):
        return lax.optimization_barrier((values, *now))[0]

    def wait(*values):
        held = lax.optimization_barrier((*values, *now))
        now[:] = [held[0]]
        return held[0] if len(values) == 1 else held[: len(values)]

    def run(call, *args):
        held = lax.optimization_barrier((*args, *now))
        outs = call(*held[: len(args)])
        now[:] = [outs[-1] if isinstance(outs, (list, tuple)) else outs]
        return outs

    row = lambda v: v.reshape(1, -1)
    stack = lambda *parts: jnp.concatenate(parts, axis=0)

    own_heads, send_heads = run(head_pieces, member_arr, joint_weight, output_weight)
    a1 = along(after(send_heads[0]), 1)
    send_hidden = run(hidden_pieces, member_arr, up_weight, down_weight)
    a2 = along(after(send_heads[0]), 2)

    def prefixes(prefix_table, inner_weight):
        hidden_prefix = jnp.tanh(jnp.dot(prefix_table, inner_weight.astype(F32), precision=PRECISE) + inner_bias)
        pairs = jnp.einsum("pr,rke->kpe", hidden_prefix, outer_weight.astype(F32), precision=PRECISE)
        pairs = jnp.pad(pairs + outer_bias[:, None, :], ((0, 0), (0, PAD - prefix_count), (0, 0)))
        ups = jnp.pad(up_bias.reshape(8, hidden // 8), ((0, 0), (0, local - hidden // 8)))
        joints = jnp.pad(joint_bias, ((0, 5), (0, 0)))
        return hidden_prefix, stack(pairs.reshape(2 * PAD, local), joints, ups)

    hidden_prefix, small = run(prefixes, prefix_table, inner_weight)
    smalls = [along(after(small), k) for k in (1, 2, 3)]
    a1 = wait(a1)
    a1x, a1y = across(after(a1), 2), across(after(a1), 4)
    x, *saved, residual = run(
        functools.partial(attend, False, prefix_count, length, width),
        member_arr, tokens, row(attention_gain), row(attention_shift), own_heads, small, segment_ids, row(output_bias),
    )
    groups = [(own_heads, saved, small)]

    def attend_more(mine, theirs, extra, residual):
        w, *saved, residual = run(
            functools.partial(attend, True, prefix_count, length, width),
            member_arr, x, mine, theirs, extra, segment_ids, residual,
        )
        groups.append((w, saved, extra))
        return residual

    a1x, a1y, a2, *smalls = wait(a1x, a1y, a2, *smalls)
    a1d, a3 = along(after(send_heads[1]), 1), along(after(send_heads[0]), 3)
    a2x, a2y = across(after(a2), 2), across(after(a2), 4)
    a1d = wait(a1d)
    mine = run(stack, a1, a1x, a1y, a1d)
    theirs = across(after(mine), 1)
    theirs = wait(theirs)
    f1 = along(after(send_hidden[0]), 1)
    residual = attend_more(mine, theirs, smalls[0], residual)

    a2x, a2y, a3 = wait(a2x, a2y, a3)
    a2d = across(after(a2x), 4)
    a3x, a3y = across(after(a3), 2), across(after(a3), 4)
    f2 = along(after(send_hidden[0]), 2)
    a2d = wait(a2d)
    mine = run(stack, a2, a2x, a2y, a2d)
    theirs = across(after(mine), 1)
    theirs = wait(theirs)
    residual = attend_more(mine, theirs, smalls[1], residual)

    a3x, a3y, f1 = wait(a3x, a3y, f1)
    a3d = across(after(a3y), 2)
    f1x, f1y = across(after(f1), 2), across(after(f1), 4)
    a3d = wait(a3d)
    mine = run(stack, a3, a3x, a3y, a3d)
    theirs = across(after(mine), 1)
    theirs = wait(theirs)
    f1d = along(after(send_hidden[1]), 1)
    residual = attend_more(mine, theirs, smalls[2], residual)

    mid, act, gp, share, gm, up_bias_sum = run(
        functools.partial(mix_own, local),
        places, residual, cotangent, row(mixer_gain), row(mixer_shift), up_weight, row(up_bias), down_weight,
        row(down_bias),
    )
    f1x, f1y, f2 = wait(f1x, f1y, f2)
    f2x, f2y = across(after(f2), 2), across(after(f2), 4)
    f3 = along(after(send_hidden[0]), 3)
    f1d = wait(f1d)
    mine = run(stack, f1, f1x, f1y, f1d)
    theirs = across(after(mine), 1)
    hidden_part = run(functools.partial(hidden_grad, batch_size), mid, cotangent, gp, act)
    theirs = wait(theirs)

    def mix_more(mine, theirs, extra, share, gm, begin, last):
        return run(
            functools.partial(mix, begin=begin, last=last), places, mid, cotangent, mine, theirs, extra, share, gm
        )

    share, gm = mix_more(mine, theirs, smalls[0], share, gm, 0, False)
    f2x, f2y, f3 = wait(f2x, f2y, f3)
    f2d = across(after(f2x), 4)
    f3x, f3y = across(after(f3), 2), across(after(f3), 4)
    f2d = wait(f2d)
    mine = run(stack, f2, f2x, f2y, f2d)
    theirs = across(after(mine), 1)
    theirs = wait(theirs)
    share, gm = mix_more(mine, theirs, smalls[1], share, gm, 0, False)
    f3x, f3y = wait(f3x, f3y)
    cut = f3.shape[0] // 2
    f3d = [across(after(f3x[:cut]), 4), across(after(f3y[cut:]), 2)]
    mine = run(stack, f3, f3x, f3y)
    theirs = across(after(mine), 1)
    theirs = wait(theirs)
    share, gm = mix_more(mine, theirs, smalls[2], share, gm, 0, False)
    f3d = wait(*f3d)
    mine = run(stack, *f3d)
    theirs = across(after(mine), 1)
    theirs = wait(theirs)
    share, gm = mix_more(mine, theirs, smalls[2], share, gm, 3, True)
    hidden_sum = lax.psum_scatter(after(hidden_part), "batch", scatter_dimension=0, tiled=False)

    low, part, sums = run(
        functools.partial(residual_back, own_width=local), places, residual, cotangent, gm, row(mixer_gain)
    )
    w, saved, extra = groups[0]
    gj, gprefix, ga = run(
        functools.partial(attend_back, True, prefix_count), member_arr, w, *saved, extra, segment_ids, low
    )
    head_part, joint_bias_sum = run(head_grad, x, low, gj, saved[3])
    head_sum = lax.psum_scatter(
        after(head_part.reshape(batch_size, -1, 4 * local)), "batch", scatter_dimension=0, tiled=False
    )

    def sums_before(gprefix, sums, joint_bias_sum, up_bias_sum):
        part = jnp.einsum("kpe,rke->pr", gprefix[:, :prefix_count], outer_weight.astype(F32), precision=PRECISE)
        rows = [gprefix.reshape(2 * PAD, local), own_columns(sums[0:4]), joint_bias_sum.reshape(3, local)]
        rows += [jnp.zeros((1, local), F32), up_bias_sum.reshape(-1, local), part.reshape(-1, local)]
        return stack(*rows)

    totals = run(sums_before, gprefix, sums, joint_bias_sum, up_bias_sum)
    turns = [1 << b for b in range((batch_size - 1).bit_length())]
    more = [(across, k) for k in turns] + [(along, 1 << b) for b in range((tensor_size - 1).bit_length())]
    split = 2 * PAD + 8 + hidden // local
    batch_totals = None
    for g, (w, saved, extra) in enumerate(groups[1:]):
        pending = None
        if more:
            send, k = more.pop(0)
            pending = send(after(totals), k)
        (ga,) = run(
            functools.partial(attend_back, False, prefix_count), member_arr, w, *saved, extra, segment_ids, low, ga
        )
        if pending is not None:
            totals = run(jnp.add, totals, wait(pending))
            if g + 1 == len(turns):
                batch_totals = totals
    while len(more) > tensor_size.bit_length() - 1:
        send, k = more.pop(0)
        totals = run(jnp.add, totals, wait(send(after(totals), k)))
        batch_totals = totals
    pending = more[0][0](after(totals), more[0][1])
    tokens_gradient, gain_sums = run(final_back, places, tokens, part, ga, row(attention_gain))
    totals = run(jnp.add, totals, wait(pending))
    for send, k in more[1:]:
        totals = run(jnp.add, totals, wait(send(after(totals), k)))
    for k in turns:
        gain_sums = run(jnp.add, gain_sums, wait(across(after(gain_sums), k)))

    grad_prefix = batch_totals[: 2 * PAD].reshape(2, PAD, local)[:, :prefix_count]
    mixed_total = batch_totals[2 * PAD : 2 * PAD + 4]
    joint_bias_total = batch_totals[2 * PAD + 4 : 2 * PAD + 7]
    up_bias_total = batch_totals[2 * PAD + 8 : split]
    grad_hidden_prefix = totals[split:].reshape(prefix_count, -1)
    outer_rows = outer_weight.shape[0] // batch_size
    hidden_own = lax.dynamic_slice_in_dim(hidden_prefix, lax.axis_index("batch") * outer_rows, outer_rows, 1)
    outer_total = jnp.einsum("pr,kpe->rke", hidden_own, grad_prefix, precision=PRECISE)
    outer_bias_total = jnp.sum(grad_prefix, axis=1)
    grad_inner = grad_hidden_prefix * (1.0 - hidden_prefix * hidden_prefix)
    inner_total = jnp.einsum("pd,pr->dr", prefix_table, grad_inner, precision=PRECISE)
    inner_bias_total = jnp.sum(grad_inner, axis=0)
    table_total = jnp.einsum("pr,dr->pd", grad_inner, inner_weight.astype(F32), precision=PRECISE)

    per = width // batch_size
    up_total, down_total = hidden_sum[:per], hidden_sum[per:].T
    head_sum = head_sum.reshape(per, 4 * local)
    joint_total = head_sum[:, : 3 * local].reshape(per, 3, local).transpose(1, 0, 2)
    output_total = head_sum[:, 3 * local :].T
    return (
        share,
        tokens_gradient,
        gain_sums[0],
        gain_sums[1],
        joint_total,
        joint_bias_total,
        output_total,
        mixed_total[2],
        mixed_total[0],
        mixed_total[1],
        up_total,
        up_bias_total.reshape(hidden),
        down_total,
        mixed_total[3],
        table_total,
        inner_total,
        inner_bias_total,
        outer_total,
        outer_bias_total,
    )


def solution(mesh):
    placed = (
        P("batch", None),
        P("batch", None),
        P(),
        P(),
        P(None, None, "tensor"),
        P(None, "tensor"),
        P("tensor", None),
        P(),
        P(),
        P(),
        P(None, "tensor"),
        P("tensor"),
        P("tensor", None),
        P(),
        P(),
        P(),
        P(),
        P(None, None, "tensor"),
        P(None, "tensor"),
        P("batch", None),
    )
    return jax.shard_map(
        shards,
        mesh=mesh,
        in_specs=placed,
        out_specs=(
            P("batch", "tensor"),
            P("batch", "tensor"),
            P("tensor"),
            P("tensor"),
            P(None, "batch", "tensor"),
            P(None, "tensor"),
            P("tensor", "batch"),
            P("tensor"),
            P("tensor"),
            P("tensor"),
            P("batch", "tensor"),
            P("tensor"),
            P("tensor", "batch"),
            P("tensor"),
            P(),
            P(),
            P(),
            P("batch", None, "tensor"),
            P(None, "tensor"),
        ),
        check_vma=False,
    )
```

```python
import functools

import jax
import jax.numpy as jnp
from jax import lax
from jax.experimental import pallas as pl
from jax.experimental.pallas import tpu as pltpu
from jax.sharding import PartitionSpec as P

HD = 64
GROUP = 4
WIDE = GROUP * HD
QB = 256
PAD = 16
TB = 256
EPSILON = 1e-05
PRECISE = lax.Precision.HIGHEST
NEGATIVE = -1e30
F32, BF16 = jnp.float32, jnp.bfloat16
NN = (((1,), (0,)), ((), ()))
NT = (((1,), (1,)), ((), ()))
TN = (((0,), (0,)), ((), ()))
shape_of = jax.ShapeDtypeStruct
BRIEF = pl.CostEstimate(flops=1024, bytes_accessed=1024, transcendentals=0)


def dot(a, b, dims=NN):
    return lax.dot_general(a, b, dims, preferred_element_type=F32)


def params(mib):
    return pltpu.CompilerParams(vmem_limit_bytes=mib * 2**20)


def resident(kernel, outs, scratch, name, mib, args, aliases={}):
    vm = pl.BlockSpec(memory_space=pltpu.VMEM)
    return pl.pallas_call(
        kernel,
        out_shape=outs,
        in_specs=[pl.BlockSpec(memory_space=pltpu.SMEM)] + [vm] * (len(args) - 1),
        out_specs=[vm] * len(outs),
        scratch_shapes=scratch,
        input_output_aliases=aliases,
        cost_estimate=BRIEF,
        compiler_params=params(mib),
        name=name,
    )(*args)


def normalize(values):
    centered = values - jnp.mean(values, axis=-1, keepdims=True)
    inverse = lax.rsqrt(jnp.mean(centered * centered, axis=-1, keepdims=True) + EPSILON)
    return centered * inverse, inverse


def heads_kernel(turn, member_ref, joint_ref, out_ref, own_ref, send_ref):
    for c in range(3):
        own_ref[c] = joint_ref[c].T
    own_ref[3] = out_ref[...]
    rows = own_ref.shape[1] // 8
    for p in range(2):
        member = member_ref[0] ^ (turn * p)
        start = pl.multiple_of(member * rows, rows)
        for c in range(4):
            send_ref[p, c * rows : (c + 1) * rows, :] = own_ref[c, pl.ds(start, rows), :].astype(F32)


def head_pieces(member, joint_weight, output_weight):
    _, width, local = joint_weight.shape
    vm = pl.BlockSpec(memory_space=pltpu.VMEM)
    return pl.pallas_call(
        functools.partial(heads_kernel, 6),
        out_shape=[shape_of((4, local, width), BF16), shape_of((2, local // 2, width), F32)],
        in_specs=[pl.BlockSpec(memory_space=pltpu.SMEM), vm, vm],
        out_specs=[vm, vm],
        cost_estimate=BRIEF,
        compiler_params=params(12),
        name="head_pieces",
    )(member, joint_weight, output_weight)


def hidden_kernel(member_ref, up_ref, down_ref, send_ref):
    rows = down_ref.shape[0]
    send_ref[0, 0:rows, :] = up_ref[...].T.astype(F32)
    send_ref[0, rows : 2 * rows, :] = down_ref[...].astype(F32)


def hidden_pieces(member, up_weight, down_weight):
    width, local = up_weight.shape
    rows = local // 8
    return pl.pallas_call(
        hidden_kernel,
        out_shape=shape_of((2, 2 * rows, width), F32),
        grid_spec=pltpu.PrefetchScalarGridSpec(
            num_scalar_prefetch=1,
            grid=(2,),
            in_specs=[
                pl.BlockSpec((width, rows), lambda p, m: (0, m[0] ^ (6 * p))),
                pl.BlockSpec((rows, width), lambda p, m: (m[0] ^ (6 * p), 0)),
            ],
            out_specs=pl.BlockSpec((1, 2 * rows, width), lambda p, m: (p, 0, 0)),
        ),
        cost_estimate=BRIEF,
        compiler_params=params(12),
        name="hidden_pieces",
    )(member, up_weight, down_weight)


def gather_kernel(places, *refs):
    sources, out_ref, sems = refs[: len(places)], refs[len(places)], refs[-1]
    copies, to = [], 0
    for n, ((start, rows), ref) in enumerate(zip(places, sources)):
        copies.append(pltpu.make_async_copy(ref.at[pl.ds(start, rows)], out_ref.at[pl.ds(to, rows)], sems.at[n]))
        to += rows
    for copy in copies:
        copy.start()
    for copy in copies:
        copy.wait()


def gather_rows(places, *arrays):
    anywhere = pl.BlockSpec(memory_space=pl.ANY)
    return pl.pallas_call(
        functools.partial(gather_kernel, places),
        in_specs=[anywhere] * len(arrays),
        out_specs=pl.BlockSpec(memory_space=pltpu.VMEM),
        out_shape=shape_of((sum(rows for _, rows in places), arrays[0].shape[1]), F32),
        scratch_shapes=[pltpu.SemaphoreType.DMA((len(places),))],
        cost_estimate=BRIEF,
        compiler_params=params(8),
        name="gather_rows",
    )(*arrays)


def reorder(values, member, dim=1):
    block = values.shape[dim] // 8
    place = lax.broadcasted_iota(jnp.int32, values.shape, dim) // block
    for bit in (1, 2, 4):
        up = pltpu.roll(values, block * bit, dim)
        down = pltpu.roll(values, values.shape[dim] - block * bit, dim)
        turned = jnp.where((place & bit) != 0, up, down)
        values = jnp.where((member & bit) != 0, turned, values)
    return values


def column_of(seg_row):
    wide = jnp.broadcast_to(seg_row.astype(F32), (128, seg_row.shape[1]))
    return wide.T[:, 0:1].astype(jnp.int32)


def extras(member, small_ref, others):
    small = small_ref[0:40, :]
    if others:
        small = reorder(small, member)
    return small[0:PAD].astype(BF16), small[PAD : 2 * PAD].astype(BF16), small[2 * PAD : 2 * PAD + 8]


def blocks_of(length):
    out = []
    for i in range(length // QB):
        first = max(0, (i * QB - length // 2 + 1) // QB) * QB
        last = (i + 1) * QB
        if first > 0 and last < length:
            first = 0
        out.append((i, first, last, (0, PAD + last) if first == 0 else (PAD + first, length + 2 * PAD)))
    return out


def strip_parts(block):
    _, first, last, (low, _) = block
    n = last - first
    return ((0, PAD), (PAD, PAD + n)) if low == 0 else ((n, n + PAD), (0, n))


def fill_prefix_mask(mask_ref, length, prefix_count):
    live = lax.broadcasted_iota(jnp.int32, (PAD, QB), 0) < prefix_count
    edge = jnp.where(live, 0.0, NEGATIVE)
    mask_ref[0:PAD, :] = edge
    mask_ref[PAD + length :, :] = edge


def fill_mask(mask_ref, seg_col, seg_row, block):
    i, first, last, _ = block
    keys = lax.broadcasted_iota(jnp.int32, (last - first, QB), 0) + first
    asks = lax.broadcasted_iota(jnp.int32, (last - first, QB), 1) + i * QB
    allowed = (seg_col[first:last] == seg_row[:, i * QB : last]) & (keys <= asks)
    mask_ref[PAD + first : PAD + last, :] = jnp.where(allowed, 0.0, NEGATIVE)


def fill_extended(ext_ref, prefix, values):
    length = values.shape[0]
    ext_ref[0:PAD, :] = prefix
    ext_ref[PAD : PAD + length, :] = values
    ext_ref[PAD + length :, :] = prefix


def head_lanes():
    return lax.broadcasted_iota(jnp.int32, (QB, WIDE), 1) // HD


def attend_scratch(length):
    return [
        pltpu.VMEM((length + 2 * PAD, QB), F32),
        pltpu.VMEM((length + 2 * PAD, WIDE), BF16),
        pltpu.VMEM((WIDE, length), BF16),
        pltpu.VMEM((2, length + PAD, QB), F32),
        pltpu.VMEM((GROUP, length), F32),
        pltpu.VMEM((GROUP, length), F32),
    ]


def attend_body(prefix_count, x_ref, w_ref, extra, segr_ref, q_ref, k_ref, v_ref, att_ref, lse_ref,
                mask_ref, ke_ref, vt_ref, s_ref, top_ref, sum_ref):
    length = x_ref.shape[0]
    pk, pv, bias = extra
    x = x_ref[...]
    q_ref[...] = ((dot(x, w_ref[0], NT) + bias[0:1]) * HD ** (-0.5)).astype(BF16)
    k = (dot(x, w_ref[1], NT) + bias[1:2]).astype(BF16)
    k_ref[...] = k
    fill_extended(ke_ref, pk, k)
    v = (dot(x, w_ref[2], NT) + bias[2:3]).astype(BF16)
    v_ref[...] = v
    vt_ref[...] = v.T
    pvt = pv.T
    seg_row = segr_ref[...]
    seg_col = column_of(seg_row)
    fill_prefix_mask(mask_ref, length, prefix_count)
    heads, zero = head_lanes(), jnp.zeros((), BF16)
    work = [(block, h) for block in blocks_of(length) for h in range(GROUP)]

    def ask(n):
        block, h = work[n]
        i, _, last, (low, high) = block
        if h == 0:
            fill_mask(mask_ref, seg_col, seg_row, block)
        asked = jnp.where(heads == h, q_ref[i * QB : last, :], zero)
        s_ref[n % 2, 0 : high - low, :] = dot(ke_ref[low:high, :], asked, NT) + mask_ref[low:high, :]

    ask(0)
    for n, (block, h) in enumerate(work):
        if n + 1 < len(work):
            ask(n + 1)
        i, first, last, (low, high) = block
        rows, span = slice(i * QB, last), slice(h * HD, (h + 1) * HD)
        (pa, pb), (ta, tb) = strip_parts(block)
        s = s_ref[n % 2, 0 : high - low, :]
        top = jnp.max(s, axis=0, keepdims=True)
        e = jnp.exp(s - top)
        total = jnp.sum(e, axis=0, keepdims=True)
        top_ref[h : h + 1, rows] = top
        sum_ref[h : h + 1, rows] = total
        e = e.astype(BF16)
        o = dot(vt_ref[span, first:last], e[ta:tb]) + dot(pvt[span, :], e[pa:pb])
        att_ref[span, rows] = (o * (1.0 / total)).astype(BF16)
    lse_ref[...] = top_ref[...] + jnp.log(sum_ref[...])


def attend_own_kernel(prefix_count, member_ref, tok_ref, gain_ref, shift_ref, w_ref, small_ref, segr_ref, bias_ref,
                      x_ref, q_ref, k_ref, v_ref, att_ref, lse_ref, out_ref, *scratch):
    length = tok_ref.shape[0]
    for t in range(0, length, TB):
        normed, _ = normalize(tok_ref[t : t + TB, :].astype(F32))
        x_ref[t : t + TB, :] = (normed * gain_ref[...] + shift_ref[...]).astype(BF16)
    attend_body(prefix_count, x_ref, w_ref, extras(member_ref[0], small_ref, False), segr_ref,
                q_ref, k_ref, v_ref, att_ref, lse_ref, *scratch)
    for t in range(0, length, TB):
        base = tok_ref[t : t + TB, :].astype(F32) + bias_ref[...]
        out_ref[t : t + TB, :] = base + dot(att_ref[:, t : t + TB], w_ref[3], TN)


def attend_others_kernel(prefix_count, carried, member_ref, x_ref, *refs):
    pieces, (small_ref, segr_ref, acc_ref) = refs[:8], refs[8:11]
    refs = refs[11 + carried :]
    w_ref, q_ref, k_ref, v_ref, att_ref, lse_ref, out_ref = refs[:7]
    half = HD // 2
    for j, ref in enumerate(pieces):
        for c in range(4):
            w_ref[c, j * half : (j + 1) * half, :] = ref[c * half : (c + 1) * half, :].astype(BF16)
    attend_body(prefix_count, x_ref, w_ref, extras(member_ref[0], small_ref, True), segr_ref,
                q_ref, k_ref, v_ref, att_ref, lse_ref, *refs[7:])

    @pl.when(pl.program_id(0) == 0)
    def _():
        out_ref[...] = acc_ref[...]

    for t in range(0, x_ref.shape[0], TB):
        out_ref[t : t + TB, :] += dot(att_ref[:, t : t + TB], w_ref[3], TN)


def attend_own(prefix_count, *args):
    length, width = args[1].shape
    return resident(
        functools.partial(attend_own_kernel, prefix_count),
        [shape_of((length, width), BF16)]
        + [shape_of((length, WIDE), BF16)] * 3
        + [shape_of((WIDE, length), BF16), shape_of((GROUP, length), F32), shape_of((length, width), F32)],
        attend_scratch(length),
        "attend_own",
        22,
        args,
    )


SCALARS = pl.BlockSpec(memory_space=pltpu.SMEM)


def once(values):
    return pl.BlockSpec(values.shape, lambda g: (0,) * len(values.shape), pipeline_mode=pl.Buffered(1))


def each(*block):
    return pl.BlockSpec((None,) + block, lambda g: (g,) + (0,) * len(block))


def rows_of(count, width):
    return pl.BlockSpec((count, width), lambda g: (g, 0))


def attend_others(prefix_count, first, count, total, member, x, pieces, small, seg, acc, carry=()):
    length, width = x.shape
    saved = [(4, WIDE, width), (length, WIDE), (length, WIDE), (length, WIDE), (WIDE, length), (GROUP, length)]
    piece = lambda at: pl.BlockSpec((128, width), lambda g: (g + at, 0))
    part = lambda block: pl.BlockSpec((None,) + block, lambda g: (g + first,) + (0,) * len(block))
    return pl.pallas_call(
        functools.partial(attend_others_kernel, prefix_count, len(carry)),
        grid=(count,),
        in_specs=[SCALARS, once(x)]
        + [piece(at) for _, at in pieces]
        + [pl.BlockSpec((48, WIDE), lambda g: (g + first, 0)), once(seg), once(acc)]
        + [pl.BlockSpec(memory_space=pl.ANY)] * len(carry),
        out_specs=[part(block) for block in saved] + [pl.BlockSpec((length, width), lambda g: (0, 0))],
        out_shape=[shape_of((total,) + block, BF16) for block in saved[:-1]]
        + [shape_of((total, GROUP, length), F32), shape_of((length, width), F32)],
        scratch_shapes=attend_scratch(length),
        input_output_aliases={13 + n: n for n in range(len(carry))},
        cost_estimate=BRIEF,
        compiler_params=params(50),
        name="attend_others",
    )(member, x, *[values for values, _ in pieces], small, seg, acc, *carry)


def back_scratch(length):
    low = lambda *shape: pltpu.VMEM(shape, BF16)
    return [
        pltpu.VMEM((length + 2 * PAD, QB), F32),
        low(length + 2 * PAD, WIDE),
        low(length + 2 * PAD, WIDE),
        low(WIDE, length),
        low(WIDE, length),
        low(WIDE, length),
        low(length, WIDE),
        pltpu.VMEM((2, length + PAD, QB), F32),
        pltpu.VMEM((2, length + PAD, QB), F32),
        pltpu.VMEM((GROUP, length), F32),
        pltpu.VMEM((2, WIDE, length), F32),
    ]


def back_body(prefix_count, extra, w_ref, q_ref, k_ref, v_ref, att_ref, lse_ref, segr_ref, low_ref, gjt_ref, gp_ref,
              mask_ref, ke_ref, ve_ref, kt_ref, qt_ref, dot_ref, do_ref, s_ref, dp_ref, delta_ref, acc_ref):
    length = q_ref.shape[0]
    pk, pv, _ = extra
    do = dot(low_ref[...], w_ref[3], NT).astype(BF16)
    do_ref[...] = do
    dot_ref[...] = do.T
    kt_ref[...] = k_ref[...].T
    qt_ref[...] = q_ref[...].T
    fill_extended(ke_ref, pk, k_ref[...])
    fill_extended(ve_ref, pv, v_ref[...])
    pkt = pk.T
    for h in range(GROUP):
        span = slice(h * HD, (h + 1) * HD)
        products = dot_ref[span, :].astype(F32) * att_ref[span, :].astype(F32)
        delta_ref[h : h + 1, :] = jnp.sum(products, axis=0, keepdims=True)
    seg_row = segr_ref[...]
    seg_col = column_of(seg_row)
    fill_prefix_mask(mask_ref, length, prefix_count)
    acc_ref[...] = jnp.zeros_like(acc_ref)
    if gp_ref is not None:
        gp_ref[...] = jnp.zeros_like(gp_ref)
    heads, zero = head_lanes(), jnp.zeros((), BF16)
    work = [(block, h) for block in blocks_of(length) for h in range(GROUP)]

    def ask(n):
        block, h = work[n]
        i, _, last, (low, high) = block
        if h == 0:
            fill_mask(mask_ref, seg_col, seg_row, block)
        rows = slice(i * QB, last)
        asked = jnp.where(heads == h, q_ref[rows, :], zero)
        grad = jnp.where(heads == h, do_ref[rows, :], zero)
        s_ref[n % 2, 0 : high - low, :] = dot(ke_ref[low:high, :], asked, NT) + mask_ref[low:high, :]
        dp_ref[n % 2, 0 : high - low, :] = dot(ve_ref[low:high, :], grad, NT)

    ask(0)
    for n, (block, h) in enumerate(work):
        if n + 1 < len(work):
            ask(n + 1)
        i, first, last, (low, high) = block
        rows, span = slice(i * QB, last), slice(h * HD, (h + 1) * HD)
        (pa, pb), (ta, tb) = strip_parts(block)
        p = jnp.exp(s_ref[n % 2, 0 : high - low, :] - lse_ref[h : h + 1, rows])
        ds = (p * (dp_ref[n % 2, 0 : high - low, :] - delta_ref[h : h + 1, rows])).astype(BF16)
        p = p.astype(BF16)
        dq = dot(kt_ref[span, first:last], ds[ta:tb]) + dot(pkt[span, :], ds[pa:pb])
        gjt_ref[span, rows] = dq.astype(BF16) * jnp.asarray(HD ** (-0.5), BF16)
        acc_ref[0, span, first:last] += dot(qt_ref[span, rows], ds[ta:tb], NT)
        acc_ref[1, span, first:last] += dot(dot_ref[span, rows], p[ta:tb], NT)
        if gp_ref is not None:
            gp_ref[0, span, :] += dot(qt_ref[span, rows], ds[pa:pb], NT)
            gp_ref[1, span, :] += dot(dot_ref[span, rows], p[pa:pb], NT)
    gjt_ref[WIDE : 2 * WIDE, :] = acc_ref[0].astype(BF16)
    gjt_ref[2 * WIDE : 3 * WIDE, :] = acc_ref[1].astype(BF16)


def take_own(out_ref, rows, values, index):
    width = out_ref.shape[1]
    for k in range(values.shape[1] // width):

        @pl.when(index == k)
        def _():
            out_ref[rows, :] = values[:, k * width : (k + 1) * width].astype(out_ref.dtype)


def norm_back(grad, normed, inverse, gain):
    scaled = grad * gain
    mean = jnp.mean(scaled, axis=-1, keepdims=True)
    return inverse * (scaled - mean - normed * jnp.mean(scaled * normed, axis=-1, keepdims=True))


def back_own_kernel(prefix_count, places_ref, res_ref, cot_ref, gm_ref, gain_ref, w_ref, q_ref, k_ref, v_ref, att_ref,
                    lse_ref, small_ref, segr_ref, low_ref, part_ref, sums_ref, gjt_ref, gp_ref, ga_ref, *scratch):
    length = res_ref.shape[0]
    sums = [0.0] * 4
    for t in range(0, length, TB):
        rows = slice(t, t + TB)
        normed, inverse = normalize(res_ref[rows, :])
        gm, cot = gm_ref[rows, :], cot_ref[rows, :].astype(F32)
        grad = cot + norm_back(gm, normed, inverse, gain_ref[...])
        low_ref[rows, :] = grad.astype(BF16)
        take_own(part_ref, rows, grad, places_ref[0])
        for n, values in enumerate((gm * normed, gm, grad, cot)):
            sums[n] = sums[n] + jnp.sum(values, axis=0, keepdims=True)
    for n in range(4):
        sums_ref[n : n + 1, :] = sums[n]
    back_body(prefix_count, extras(places_ref[1], small_ref, False), w_ref, q_ref, k_ref, v_ref, att_ref, lse_ref,
              segr_ref, low_ref, gjt_ref, gp_ref, *scratch)
    w = w_ref[0:3].reshape(3 * WIDE, w_ref.shape[2])
    for t in range(0, length, TB):
        ga_ref[t : t + TB, :] = dot(gjt_ref[:, t : t + TB], w, TN)


def back_others_kernel(prefix_count, places_ref, w_ref, q_ref, k_ref, v_ref, att_ref, lse_ref, small_ref, segr_ref,
                       low_ref, in_ref, tok_ref, part_ref, gain_ref, out_ref, sums_ref, ga_ref, gjt_ref, *scratch):
    back_body(prefix_count, extras(places_ref[1], small_ref, True), w_ref, q_ref, k_ref, v_ref, att_ref, lse_ref,
              segr_ref, low_ref, gjt_ref, None, *scratch)
    w = w_ref[0:3].reshape(3 * WIDE, w_ref.shape[2])
    length, step = low_ref.shape[0], pl.program_id(0)
    final = pl.num_programs(0) - 1

    @pl.when(step == 0)
    def _():
        for t in range(0, length, TB):
            ga_ref[t : t + TB, :] = in_ref[t : t + TB, :] + dot(gjt_ref[:, t : t + TB], w, TN)

    @pl.when((step > 0) & (step < final))
    def _():
        for t in range(0, length, TB):
            ga_ref[t : t + TB, :] += dot(gjt_ref[:, t : t + TB], w, TN)

    @pl.when(step == final)
    def _():
        sums = [0.0, 0.0]
        for t in range(0, length, TB):
            rows = slice(t, t + TB)
            ga = ga_ref[rows, :] + dot(gjt_ref[:, rows], w, TN)
            normed, inverse = normalize(tok_ref[rows, :].astype(F32))
            grad = norm_back(ga, normed, inverse, gain_ref[...])
            width = out_ref.shape[1]
            for k in range(grad.shape[1] // width):

                @pl.when(places_ref[0] == k)
                def _():
                    out_ref[rows, :] = (part_ref[rows, :] + grad[:, k * width : (k + 1) * width]).astype(BF16)

            sums[0] = sums[0] + jnp.sum(ga * normed, axis=0, keepdims=True)
            sums[1] = sums[1] + jnp.sum(ga, axis=0, keepdims=True)
        sums_ref[...] = jnp.zeros_like(sums_ref)
        for n in range(2):
            take_own(sums_ref, slice(n, n + 1), sums[n], places_ref[0])


def back_own(prefix_count, *args):
    length, width = args[1].shape
    return resident(
        functools.partial(back_own_kernel, prefix_count),
        [
            shape_of((length, width), BF16),
            shape_of((length, WIDE), F32),
            shape_of((8, width), F32),
            shape_of((3 * WIDE, length), BF16),
            shape_of((2, WIDE, PAD), F32),
            shape_of((length, width), F32),
        ],
        back_scratch(length),
        "back_own",
        30,
        args,
    )


def back_others(prefix_count, places, saved, small, seg, low, ga, tokens, part, gain):
    length, width = low.shape
    return pl.pallas_call(
        functools.partial(back_others_kernel, prefix_count),
        grid=(saved[0].shape[0],),
        in_specs=[SCALARS]
        + [each(*values.shape[1:]) for values in saved]
        + [rows_of(48, WIDE)]
        + [once(values) for values in (seg, low, ga, tokens, part, gain)],
        out_specs=[pl.BlockSpec((length, WIDE), lambda g: (0, 0)), pl.BlockSpec((8, WIDE), lambda g: (0, 0))],
        out_shape=[shape_of((length, WIDE), BF16), shape_of((8, WIDE), F32)],
        scratch_shapes=[pltpu.VMEM((length, width), F32), pltpu.VMEM((3 * WIDE, length), BF16)] + back_scratch(length),
        cost_estimate=BRIEF,
        compiler_params=params(50),
        name="back_others",
    )(places, *saved, small, seg, low, ga, tokens, part, gain)


def gelu_pair(v):
    c = 0.7978845608028654
    square = v * v
    t = jnp.tanh(v * (c + (0.044715 * c) * square))
    half = 0.5 + 0.5 * t
    return v * half, half + (0.5 * v) * (1.0 - t * t) * (c + (3.0 * 0.044715 * c) * square)


def mix_rows(mid, cot, up_ref, up_dims, bias, down_ref, act_ref, gp_ref, rows, pre_ref, g_ref):
    hidden = down_ref.shape[0]
    chunks = [slice(c, c + TB) for c in range(0, hidden, TB)]

    def ask(n):
        up = up_ref[:, chunks[n]] if up_dims is NN else up_ref[chunks[n], :]
        pre_ref[n % 2] = dot(mid, up, up_dims) + bias[:, chunks[n]]
        g_ref[n % 2] = dot(cot, down_ref[chunks[n], :], NT)

    ask(0)
    for n, chunk in enumerate(chunks):
        if n + 1 < len(chunks):
            ask(n + 1)
        act, slope = gelu_pair(pre_ref[n % 2])
        act_ref[rows, chunk] = act.astype(BF16)
        gp_ref[rows, chunk] = (g_ref[n % 2] * slope).astype(BF16)


def mix_own_kernel(z_ref, res_ref, cot_ref, gain_ref, shift_ref, up_ref, bias_ref, down_ref, dbias_ref,
                   mid_ref, act_ref, gp_ref, share_ref, bsum_ref, gm_ref, pre_ref, g_ref):
    width = share_ref.shape[1]
    own = pl.ds(pl.multiple_of(z_ref[0] * width, width), width)
    every = slice(0, TB)
    normed, _ = normalize(res_ref[...])
    mid = (normed * gain_ref[...] + shift_ref[...]).astype(BF16)
    mid_ref[...] = mid
    mix_rows(mid, cot_ref[...], up_ref, NN, bias_ref[...], down_ref, act_ref, gp_ref, every, pre_ref, g_ref)
    share_ref[...] = res_ref[:, own] + dbias_ref[:, own] + dot(act_ref[...], down_ref[:, own])
    gp = gp_ref[...]
    gm_ref[...] = dot(gp, up_ref[...], NT)

    @pl.when(pl.program_id(0) == 0)
    def _():
        bsum_ref[...] = jnp.zeros_like(bsum_ref)

    bsum_ref[...] += jnp.sum(gp.astype(F32), axis=0, keepdims=True)


def mix_own(own_width, z, residual, cotangent, gain, shift, up, up_bias, down, down_bias):
    length, width = residual.shape
    hidden = up.shape[1]
    rows = lambda w: rows_of(TB, w)
    fixed = [once(values) for values in (gain, shift, up, up_bias, down, down_bias)]
    return pl.pallas_call(
        mix_own_kernel,
        grid=(length // TB,),
        in_specs=[SCALARS, rows(width), rows(width)] + fixed,
        out_specs=[rows(width), rows(hidden), rows(hidden), rows(own_width), pl.BlockSpec((1, hidden), lambda t: (0, 0)), rows(width)],
        out_shape=[
            shape_of((length, width), BF16),
            shape_of((length, hidden), BF16),
            shape_of((length, hidden), BF16),
            shape_of((length, own_width), F32),
            shape_of((1, hidden), F32),
            shape_of((length, width), F32),
        ],
        scratch_shapes=[pltpu.VMEM((2, TB, TB), F32)] * 2,
        cost_estimate=BRIEF,
        compiler_params=params(36),
        name="mix_own",
    )(z, residual, cotangent, gain, shift, up, up_bias, down, down_bias)


def mix_kernel(places, z_ref, mid_ref, cot_ref, small_ref, share_in, gm_in, *refs):
    pieces, per = len(places), 128
    share_ref, gm_ref, up_ref, down_ref, part_ref, act_ref, gp_ref, pre_ref, g_ref = refs[2 * pieces :]
    width = share_ref.shape[1]
    own = pl.ds(pl.multiple_of(z_ref[0] * width, width), width)

    @pl.when(pl.program_id(0) == 0)
    def _():
        for j in range(pieces):
            up_ref[j * per : (j + 1) * per, :] = refs[2 * j][...].astype(BF16)
            down_ref[j * per : (j + 1) * per, :] = refs[2 * j + 1][...].astype(BF16)
        part_ref[...] = down_ref[:, own]

    biases = {k: reorder(small_ref[48 * k + 40 : 48 * k + 48, 0:per], z_ref[1], 0) for k, _ in places}
    bias = jnp.concatenate([biases[k][j : j + 1] for k, j in places], axis=1)
    every = slice(0, TB)
    mix_rows(mid_ref[...], cot_ref[...], up_ref, NT, bias, down_ref, act_ref, gp_ref, every, pre_ref, g_ref)
    share_ref[...] = (share_in[...] + dot(act_ref[...], part_ref[...])).astype(share_ref.dtype)
    gm_ref[...] = gm_in[...] + dot(gp_ref[...], up_ref[...])


def mix(places, blocks, last, z, mid, cotangent, small, share, gm, *arrays):
    length, width = mid.shape
    hidden = 128 * len(places)
    own_width = share.shape[1]
    rows = lambda w: rows_of(TB, w)
    low = lambda *shape: pltpu.VMEM(shape, BF16)
    piece = lambda at: pl.BlockSpec((128, width), lambda t: (at, 0), pipeline_mode=pl.Buffered(1))
    return pl.pallas_call(
        functools.partial(mix_kernel, places),
        grid=(length // TB,),
        in_specs=[SCALARS, rows(width), rows(width), once(small), rows(own_width), rows(width)]
        + [piece(at) for at in blocks],
        out_specs=[rows(own_width), rows(width)],
        out_shape=[shape_of((length, own_width), BF16 if last else F32), shape_of((length, width), F32)],
        scratch_shapes=[low(hidden, width), low(hidden, width), low(hidden, own_width), low(TB, hidden), low(TB, hidden)]
        + [pltpu.VMEM((2, TB, TB), F32)] * 2,
        input_output_aliases={5: 1} if last else {4: 0, 5: 1},
        cost_estimate=BRIEF,
        compiler_params=params(40),
        name="mix_others",
    )(z, mid, cotangent, small, share, gm, *arrays)


def hidden_grad_kernel(member_ref, mid_ref, cot_ref, gp_ref, act_ref, keep_ref, send_ref):
    half = TB // 2
    for at, left, right in ((0, mid_ref, gp_ref), (half, cot_ref, act_ref)):
        grad = dot(left[...], right[...], TN)
        for core in range(2):

            @pl.when((member_ref[0] & 1) == core)
            def _():
                keep_ref[at : at + half, :] = grad[core * half : (core + 1) * half]
                send_ref[at : at + half, :] = grad[(1 - core) * half : (2 - core) * half]


def hidden_grad(member, mid, cotangent, gp, act):
    length, width = mid.shape
    hidden = gp.shape[1]
    column = pl.BlockSpec((length, TB), lambda j, m: (0, j))
    whole = pl.BlockSpec((length, hidden), lambda j, m: (0, 0), pipeline_mode=pl.Buffered(1))
    out = pl.BlockSpec((None, TB, hidden), lambda j, m: (j ^ (m[0] >> 1), 0, 0))
    return pl.pallas_call(
        hidden_grad_kernel,
        grid_spec=pltpu.PrefetchScalarGridSpec(
            num_scalar_prefetch=1,
            grid=(width // TB,),
            in_specs=[column, column, whole, whole],
            out_specs=[out, out],
        ),
        out_shape=[shape_of((width // TB, TB, hidden), F32)] * 2,
        cost_estimate=BRIEF,
        compiler_params=params(30),
        name="hidden_grad",
    )(member, mid, cotangent, gp, act)


def fold_kernel(z_ref, keep_ref, got_ref, near_ref, far_x_ref, far_y_ref, stay_ref):
    half = keep_ref.shape[1] // 2
    for s in range(4):
        total = keep_ref[s] + got_ref[s]
        top, bottom = total[:half], total[half:]
        if s == 0:
            near_ref[...] = total
        if s == 1:
            far_x_ref[0] = top
            stay_ref[1] = bottom
        if s == 2:
            stay_ref[0] = top
            far_y_ref[0] = bottom
        if s == 3:
            far_x_ref[1] = top
            far_y_ref[1] = bottom


def fold(z, keep, got):
    _, rows, hidden = keep.shape
    lanes = 256
    block = lambda *shape: pl.BlockSpec(shape + (lanes,), lambda g: (0,) * len(shape) + (g,))
    two = (2, rows // 2)
    return pl.pallas_call(
        fold_kernel,
        grid=(hidden // lanes,),
        in_specs=[SCALARS, block(4, rows), block(4, rows)],
        out_specs=[block(rows), block(*two), block(*two), block(*two)],
        out_shape=[shape_of((rows, hidden), F32)] + [shape_of(two + (hidden,), F32)] * 3,
        cost_estimate=BRIEF,
        compiler_params=params(20),
        name="fold",
    )(z, keep, got)


def head_grad_kernel(prefix_count, z_ref, x_ref, low_ref, gjt_ref, att_ref, gp_ref, sums_ref, ups_ref, outer_ref,
                     out_ref, pack_ref):
    wide = gjt_ref.shape[0]
    for start, left, right in ((0, gjt_ref, x_ref), (wide, att_ref, low_ref)):
        for r in range(0, left.shape[0], TB):
            grad = dot(left[r : r + TB, :], right[...])
            for j in range(out_ref.shape[0]):
                out_ref[j, start + r : start + r + TB, :] = grad[:, 128 * j : 128 * (j + 1)]
    pack_ref[...] = jnp.zeros_like(pack_ref)
    inner = 0.0
    for k in range(2):
        gp = gp_ref[k].T
        pack_ref[k * PAD : (k + 1) * PAD, :] = gp
        for _ in range(3):
            part = gp.astype(BF16)
            inner = inner + dot(part, outer_ref[:, k * WIDE : (k + 1) * WIDE], NT)
            gp = gp - part.astype(F32)
    for k in range(sums_ref.shape[1] // WIDE):

        @pl.when(z_ref[0] == k)
        def _():
            pack_ref[2 * PAD : 2 * PAD + 4, :] = sums_ref[0:4, k * WIDE : (k + 1) * WIDE]

    ones = jnp.ones((8, gjt_ref.shape[1]), BF16)
    joint = dot(ones, gjt_ref[...], NT)
    for k in range(3):
        pack_ref[2 * PAD + 4 + k : 2 * PAD + 5 + k, :] = joint[0:1, k * WIDE : (k + 1) * WIDE]
    for k in range(ups_ref.shape[1] // WIDE):
        pack_ref[2 * PAD + 8 + k : 2 * PAD + 9 + k, :] = ups_ref[:, k * WIDE : (k + 1) * WIDE]
    begin = 2 * PAD + 8 + ups_ref.shape[1] // WIDE
    for k in range(inner.shape[1] // WIDE):
        to = slice(begin + k * prefix_count, begin + (k + 1) * prefix_count)
        pack_ref[to, :] = inner[0:prefix_count, k * WIDE : (k + 1) * WIDE]


def head_grad(prefix_count, *args):
    width = args[1].shape[1]
    rows = args[3].shape[0] + args[4].shape[0]
    packed = 2 * PAD + 8 + args[7].shape[1] // WIDE + args[8].shape[0] // WIDE * prefix_count
    return resident(
        functools.partial(head_grad_kernel, prefix_count),
        [shape_of((width // 128, rows, 128), F32), shape_of((-(-packed // 8) * 8, WIDE), F32)],
        [],
        "head_grad",
        16,
        args,
    )


def shards(
    tokens, segment_ids, attention_gain, attention_shift, joint_weight, joint_bias, output_weight, output_bias,
    mixer_gain, mixer_shift, up_weight, up_bias, down_weight, down_bias, prefix_table, inner_weight, inner_bias,
    outer_weight, outer_bias, cotangent,
):
    length, width = tokens.shape
    local = joint_weight.shape[2]
    hidden = up_weight.shape[1]
    prefix_count = prefix_table.shape[0]
    batch_size, tensor_size = lax.axis_size("batch"), lax.axis_size("tensor")
    z = lax.axis_index("tensor").astype(jnp.int32)
    member = (lax.axis_index("batch") % 8).astype(jnp.int32)
    member_arr, places = member.reshape(1), jnp.stack([z, member])

    def own_columns(values):
        return lax.dynamic_slice_in_dim(values, z * local, local, values.ndim - 1)

    def along(values, k):
        return lax.ppermute(values, "tensor", [(i, i ^ k) for i in range(tensor_size)])

    def across(values, k):
        return lax.ppermute(values, "batch", [(i, i ^ k) for i in range(batch_size)])

    now = [member_arr]

    def after(values):
        return lax.optimization_barrier((values, *now))[0]

    def wait(*values):
        held = lax.optimization_barrier((*values, *now))
        now[:] = [held[0]]
        return held[0] if len(values) == 1 else held[: len(values)]

    def run(call, *args):
        outs = call(after(args[0]), *args[1:])
        now[:] = [outs[-1] if isinstance(outs, (list, tuple)) else outs]
        return outs

    row = lambda v: v.reshape(1, -1)
    stack = lambda *parts: jnp.concatenate(parts, axis=0)

    def gather(*parts):
        places = [(start, rows) for _, start, rows in parts]
        arrays = [values for values, _, _ in parts]
        return run(lambda *arrays: gather_rows(places, *arrays), *arrays)

    def rows(values, block, count=1):
        return values, block * 128, count * 128

    whole = lambda values: (values, 0, values.shape[0])

    own_heads, send_heads = run(head_pieces, member_arr, joint_weight, output_weight)
    a1, a2 = along(after(send_heads[0]), 1), along(after(send_heads[0]), 2)

    def prefixes(prefix_table, inner_weight):
        hidden_prefix = jnp.tanh(jnp.dot(prefix_table, inner_weight.astype(F32), precision=PRECISE) + inner_bias)
        pairs = jnp.einsum("pr,rke->kpe", hidden_prefix, outer_weight.astype(F32), precision=PRECISE)
        pairs = jnp.pad(pairs + outer_bias[:, None, :], ((0, 0), (0, PAD - prefix_count), (0, 0)))
        ups = jnp.pad(up_bias.reshape(8, hidden // 8), ((0, 0), (0, local - hidden // 8)))
        joints = jnp.pad(joint_bias, ((0, 5), (0, 0)))
        return hidden_prefix, stack(pairs.reshape(2 * PAD, local), joints, ups)

    hidden_prefix, small = run(prefixes, prefix_table, inner_weight)
    send_hidden = run(hidden_pieces, member_arr, up_weight, down_weight)
    a1, a2 = wait(a1, a2)
    a12 = gather(whole(a1), whole(a2))
    x12, y12 = across(after(a12), 2), across(after(a12), 4)
    a3, a1d = along(after(send_heads[0]), 3), along(after(send_heads[1]), 1)
    c12 = across(after(a12), 1)
    x, *saved_own, residual = run(
        functools.partial(attend_own, prefix_count),
        member_arr, tokens, row(attention_gain), row(attention_shift), own_heads, small, segment_ids, row(output_bias),
    )
    x12, y12, a3, a1d, c12 = wait(x12, y12, a3, a1d, c12)

    y3 = gather(whole(a3), rows(x12, 1))
    x3, y3 = across(after(a3), 2), across(after(y3), 4)
    f1, f2 = along(after(send_hidden[0]), 1), along(after(send_hidden[0]), 2)
    gb = gather(whole(x12), whole(y12), whole(a3))
    cb = across(after(gb), 1)
    x3, y3, cb = wait(x3, y3, cb)
    a3d = across(after(y3[0:128]), 2)
    a3d, f1, f2 = wait(a3d, f1, f2)

    smalls = [along(after(small), k) for k in (1, 2, 3)]
    f12 = gather(whole(f1), whole(f2))
    gc = gather(whole(a1d), rows(y3, 1), whole(x3), rows(y3, 0), whole(a3d))
    extra = run(stack, *wait(*smalls))
    fx, fy = across(after(f12), 2), across(after(f12), 4)
    f3, f1d = along(after(send_hidden[0]), 3), along(after(send_hidden[1]), 1)
    cc = wait(across(after(gc), 1))
    *saved_others, residual = run(
        functools.partial(attend_others, prefix_count, 0, 2, 3),
        member_arr, x, [(a12, 0), (c12, 0), (x12, 0), (cb, 0), (y12, 0), (cb, 2), (gc, 0), (cc, 0)], extra,
        segment_ids, residual,
    )
    *saved_others, residual = run(
        functools.partial(attend_others, prefix_count, 2, 1, 3),
        member_arr, x, [(a3, 0), (cb, 4), (x3, 0), (cc, 2), (y3, 0), (cc, 3), (gc, 4), (cc, 4)], extra,
        segment_ids, residual, saved_others,
    )
    fx, fy, f3, f1d = wait(fx, fy, f3, f1d)

    x4 = gather(whole(f3), rows(fy, 3))
    y4 = gather(whole(f3), rows(fx, 2))
    x4, y4 = across(after(x4), 2), across(after(y4), 4)
    g1 = gather(whole(f1), rows(fx, 0, 2), rows(fy, 0, 2), whole(f1d))
    c1 = across(after(g1), 1)
    mid, act, gp, share, up_bias_sum, gm = run(
        functools.partial(mix_own, local),
        places, residual, cotangent, row(mixer_gain), row(mixer_shift), up_weight, row(up_bias), down_weight,
        row(down_bias),
    )
    quick = batch_size == 8
    if quick:
        keep, send = run(hidden_grad, member_arr, mid, cotangent, gp, act)
    c1 = wait(c1)

    def mix_more(pieces, share, gm, last=False):
        order = [(slot, j) for slot, j, _, _ in pieces]
        flat = [part for _, _, up, down in pieces for part in (up, down)]
        return run(
            functools.partial(mix, order, [at for _, at in flat], last),
            places, mid, cotangent, extra, share, gm, *[values for values, _ in flat],
        )

    def pair(values, at):
        return (values, at), (values, at + 1)

    share, gm = mix_more(
        [(0, 2 * k + side, *pair(values, 2 * k)) for k in range(4) for side, values in ((0, g1), (1, c1))], share, gm
    )
    x4, y4 = wait(x4, y4)

    x5, y5 = across(after(y4[128:256]), 2), across(after(x4[0:128]), 4)
    g2 = gather(whole(f2), rows(fx, 2, 2), rows(fy, 2, 2))
    c2 = wait(across(after(g2), 1))
    g3 = gather(rows(y4, 2), rows(x4, 2), whole(f3), rows(x4, 0, 2), rows(y4, 0, 2))
    c3 = across(after(g3), 1)
    share, gm = mix_more(
        [(1, 2 * k + side, *pair(values, 2 * k)) for k in range(3) for side, values in ((0, g2), (1, c2))], share, gm
    )
    x5, y5, c3 = wait(x5, y5, c3)

    g4 = gather(whole(y5), whole(x5))
    c4 = across(after(g4), 1)
    if quick:
        got = across(after(send), 1)
    pieces = [(1, 6 + side, *pair(values, 0)) for side, values in ((0, g3), (1, c3))]
    pieces += [(2, 2 * k + side, *pair(values, 2 + 2 * k)) for k in range(3) for side, values in ((0, g3), (1, c3))]
    share, gm = mix_more(pieces, share, gm)
    c4 = wait(c4)
    share, gm = mix_more([(2, 6 + side, *pair(values, 0)) for side, values in ((0, g4), (1, c4))], share, gm, True)
    if quick:
        got = wait(got)
        near, far_x, far_y, stay = run(fold, places, keep, got)
        far_x, far_y = across(after(far_x), 2), across(after(far_y), 4)
    low, part, sums, gjt, gprefix, ga = run(
        functools.partial(back_own, prefix_count),
        places, residual, cotangent, gm, row(mixer_gain), own_heads, *saved_own, small, segment_ids,
    )
    if quick:
        far_x, far_y = wait(far_x, far_y)

        def halfway(stay, near, far_x, far_y):
            return stay[0] + far_x[1], stay[1] + far_y[1], near + stack(far_x[0], far_y[0])

        top, bottom, near = run(halfway, stay, near, far_x, far_y)
        top, bottom = across(after(top), 4), across(after(bottom), 2)
    head_part, totals = run(
        functools.partial(head_grad, prefix_count),
        places, x, low, gjt, saved_own[3], gprefix, sums, up_bias_sum, outer_weight.reshape(outer_weight.shape[0], -1),
    )
    per = width // batch_size
    head_part = head_part.reshape(-1, 4 * local, 128 // per, per).transpose(0, 2, 1, 3)
    head_sum = lax.psum_scatter(
        after(head_part.reshape(batch_size, 4 * local, per)), "batch", scatter_dimension=0, tiled=False
    )

    def spread(values, send, bits):
        if len(bits) == 1:
            return (send(after(values), bits[0]),)
        return tuple(send(after(values), k) for k in (bits[0], bits[1], bits[0] + bits[1]))

    def gather(values, others):
        others = wait(*others) if len(others) > 1 else (wait(*others),)
        total = values + others[0]
        return total + (others[1] + others[2]) if len(others) == 3 else total

    def rounds_of(send, size):
        bits = [1 << b for b in range((size - 1).bit_length())]
        return [(send, bits[k : k + 2]) for k in range(0, len(bits), 2)]

    over_batch, over_tensor = rounds_of(across, batch_size), rounds_of(along, tensor_size)
    turns = over_batch + over_tensor
    done = 0
    batch_totals = None

    def turn(others):
        nonlocal totals, done, batch_totals
        totals = gather(totals, others)
        done += 1
        if done == len(over_batch):
            batch_totals = totals

    others = spread(totals, *turns[0])
    tokens_gradient, gain_sums = run(
        functools.partial(back_others, prefix_count),
        places, saved_others, extra, segment_ids, low, ga, tokens, part, row(attention_gain),
    )
    turn(others)
    if quick:
        top, bottom = wait(top, bottom)
        hidden_sum = near + stack(top, bottom)
    else:
        ups = jnp.dot(mid.T, gp, preferred_element_type=F32).reshape(batch_size, per, hidden)
        downs = jnp.dot(cotangent.T, act, preferred_element_type=F32).reshape(batch_size, per, hidden)
        hidden_sum = lax.psum_scatter(jnp.concatenate([ups, downs], axis=1), "batch", scatter_dimension=0, tiled=False)
    for n in range(max(len(turns) - 1, len(over_batch))):
        first = spread(totals, *turns[done]) if done < len(turns) else None
        second = spread(gain_sums, *over_batch[n]) if n < len(over_batch) else None
        if first is not None:
            turn(first)
        if second is not None:
            gain_sums = gather(gain_sums, second)
    split = 2 * PAD + 8 + hidden // local
    halves = outer_weight.shape[0] // local
    inner = totals[split : split + halves * prefix_count].reshape(halves, prefix_count, local)

    grad_prefix = batch_totals[: 2 * PAD].reshape(2, PAD, local)[:, :prefix_count]
    mixed_total = batch_totals[2 * PAD : 2 * PAD + 4]
    joint_bias_total = batch_totals[2 * PAD + 4 : 2 * PAD + 7]
    up_bias_total = batch_totals[2 * PAD + 8 : split]
    grad_hidden_prefix = inner.transpose(1, 0, 2).reshape(prefix_count, -1)
    outer_rows = outer_weight.shape[0] // batch_size
    hidden_own = lax.dynamic_slice_in_dim(hidden_prefix, lax.axis_index("batch") * outer_rows, outer_rows, 1)
    outer_total = jnp.einsum("pr,kpe->rke", hidden_own, grad_prefix, precision=PRECISE)
    outer_bias_total = jnp.sum(grad_prefix, axis=1)
    grad_inner = grad_hidden_prefix * (1.0 - hidden_prefix * hidden_prefix)
    inner_total = jnp.einsum("pd,pr->dr", prefix_table, grad_inner, precision=PRECISE)
    inner_bias_total = jnp.sum(grad_inner, axis=0)
    table_total = jnp.einsum("pr,dr->pd", grad_inner, inner_weight.astype(F32), precision=PRECISE)

    up_total, down_total = hidden_sum[:per], hidden_sum[per:].T
    joint_total = head_sum[: 3 * local].reshape(3, local, per).transpose(0, 2, 1)
    output_total = head_sum[3 * local :]
    return (
        share,
        tokens_gradient,
        gain_sums[0],
        gain_sums[1],
        joint_total,
        joint_bias_total,
        output_total,
        mixed_total[2],
        mixed_total[0],
        mixed_total[1],
        up_total,
        up_bias_total.reshape(hidden),
        down_total,
        mixed_total[3],
        table_total,
        inner_total,
        inner_bias_total,
        outer_total,
        outer_bias_total,
    )


def solution(mesh):
    placed = (
        P("batch", None),
        P("batch", None),
        P(),
        P(),
        P(None, None, "tensor"),
        P(None, "tensor"),
        P("tensor", None),
        P(),
        P(),
        P(),
        P(None, "tensor"),
        P("tensor"),
        P("tensor", None),
        P(),
        P(),
        P(),
        P(),
        P(None, None, "tensor"),
        P(None, "tensor"),
        P("batch", None),
    )
    return jax.shard_map(
        shards,
        mesh=mesh,
        in_specs=placed,
        out_specs=(
            P("batch", "tensor"),
            P("batch", "tensor"),
            P("tensor"),
            P("tensor"),
            P(None, "batch", "tensor"),
            P(None, "tensor"),
            P("tensor", "batch"),
            P("tensor"),
            P("tensor"),
            P("tensor"),
            P("batch", "tensor"),
            P("tensor"),
            P("tensor", "batch"),
            P("tensor"),
            P(),
            P(),
            P(),
            P("batch", None, "tensor"),
            P(None, "tensor"),
        ),
        check_vma=False,
    )
```

```python
import functools

import jax
import jax.numpy as jnp
from jax import lax
from jax.experimental import pallas as pl
from jax.experimental.pallas import tpu as pltpu
from jax.sharding import PartitionSpec as P

HD = 64
GROUP = 4
WIDE = GROUP * HD
QB = 256
CUT = 64
PAD = 16
TB = 256
EPSILON = 1e-05
PRECISE = lax.Precision.HIGHEST
NEGATIVE = -1e30
F32, BF16 = jnp.float32, jnp.bfloat16
NN = (((1,), (0,)), ((), ()))
NT = (((1,), (1,)), ((), ()))
TN = (((0,), (0,)), ((), ()))
shape_of = jax.ShapeDtypeStruct
BRIEF = pl.CostEstimate(flops=1024, bytes_accessed=1024, transcendentals=0)


def dot(a, b, dims=NN):
    return lax.dot_general(a, b, dims, preferred_element_type=F32)


def params(mib):
    return pltpu.CompilerParams(vmem_limit_bytes=mib * 2**20)


def resident(kernel, outs, scratch, name, mib, args, aliases={}):
    vm = pl.BlockSpec(memory_space=pltpu.VMEM)
    return pl.pallas_call(
        kernel,
        out_shape=outs,
        in_specs=[pl.BlockSpec(memory_space=pltpu.SMEM)] + [vm] * (len(args) - 1),
        out_specs=[vm] * len(outs),
        scratch_shapes=scratch,
        input_output_aliases=aliases,
        cost_estimate=BRIEF,
        compiler_params=params(mib),
        name=name,
    )(*args)


def normalize(values):
    centered = values - jnp.mean(values, axis=-1, keepdims=True)
    inverse = lax.rsqrt(jnp.mean(centered * centered, axis=-1, keepdims=True) + EPSILON)
    return centered * inverse, inverse


def heads_kernel(turn, member_ref, joint_ref, out_ref, own_ref, send_ref):
    for c in range(3):
        own_ref[c] = joint_ref[c].T
    own_ref[3] = out_ref[...]
    rows = own_ref.shape[1] // 8
    for p in range(2):
        member = member_ref[0] ^ (turn * p)
        start = pl.multiple_of(member * rows, rows)
        for c in range(4):
            send_ref[p, c * rows : (c + 1) * rows, :] = own_ref[c, pl.ds(start, rows), :].astype(F32)


def head_pieces(member, joint_weight, output_weight):
    _, width, local = joint_weight.shape
    vm = pl.BlockSpec(memory_space=pltpu.VMEM)
    return pl.pallas_call(
        functools.partial(heads_kernel, 6),
        out_shape=[shape_of((4, local, width), BF16), shape_of((2, local // 2, width), F32)],
        in_specs=[pl.BlockSpec(memory_space=pltpu.SMEM), vm, vm],
        out_specs=[vm, vm],
        cost_estimate=BRIEF,
        compiler_params=params(12),
        name="head_pieces",
    )(member, joint_weight, output_weight)


def hidden_kernel(member_ref, up_ref, down_ref, send_ref):
    rows = down_ref.shape[0]
    send_ref[0, 0:rows, :] = up_ref[...].T.astype(F32)
    send_ref[0, rows : 2 * rows, :] = down_ref[...].astype(F32)


def hidden_pieces(member, up_weight, down_weight):
    width, local = up_weight.shape
    rows = local // 8
    return pl.pallas_call(
        hidden_kernel,
        out_shape=shape_of((2, 2 * rows, width), F32),
        grid_spec=pltpu.PrefetchScalarGridSpec(
            num_scalar_prefetch=1,
            grid=(2,),
            in_specs=[
                pl.BlockSpec((width, rows), lambda p, m: (0, m[0] ^ (6 * p))),
                pl.BlockSpec((rows, width), lambda p, m: (m[0] ^ (6 * p), 0)),
            ],
            out_specs=pl.BlockSpec((1, 2 * rows, width), lambda p, m: (p, 0, 0)),
        ),
        cost_estimate=BRIEF,
        compiler_params=params(12),
        name="hidden_pieces",
    )(member, up_weight, down_weight)


def gather_kernel(places, *refs):
    sources, out_ref, sems = refs[: len(places)], refs[len(places)], refs[-1]
    copies, to = [], 0
    for (start, rows), ref in zip(places, sources):
        for at in range(0, rows, CUT):
            source, target = ref.at[pl.ds(start + at, CUT)], out_ref.at[pl.ds(to + at, CUT)]
            copies.append(pltpu.make_async_copy(source, target, sems.at[len(copies)]))
        to += rows
    for copy in copies:
        copy.start()
    for copy in copies:
        copy.wait()


def gather_rows(places, *arrays):
    anywhere = pl.BlockSpec(memory_space=pl.ANY)
    return pl.pallas_call(
        functools.partial(gather_kernel, places),
        in_specs=[anywhere] * len(arrays),
        out_specs=pl.BlockSpec(memory_space=pltpu.VMEM),
        out_shape=shape_of((sum(rows for _, rows in places), arrays[0].shape[1]), F32),
        scratch_shapes=[pltpu.SemaphoreType.DMA((sum(rows for _, rows in places) // CUT,))],
        cost_estimate=BRIEF,
        compiler_params=params(8),
        name="gather_rows",
    )(*arrays)


def reorder(values, member, dim=1):
    block = values.shape[dim] // 8
    place = lax.broadcasted_iota(jnp.int32, values.shape, dim) // block
    for bit in (1, 2, 4):
        up = pltpu.roll(values, block * bit, dim)
        down = pltpu.roll(values, values.shape[dim] - block * bit, dim)
        turned = jnp.where((place & bit) != 0, up, down)
        values = jnp.where((member & bit) != 0, turned, values)
    return values


def column_of(seg_row):
    wide = jnp.broadcast_to(seg_row.astype(F32), (128, seg_row.shape[1]))
    return wide.T[:, 0:1].astype(jnp.int32)


def extras(member, small_ref, others):
    small = small_ref[0:40, :]
    if others:
        small = reorder(small, member)
    return small[0:PAD].astype(BF16), small[PAD : 2 * PAD].astype(BF16), small[2 * PAD : 2 * PAD + 8]


def blocks_of(length):
    out = []
    for i in range(length // QB):
        first = max(0, (i * QB - length // 2 + 1) // QB) * QB
        last = (i + 1) * QB
        if first > 0 and last < length:
            first = 0
        out.append((i, first, last, (0, PAD + last) if first == 0 else (PAD + first, length + 2 * PAD)))
    return out


def strip_parts(block):
    _, first, last, (low, _) = block
    n = last - first
    return ((0, PAD), (PAD, PAD + n)) if low == 0 else ((n, n + PAD), (0, n))


def fill_prefix_mask(mask_ref, length, prefix_count):
    live = lax.broadcasted_iota(jnp.int32, (PAD, QB), 0) < prefix_count
    edge = jnp.where(live, 0.0, NEGATIVE)
    mask_ref[0:PAD, :] = edge
    mask_ref[PAD + length :, :] = edge


def fill_mask(mask_ref, seg_col, seg_row, block):
    i, first, last, _ = block
    keys = lax.broadcasted_iota(jnp.int32, (last - first, QB), 0) + first
    asks = lax.broadcasted_iota(jnp.int32, (last - first, QB), 1) + i * QB
    allowed = (seg_col[first:last] == seg_row[:, i * QB : last]) & (keys <= asks)
    mask_ref[PAD + first : PAD + last, :] = jnp.where(allowed, 0.0, NEGATIVE)


def fill_extended(ext_ref, prefix, values):
    length = values.shape[0]
    ext_ref[0:PAD, :] = prefix
    ext_ref[PAD : PAD + length, :] = values
    ext_ref[PAD + length :, :] = prefix


def head_lanes():
    return lax.broadcasted_iota(jnp.int32, (QB, WIDE), 1) // HD


def attend_scratch(length):
    return [
        pltpu.VMEM((length + 2 * PAD, QB), F32),
        pltpu.VMEM((length + 2 * PAD, WIDE), BF16),
        pltpu.VMEM((WIDE, length), BF16),
        pltpu.VMEM((2, length + PAD, QB), F32),
        pltpu.VMEM((GROUP, length), F32),
        pltpu.VMEM((GROUP, length), F32),
    ]


def attend_body(prefix_count, x_ref, w_ref, extra, segr_ref, q_ref, k_ref, v_ref, att_ref, lse_ref,
                mask_ref, ke_ref, vt_ref, s_ref, top_ref, sum_ref):
    length = x_ref.shape[0]
    pk, pv, bias = extra
    x = x_ref[...]
    q_ref[...] = ((dot(x, w_ref[0], NT) + bias[0:1]) * HD ** (-0.5)).astype(BF16)
    k = (dot(x, w_ref[1], NT) + bias[1:2]).astype(BF16)
    k_ref[...] = k
    fill_extended(ke_ref, pk, k)
    v = (dot(x, w_ref[2], NT) + bias[2:3]).astype(BF16)
    v_ref[...] = v
    vt_ref[...] = v.T
    pvt = pv.T
    seg_row = segr_ref[...]
    seg_col = column_of(seg_row)
    fill_prefix_mask(mask_ref, length, prefix_count)
    heads, zero = head_lanes(), jnp.zeros((), BF16)
    work = [(block, h) for block in blocks_of(length) for h in range(GROUP)]

    def ask(n):
        block, h = work[n]
        i, _, last, (low, high) = block
        if h == 0:
            fill_mask(mask_ref, seg_col, seg_row, block)
        asked = jnp.where(heads == h, q_ref[i * QB : last, :], zero)
        s_ref[n % 2, 0 : high - low, :] = dot(ke_ref[low:high, :], asked, NT) + mask_ref[low:high, :]

    ask(0)
    for n, (block, h) in enumerate(work):
        if n + 1 < len(work):
            ask(n + 1)
        i, first, last, (low, high) = block
        rows, span = slice(i * QB, last), slice(h * HD, (h + 1) * HD)
        (pa, pb), (ta, tb) = strip_parts(block)
        s = s_ref[n % 2, 0 : high - low, :]
        top = jnp.max(s, axis=0, keepdims=True)
        e = jnp.exp(s - top)
        total = jnp.sum(e, axis=0, keepdims=True)
        top_ref[h : h + 1, rows] = top
        sum_ref[h : h + 1, rows] = total
        e = e.astype(BF16)
        o = dot(vt_ref[span, first:last], e[ta:tb]) + dot(pvt[span, :], e[pa:pb])
        att_ref[span, rows] = (o * (1.0 / total)).astype(BF16)
    lse_ref[...] = top_ref[...] + jnp.log(sum_ref[...])


def attend_own_kernel(prefix_count, member_ref, tok_ref, gain_ref, shift_ref, w_ref, small_ref, segr_ref, bias_ref,
                      x_ref, q_ref, k_ref, v_ref, att_ref, lse_ref, out_ref, *scratch):
    length = tok_ref.shape[0]
    for t in range(0, length, TB):
        normed, _ = normalize(tok_ref[t : t + TB, :].astype(F32))
        x_ref[t : t + TB, :] = (normed * gain_ref[...] + shift_ref[...]).astype(BF16)
    attend_body(prefix_count, x_ref, w_ref, extras(member_ref[0], small_ref, False), segr_ref,
                q_ref, k_ref, v_ref, att_ref, lse_ref, *scratch)
    for t in range(0, length, TB):
        base = tok_ref[t : t + TB, :].astype(F32) + bias_ref[...]
        out_ref[t : t + TB, :] = base + dot(att_ref[:, t : t + TB], w_ref[3], TN)


def attend_others_kernel(prefix_count, carried, member_ref, x_ref, *refs):
    pieces, (small_ref, segr_ref, acc_ref) = refs[:8], refs[8:11]
    refs = refs[11 + carried :]
    w_ref, q_ref, k_ref, v_ref, att_ref, lse_ref, out_ref = refs[:7]
    half = HD // 2
    for j, ref in enumerate(pieces):
        for c in range(4):
            w_ref[c, j * half : (j + 1) * half, :] = ref[c * half : (c + 1) * half, :].astype(BF16)
    attend_body(prefix_count, x_ref, w_ref, extras(member_ref[0], small_ref, True), segr_ref,
                q_ref, k_ref, v_ref, att_ref, lse_ref, *refs[7:])

    @pl.when(pl.program_id(0) == 0)
    def _():
        out_ref[...] = acc_ref[...]

    for t in range(0, x_ref.shape[0], TB):
        out_ref[t : t + TB, :] += dot(att_ref[:, t : t + TB], w_ref[3], TN)


def attend_own(prefix_count, *args):
    length, width = args[1].shape
    return resident(
        functools.partial(attend_own_kernel, prefix_count),
        [shape_of((length, width), BF16)]
        + [shape_of((length, WIDE), BF16)] * 3
        + [shape_of((WIDE, length), BF16), shape_of((GROUP, length), F32), shape_of((length, width), F32)],
        attend_scratch(length),
        "attend_own",
        22,
        args,
    )


SCALARS = pl.BlockSpec(memory_space=pltpu.SMEM)


def once(values):
    return pl.BlockSpec(values.shape, lambda g: (0,) * len(values.shape), pipeline_mode=pl.Buffered(1))


def each(*block):
    return pl.BlockSpec((None,) + block, lambda g: (g,) + (0,) * len(block))


def rows_of(count, width):
    return pl.BlockSpec((count, width), lambda g: (g, 0))


def attend_others(prefix_count, first, count, total, member, x, pieces, small, seg, acc, carry=()):
    length, width = x.shape
    saved = [(4, WIDE, width), (length, WIDE), (length, WIDE), (length, WIDE), (WIDE, length), (GROUP, length)]
    piece = lambda at: pl.BlockSpec((128, width), lambda g: (g + at, 0))
    part = lambda block: pl.BlockSpec((None,) + block, lambda g: (g + first,) + (0,) * len(block))
    return pl.pallas_call(
        functools.partial(attend_others_kernel, prefix_count, len(carry)),
        grid=(count,),
        in_specs=[SCALARS, once(x)]
        + [piece(at) for _, at in pieces]
        + [pl.BlockSpec((48, WIDE), lambda g: (g + first, 0)), once(seg), once(acc)]
        + [pl.BlockSpec(memory_space=pl.ANY)] * len(carry),
        out_specs=[part(block) for block in saved] + [pl.BlockSpec((length, width), lambda g: (0, 0))],
        out_shape=[shape_of((total,) + block, BF16) for block in saved[:-1]]
        + [shape_of((total, GROUP, length), F32), shape_of((length, width), F32)],
        scratch_shapes=attend_scratch(length),
        input_output_aliases={13 + n: n for n in range(len(carry))},
        cost_estimate=BRIEF,
        compiler_params=params(50),
        name="attend_others",
    )(member, x, *[values for values, _ in pieces], small, seg, acc, *carry)


def back_scratch(length):
    low = lambda *shape: pltpu.VMEM(shape, BF16)
    return [
        pltpu.VMEM((length + 2 * PAD, QB), F32),
        low(length + 2 * PAD, WIDE),
        low(length + 2 * PAD, WIDE),
        low(WIDE, length),
        low(WIDE, length),
        low(WIDE, length),
        low(length, WIDE),
        pltpu.VMEM((2, length + PAD, QB), F32),
        pltpu.VMEM((2, length + PAD, QB), F32),
        pltpu.VMEM((GROUP, length), F32),
        pltpu.VMEM((2, WIDE, length), F32),
    ]


def back_body(prefix_count, extra, w_ref, q_ref, k_ref, v_ref, att_ref, lse_ref, segr_ref, low_ref, gjt_ref, gp_ref,
              mask_ref, ke_ref, ve_ref, kt_ref, qt_ref, dot_ref, do_ref, s_ref, dp_ref, delta_ref, acc_ref):
    length = q_ref.shape[0]
    pk, pv, _ = extra
    do = dot(low_ref[...], w_ref[3], NT).astype(BF16)
    do_ref[...] = do
    dot_ref[...] = do.T
    kt_ref[...] = k_ref[...].T
    qt_ref[...] = q_ref[...].T
    fill_extended(ke_ref, pk, k_ref[...])
    fill_extended(ve_ref, pv, v_ref[...])
    pkt = pk.T
    for h in range(GROUP):
        span = slice(h * HD, (h + 1) * HD)
        products = dot_ref[span, :].astype(F32) * att_ref[span, :].astype(F32)
        delta_ref[h : h + 1, :] = jnp.sum(products, axis=0, keepdims=True)
    seg_row = segr_ref[...]
    seg_col = column_of(seg_row)
    fill_prefix_mask(mask_ref, length, prefix_count)
    acc_ref[...] = jnp.zeros_like(acc_ref)
    if gp_ref is not None:
        gp_ref[...] = jnp.zeros_like(gp_ref)
    heads, zero = head_lanes(), jnp.zeros((), BF16)
    work = [(block, h) for block in blocks_of(length) for h in range(GROUP)]

    def ask(n):
        block, h = work[n]
        i, _, last, (low, high) = block
        if h == 0:
            fill_mask(mask_ref, seg_col, seg_row, block)
        rows = slice(i * QB, last)
        asked = jnp.where(heads == h, q_ref[rows, :], zero)
        grad = jnp.where(heads == h, do_ref[rows, :], zero)
        s_ref[n % 2, 0 : high - low, :] = dot(ke_ref[low:high, :], asked, NT) + mask_ref[low:high, :]
        dp_ref[n % 2, 0 : high - low, :] = dot(ve_ref[low:high, :], grad, NT)

    ask(0)
    for n, (block, h) in enumerate(work):
        if n + 1 < len(work):
            ask(n + 1)
        i, first, last, (low, high) = block
        rows, span = slice(i * QB, last), slice(h * HD, (h + 1) * HD)
        (pa, pb), (ta, tb) = strip_parts(block)
        p = jnp.exp(s_ref[n % 2, 0 : high - low, :] - lse_ref[h : h + 1, rows])
        ds = (p * (dp_ref[n % 2, 0 : high - low, :] - delta_ref[h : h + 1, rows])).astype(BF16)
        p = p.astype(BF16)
        dq = dot(kt_ref[span, first:last], ds[ta:tb]) + dot(pkt[span, :], ds[pa:pb])
        gjt_ref[span, rows] = dq.astype(BF16) * jnp.asarray(HD ** (-0.5), BF16)
        acc_ref[0, span, first:last] += dot(qt_ref[span, rows], ds[ta:tb], NT)
        acc_ref[1, span, first:last] += dot(dot_ref[span, rows], p[ta:tb], NT)
        if gp_ref is not None:
            gp_ref[0, span, :] += dot(qt_ref[span, rows], ds[pa:pb], NT)
            gp_ref[1, span, :] += dot(dot_ref[span, rows], p[pa:pb], NT)
    gjt_ref[WIDE : 2 * WIDE, :] = acc_ref[0].astype(BF16)
    gjt_ref[2 * WIDE : 3 * WIDE, :] = acc_ref[1].astype(BF16)


def take_own(out_ref, rows, values, index):
    width = out_ref.shape[1]
    for k in range(values.shape[1] // width):

        @pl.when(index == k)
        def _():
            out_ref[rows, :] = values[:, k * width : (k + 1) * width].astype(out_ref.dtype)


def norm_back(grad, normed, inverse, gain):
    scaled = grad * gain
    mean = jnp.mean(scaled, axis=-1, keepdims=True)
    return inverse * (scaled - mean - normed * jnp.mean(scaled * normed, axis=-1, keepdims=True))


def pack_sums(prefix_count, z, gp_ref, sums, gjt_ref, ups_ref, outer_ref, pack_ref):
    pack_ref[...] = jnp.zeros_like(pack_ref)
    inner = 0.0
    for k in range(2):
        gp = gp_ref[k].T
        pack_ref[k * PAD : (k + 1) * PAD, :] = gp
        for _ in range(3):
            part = gp.astype(BF16)
            inner = inner + dot(part, outer_ref[:, k * WIDE : (k + 1) * WIDE], NT)
            gp = gp - part.astype(F32)
    for n in range(4):
        take_own(pack_ref, slice(2 * PAD + n, 2 * PAD + n + 1), sums[n], z)
    joint = dot(jnp.ones((8, gjt_ref.shape[1]), BF16), gjt_ref[...], NT)
    for k in range(3):
        pack_ref[2 * PAD + 4 + k : 2 * PAD + 5 + k, :] = joint[0:1, k * WIDE : (k + 1) * WIDE]
    for k in range(ups_ref.shape[1] // WIDE):
        pack_ref[2 * PAD + 8 + k : 2 * PAD + 9 + k, :] = ups_ref[:, k * WIDE : (k + 1) * WIDE]
    begin = 2 * PAD + 8 + ups_ref.shape[1] // WIDE
    for k in range(inner.shape[1] // WIDE):
        to = slice(begin + k * prefix_count, begin + (k + 1) * prefix_count)
        pack_ref[to, :] = inner[0:prefix_count, k * WIDE : (k + 1) * WIDE]


def back_own_kernel(prefix_count, places_ref, res_ref, cot_ref, gm_ref, gain_ref, w_ref, q_ref, k_ref, v_ref, att_ref,
                    lse_ref, small_ref, segr_ref, ups_ref, outer_ref, low_ref, part_ref, gjt_ref, pack_ref, ga_ref, gp_ref,
                    *scratch):
    length = res_ref.shape[0]
    sums = [0.0] * 4
    for t in range(0, length, TB):
        rows = slice(t, t + TB)
        normed, inverse = normalize(res_ref[rows, :])
        gm, cot = gm_ref[rows, :], cot_ref[rows, :].astype(F32)
        grad = cot + norm_back(gm, normed, inverse, gain_ref[...])
        low_ref[rows, :] = grad.astype(BF16)
        take_own(part_ref, rows, grad, places_ref[0])
        for n, values in enumerate((gm * normed, gm, grad, cot)):
            sums[n] = sums[n] + jnp.sum(values, axis=0, keepdims=True)
    back_body(prefix_count, extras(places_ref[1], small_ref, False), w_ref, q_ref, k_ref, v_ref, att_ref, lse_ref,
              segr_ref, low_ref, gjt_ref, gp_ref, *scratch)
    w = w_ref[0:3].reshape(3 * WIDE, w_ref.shape[2])
    for t in range(0, length, TB):
        ga_ref[t : t + TB, :] = dot(gjt_ref[:, t : t + TB], w, TN)
    pack_sums(prefix_count, places_ref[0], gp_ref, sums, gjt_ref, ups_ref, outer_ref, pack_ref)


def back_others_kernel(prefix_count, places_ref, w_ref, q_ref, k_ref, v_ref, att_ref, lse_ref, small_ref, segr_ref,
                       low_ref, gain_ref, from_ga, from_tok, from_part, out_ref, sums_ref, ga_ref, tok_ref, part_ref, sems, gjt_ref,
                       *scratch):
    length, step = low_ref.shape[0], pl.program_id(0)
    final = pl.num_programs(0) - 1
    pairs = ((from_ga, ga_ref), (from_tok, tok_ref), (from_part, part_ref))
    copies = [pltpu.make_async_copy(source, target, sems.at[n]) for n, (source, target) in enumerate(pairs)]

    @pl.when(step == 0)
    def _():
        for copy in copies:
            copy.start()

    back_body(prefix_count, extras(places_ref[1], small_ref, True), w_ref, q_ref, k_ref, v_ref, att_ref, lse_ref,
              segr_ref, low_ref, gjt_ref, None, *scratch)
    w = w_ref[0:3].reshape(3 * WIDE, w_ref.shape[2])

    @pl.when(step == 0)
    def _():
        for copy in copies:
            copy.wait()

    @pl.when(step < final)
    def _():
        for t in range(0, length, TB):
            ga_ref[t : t + TB, :] += dot(gjt_ref[:, t : t + TB], w, TN)

    @pl.when(step == final)
    def _():
        sums = [0.0, 0.0]
        for t in range(0, length, TB):
            rows = slice(t, t + TB)
            ga = ga_ref[rows, :] + dot(gjt_ref[:, rows], w, TN)
            normed, inverse = normalize(tok_ref[rows, :].astype(F32))
            grad = norm_back(ga, normed, inverse, gain_ref[...])
            width = out_ref.shape[1]
            for k in range(grad.shape[1] // width):

                @pl.when(places_ref[0] == k)
                def _():
                    out_ref[rows, :] = (part_ref[rows, :] + grad[:, k * width : (k + 1) * width]).astype(BF16)

            sums[0] = sums[0] + jnp.sum(ga * normed, axis=0, keepdims=True)
            sums[1] = sums[1] + jnp.sum(ga, axis=0, keepdims=True)
        sums_ref[...] = jnp.zeros_like(sums_ref)
        for n in range(2):
            take_own(sums_ref, slice(n, n + 1), sums[n], places_ref[0])


def back_own(prefix_count, *args):
    length, width = args[1].shape
    ups, outer = args[-2:]
    packed = 2 * PAD + 8 + ups.shape[1] // WIDE + outer.shape[0] // WIDE * prefix_count
    return resident(
        functools.partial(back_own_kernel, prefix_count),
        [
            shape_of((length, width), BF16),
            shape_of((length, WIDE), F32),
            shape_of((3 * WIDE, length), BF16),
            shape_of((-(-packed // 8) * 8, WIDE), F32),
            shape_of((length, width), F32),
        ],
        [pltpu.VMEM((2, WIDE, PAD), F32)] + back_scratch(length),
        "back_own",
        30,
        args,
    )


def back_others(prefix_count, places, saved, small, seg, low, ga, tokens, part, gain):
    length, width = low.shape
    return pl.pallas_call(
        functools.partial(back_others_kernel, prefix_count),
        grid=(saved[0].shape[0],),
        in_specs=[SCALARS]
        + [each(*values.shape[1:]) for values in saved]
        + [rows_of(48, WIDE)]
        + [once(values) for values in (seg, low, gain)]
        + [pl.BlockSpec(memory_space=pl.ANY)] * 3,
        out_specs=[pl.BlockSpec((length, WIDE), lambda g: (0, 0)), pl.BlockSpec((8, WIDE), lambda g: (0, 0))],
        out_shape=[shape_of((length, WIDE), BF16), shape_of((8, WIDE), F32)],
        scratch_shapes=[
            pltpu.VMEM((length, width), F32),
            pltpu.VMEM((length, width), BF16),
            pltpu.VMEM((length, WIDE), F32),
            pltpu.SemaphoreType.DMA((3,)),
            pltpu.VMEM((3 * WIDE, length), BF16),
        ]
        + back_scratch(length),
        cost_estimate=BRIEF,
        compiler_params=params(50),
        name="back_others",
    )(places, *saved, small, seg, low, gain, ga, tokens, part)


def gelu_pair(v):
    c = 0.7978845608028654
    square = v * v
    t = jnp.tanh(v * (c + (0.044715 * c) * square))
    half = 0.5 + 0.5 * t
    return v * half, half + (0.5 * v) * (1.0 - t * t) * (c + (3.0 * 0.044715 * c) * square)


def mix_rows(mid, cot, up_ref, up_dims, bias, down_ref, act_ref, gp_ref, rows, pre_ref, g_ref):
    hidden = down_ref.shape[0]
    chunks = [slice(c, c + TB) for c in range(0, hidden, TB)]

    def ask(n):
        up = up_ref[:, chunks[n]] if up_dims is NN else up_ref[chunks[n], :]
        pre_ref[n % 2] = dot(mid, up, up_dims) + bias[:, chunks[n]]
        g_ref[n % 2] = dot(cot, down_ref[chunks[n], :], NT)

    ask(0)
    for n, chunk in enumerate(chunks):
        if n + 1 < len(chunks):
            ask(n + 1)
        act, slope = gelu_pair(pre_ref[n % 2])
        act_ref[rows, chunk] = act.astype(BF16)
        gp_ref[rows, chunk] = (g_ref[n % 2] * slope).astype(BF16)


def mix_own_kernel(z_ref, res_ref, cot_ref, gain_ref, shift_ref, up_ref, bias_ref, down_ref, dbias_ref,
                   mid_ref, act_ref, gp_ref, share_ref, bsum_ref, gm_ref, pre_ref, g_ref):
    width = share_ref.shape[1]
    own = pl.ds(pl.multiple_of(z_ref[0] * width, width), width)
    every = slice(0, TB)
    normed, _ = normalize(res_ref[...])
    mid = (normed * gain_ref[...] + shift_ref[...]).astype(BF16)
    mid_ref[...] = mid
    mix_rows(mid, cot_ref[...], up_ref, NN, bias_ref[...], down_ref, act_ref, gp_ref, every, pre_ref, g_ref)
    share_ref[...] = res_ref[:, own] + dbias_ref[:, own] + dot(act_ref[...], down_ref[:, own])
    gp = gp_ref[...]
    gm_ref[...] = dot(gp, up_ref[...], NT)

    @pl.when(pl.program_id(0) == 0)
    def _():
        bsum_ref[...] = jnp.zeros_like(bsum_ref)

    bsum_ref[...] += jnp.sum(gp.astype(F32), axis=0, keepdims=True)


def mix_own(own_width, z, residual, cotangent, gain, shift, up, up_bias, down, down_bias):
    length, width = residual.shape
    hidden = up.shape[1]
    rows = lambda w: rows_of(TB, w)
    fixed = [once(values) for values in (gain, shift, up, up_bias, down, down_bias)]
    return pl.pallas_call(
        mix_own_kernel,
        grid=(length // TB,),
        in_specs=[SCALARS, rows(width), rows(width)] + fixed,
        out_specs=[rows(width), rows(hidden), rows(hidden), rows(own_width), pl.BlockSpec((1, hidden), lambda t: (0, 0)), rows(width)],
        out_shape=[
            shape_of((length, width), BF16),
            shape_of((length, hidden), BF16),
            shape_of((length, hidden), BF16),
            shape_of((length, own_width), F32),
            shape_of((1, hidden), F32),
            shape_of((length, width), F32),
        ],
        scratch_shapes=[pltpu.VMEM((2, TB, TB), F32)] * 2,
        cost_estimate=BRIEF,
        compiler_params=params(36),
        name="mix_own",
    )(z, residual, cotangent, gain, shift, up, up_bias, down, down_bias)


def mix_kernel(places, z_ref, mid_ref, cot_ref, small_ref, share_in, gm_in, *refs):
    pieces, per = len(places), 128
    share_ref, gm_ref, up_ref, down_ref, part_ref, act_ref, gp_ref, pre_ref, g_ref = refs[2 * pieces :]
    width = share_ref.shape[1]
    own = pl.ds(pl.multiple_of(z_ref[0] * width, width), width)

    @pl.when(pl.program_id(0) == 0)
    def _():
        for j in range(pieces):
            up_ref[j * per : (j + 1) * per, :] = refs[2 * j][...].astype(BF16)
            down_ref[j * per : (j + 1) * per, :] = refs[2 * j + 1][...].astype(BF16)
        part_ref[...] = down_ref[:, own]

    biases = {k: reorder(small_ref[48 * k + 40 : 48 * k + 48, 0:per], z_ref[1], 0) for k, _ in places}
    bias = jnp.concatenate([biases[k][j : j + 1] for k, j in places], axis=1)
    every = slice(0, TB)
    mix_rows(mid_ref[...], cot_ref[...], up_ref, NT, bias, down_ref, act_ref, gp_ref, every, pre_ref, g_ref)
    share_ref[...] = (share_in[...] + dot(act_ref[...], part_ref[...])).astype(share_ref.dtype)
    gm_ref[...] = gm_in[...] + dot(gp_ref[...], up_ref[...])


def mix(places, blocks, last, z, mid, cotangent, small, share, gm, *arrays):
    length, width = mid.shape
    hidden = 128 * len(places)
    own_width = share.shape[1]
    rows = lambda w: rows_of(TB, w)
    low = lambda *shape: pltpu.VMEM(shape, BF16)
    piece = lambda at: pl.BlockSpec((128, width), lambda t: (at, 0), pipeline_mode=pl.Buffered(1))
    return pl.pallas_call(
        functools.partial(mix_kernel, places),
        grid=(length // TB,),
        in_specs=[SCALARS, rows(width), rows(width), once(small), rows(own_width), rows(width)]
        + [piece(at) for at in blocks],
        out_specs=[rows(own_width), rows(width)],
        out_shape=[shape_of((length, own_width), BF16 if last else F32), shape_of((length, width), F32)],
        scratch_shapes=[low(hidden, width), low(hidden, width), low(hidden, own_width), low(TB, hidden), low(TB, hidden)]
        + [pltpu.VMEM((2, TB, TB), F32)] * 2,
        input_output_aliases={5: 1} if last else {4: 0, 5: 1},
        cost_estimate=BRIEF,
        compiler_params=params(40),
        name="mix_others",
    )(z, mid, cotangent, small, share, gm, *arrays)


def hidden_grad_kernel(mid_ref, cot_ref, gp_ref, act_ref, out_ref):
    parts, per = out_ref.shape[0], out_ref.shape[1] // 2
    for at, left, right in ((0, mid_ref, gp_ref), (per, cot_ref, act_ref)):
        grad = dot(left[...], right[...], TN)
        for a in range(parts):
            out_ref[a, at : at + per, :] = grad[a * per : (a + 1) * per]


def hidden_grad(parts, mid, cotangent, gp, act):
    length, width = mid.shape
    hidden = gp.shape[1]
    per = width // parts
    column = pl.BlockSpec((length, TB), lambda j: (0, j))
    return pl.pallas_call(
        hidden_grad_kernel,
        grid=(width // TB,),
        in_specs=[column, column, once(gp), once(act)],
        out_specs=pl.BlockSpec((TB // per, 2 * per, hidden), lambda j: (j, 0, 0)),
        out_shape=shape_of((parts, 2 * per, hidden), F32),
        cost_estimate=BRIEF,
        compiler_params=params(30),
        name="hidden_grad",
    )(mid, cotangent, gp, act)


def head_grad_kernel(z_ref, x_ref, low_ref, gjt_ref, att_ref, out_ref):
    wide = gjt_ref.shape[0]
    for start, left, right in ((0, gjt_ref, x_ref), (wide, att_ref, low_ref)):
        for r in range(0, left.shape[0], TB):
            grad = dot(left[r : r + TB, :], right[...])
            for j in range(out_ref.shape[0]):
                out_ref[j, start + r : start + r + TB, :] = grad[:, 128 * j : 128 * (j + 1)]


def head_grad(*args):
    width = args[1].shape[1]
    rows = args[3].shape[0] + args[4].shape[0]
    return resident(
        head_grad_kernel, [shape_of((width // 128, rows, 128), F32)], [], "head_grad", 16, args
    )


def shards(
    tokens, segment_ids, attention_gain, attention_shift, joint_weight, joint_bias, output_weight, output_bias,
    mixer_gain, mixer_shift, up_weight, up_bias, down_weight, down_bias, prefix_table, inner_weight, inner_bias,
    outer_weight, outer_bias, cotangent,
):
    length, width = tokens.shape
    local = joint_weight.shape[2]
    hidden = up_weight.shape[1]
    prefix_count = prefix_table.shape[0]
    batch_size, tensor_size = lax.axis_size("batch"), lax.axis_size("tensor")
    z = lax.axis_index("tensor").astype(jnp.int32)
    member = (lax.axis_index("batch") % 8).astype(jnp.int32)
    member_arr, places = member.reshape(1), jnp.stack([z, member])

    def own_columns(values):
        return lax.dynamic_slice_in_dim(values, z * local, local, values.ndim - 1)

    def along(values, k):
        return lax.ppermute(values, "tensor", [(i, i ^ k) for i in range(tensor_size)])

    def across(values, k):
        return lax.ppermute(values, "batch", [(i, i ^ k) for i in range(batch_size)])

    now = [member_arr]

    def after(values):
        return lax.optimization_barrier((values, *now))[0]

    def wait(*values):
        held = lax.optimization_barrier((*values, *now))
        now[:] = [held[0]]
        return held[0] if len(values) == 1 else held[: len(values)]

    def run(call, *args):
        outs = call(after(args[0]), *args[1:])
        now[:] = [outs[-1] if isinstance(outs, (list, tuple)) else outs]
        return outs

    row = lambda v: v.reshape(1, -1)
    stack = lambda *parts: jnp.concatenate(parts, axis=0)

    def gather(*parts):
        places = [(start, rows) for _, start, rows in parts]
        arrays = [values for values, _, _ in parts]
        return run(lambda *arrays: gather_rows(places, *arrays), *arrays)

    def rows(values, block, count=1):
        return values, block * 128, count * 128

    whole = lambda values: (values, 0, values.shape[0])

    own_heads, send_heads = run(head_pieces, member_arr, joint_weight, output_weight)
    a1, a2 = along(after(send_heads[0]), 1), along(after(send_heads[0]), 2)

    def prefixes(prefix_table, inner_weight):
        hidden_prefix = jnp.tanh(jnp.dot(prefix_table, inner_weight.astype(F32), precision=PRECISE) + inner_bias)
        pairs = jnp.einsum("pr,rke->kpe", hidden_prefix, outer_weight.astype(F32), precision=PRECISE)
        pairs = jnp.pad(pairs + outer_bias[:, None, :], ((0, 0), (0, PAD - prefix_count), (0, 0)))
        ups = jnp.pad(up_bias.reshape(8, hidden // 8), ((0, 0), (0, local - hidden // 8)))
        joints = jnp.pad(joint_bias, ((0, 5), (0, 0)))
        return hidden_prefix, stack(pairs.reshape(2 * PAD, local), joints, ups)

    hidden_prefix, small = run(prefixes, prefix_table, inner_weight)
    send_hidden = run(hidden_pieces, member_arr, up_weight, down_weight)
    smalls = [along(after(small), k) for k in (1, 2, 3)]
    a1, a2, *smalls = wait(a1, a2, *smalls)
    a12 = gather(whole(a1), whole(a2))
    x12, y12 = across(after(a12), 2), across(after(a12), 4)
    a3, a1d = along(after(send_heads[0]), 3), along(after(send_heads[1]), 1)
    c12 = across(after(a12), 1)
    x, *saved_own, residual = run(
        functools.partial(attend_own, prefix_count),
        member_arr, tokens, row(attention_gain), row(attention_shift), own_heads, small, segment_ids, row(output_bias),
    )
    extra = stack(*smalls)
    x12, y12, a3, a1d, c12 = wait(x12, y12, a3, a1d, c12)

    y3 = gather(whole(a3), rows(x12, 1))
    x3, y3 = across(after(a3), 2), across(after(y3), 4)
    f1, f2 = along(after(send_hidden[0]), 1), along(after(send_hidden[0]), 2)
    gb = gather(whole(x12), whole(y12), whole(a3), whole(a1d))
    cb = across(after(gb), 1)
    x3, y3, cb = wait(x3, y3, cb)
    a2d = run(lambda values: values[128:256], y3)
    ca2d = across(after(a2d), 1)
    a3d = across(after(y3[0:128]), 2)
    d12 = gather(whole(a1d), whole(a2d))
    ca2d = wait(ca2d)
    cd12 = gather(rows(cb, 5), whole(ca2d))
    *saved_others, residual = run(
        functools.partial(attend_others, prefix_count, 0, 2, 3),
        member_arr, x, [(a12, 0), (c12, 0), (x12, 0), (cb, 0), (y12, 0), (cb, 2), (d12, 0), (cd12, 0)], extra,
        segment_ids, residual,
    )
    a3d, f1, f2 = wait(a3d, f1, f2)

    f12 = gather(whole(f1), whole(f2))
    gc = gather(whole(x3), rows(y3, 0), whole(a3d), whole(f1), whole(f2))
    fx, fy = across(after(f12), 2), across(after(f12), 4)
    f3, f1d = along(after(send_hidden[0]), 3), along(after(send_hidden[1]), 1)
    cc = wait(across(after(gc), 1))
    *saved_others, residual = run(
        functools.partial(attend_others, prefix_count, 2, 1, 3),
        member_arr, x, [(a3, 0), (cb, 4), (x3, 0), (cc, 0), (y3, 0), (cc, 1), (a3d, 0), (cc, 2)], extra,
        segment_ids, residual, saved_others,
    )
    mid, act, gp, share, up_bias_sum, gm = run(
        functools.partial(mix_own, local),
        places, residual, cotangent, row(mixer_gain), row(mixer_shift), up_weight, row(up_bias), down_weight,
        row(down_bias),
    )
    hidden_part = run(functools.partial(hidden_grad, batch_size), mid, cotangent, gp, act)
    fx, fy, f3, f1d = wait(fx, fy, f3, f1d)

    x4 = gather(whole(f3), rows(fy, 3))
    y4 = gather(whole(f3), rows(fx, 2))
    x4, y4 = across(after(x4), 2), across(after(y4), 4)
    cfx, cfy, cf1d = [across(after(values), 1) for values in (fx, fy, f1d)]
    cfx, cfy, cf1d = wait(cfx, cfy, cf1d)

    def mix_more(pieces, share, gm, last=False):
        order = [(slot, j) for slot, j, _, _ in pieces]
        flat = [part for _, _, up, down in pieces for part in (up, down)]
        return run(
            functools.partial(mix, order, [at for _, at in flat], last),
            places, mid, cotangent, extra, share, gm, *[values for values, _ in flat],
        )

    def pair(values, at):
        return (values, at), (values, at + 1)

    def both(slot, number, mine, theirs):
        return [(slot, number, *pair(*mine)), (slot, number + 1, *pair(*theirs))]

    pieces = both(0, 0, (f12, 0), (cc, 3)) + both(0, 2, (fx, 0), (cfx, 0))
    share, gm = mix_more(pieces + both(0, 4, (fy, 0), (cfy, 0)) + both(0, 6, (f1d, 0), (cf1d, 0)), share, gm)
    pieces = both(1, 0, (f12, 2), (cc, 5)) + both(1, 2, (fx, 2), (cfx, 2))
    share, gm = mix_more(pieces + both(1, 4, (fy, 2), (cfy, 2)), share, gm)
    x4, y4 = wait(x4, y4)

    hidden_sum = lax.psum_scatter(after(hidden_part), "batch", scatter_dimension=0, tiled=False)
    x5, y5 = across(after(y4[128:256]), 2), across(after(x4[0:128]), 4)
    cx4, cy4, cf3 = wait(*[across(after(values), 1) for values in (x4, y4, f3)])
    pieces = [(1, 6, (y4, 2), (x4, 2)), (1, 7, (cy4, 2), (cx4, 2))] + both(2, 0, (f3, 0), (cf3, 0))
    share, gm = mix_more(pieces + both(2, 2, (x4, 0), (cx4, 0)) + both(2, 4, (y4, 0), (cy4, 0)), share, gm)
    x5, y5 = wait(x5, y5)

    cx5, cy5 = wait(across(after(x5), 1), across(after(y5), 1))
    share, gm = mix_more([(2, 6, (y5, 0), (x5, 0)), (2, 7, (cy5, 0), (cx5, 0))], share, gm, True)
    low, part, gjt, totals, ga = run(
        functools.partial(back_own, prefix_count),
        places, residual, cotangent, gm, row(mixer_gain), own_heads, *saved_own, small, segment_ids, up_bias_sum,
        outer_weight.reshape(outer_weight.shape[0], -1),
    )

    def spread(values, send, bits):
        if len(bits) == 1:
            return (send(after(values), bits[0]),)
        return tuple(send(after(values), k) for k in (bits[0], bits[1], bits[0] + bits[1]))

    def gather_sum(values, others):
        others = wait(*others) if len(others) > 1 else (wait(*others),)
        total = values + others[0]
        return total + (others[1] + others[2]) if len(others) == 3 else total

    def rounds_of(send, size):
        bits = [1 << b for b in range((size - 1).bit_length())]
        return [(send, bits[k : k + 2]) for k in range(0, len(bits), 2)]

    over_batch, over_tensor = rounds_of(across, batch_size), rounds_of(along, tensor_size)
    others = spread(totals, *over_batch[0])
    (head_part,) = run(head_grad, places, x, low, gjt, saved_own[3])
    per = width // batch_size
    head_part = head_part.reshape(-1, 4 * local, 128 // per, per).transpose(0, 2, 1, 3)
    totals = gather_sum(totals, others)
    for send, bits in over_batch[1:]:
        totals = gather_sum(totals, spread(totals, send, bits))
    batch_totals = totals
    others = spread(totals, *over_tensor[0])
    hidden_sum = wait(hidden_sum)
    head_sum = lax.psum_scatter(
        after(head_part.reshape(batch_size, 4 * local, per)), "batch", scatter_dimension=0, tiled=False
    )
    tokens_gradient, gain_sums = run(
        functools.partial(back_others, prefix_count),
        places, saved_others, extra, segment_ids, low, ga, tokens, part, row(attention_gain),
    )
    totals = gather_sum(totals, others)
    for send, bits in over_tensor[1:]:
        totals = gather_sum(totals, spread(totals, send, bits))
    for send, bits in over_batch:
        gain_sums = gather_sum(gain_sums, spread(gain_sums, send, bits))
    split = 2 * PAD + 8 + hidden // local
    halves = outer_weight.shape[0] // local
    inner = totals[split : split + halves * prefix_count].reshape(halves, prefix_count, local)

    grad_prefix = batch_totals[: 2 * PAD].reshape(2, PAD, local)[:, :prefix_count]
    mixed_total = batch_totals[2 * PAD : 2 * PAD + 4]
    joint_bias_total = batch_totals[2 * PAD + 4 : 2 * PAD + 7]
    up_bias_total = batch_totals[2 * PAD + 8 : split]
    grad_hidden_prefix = inner.transpose(1, 0, 2).reshape(prefix_count, -1)
    outer_rows = outer_weight.shape[0] // batch_size
    hidden_own = lax.dynamic_slice_in_dim(hidden_prefix, lax.axis_index("batch") * outer_rows, outer_rows, 1)
    outer_total = jnp.einsum("pr,kpe->rke", hidden_own, grad_prefix, precision=PRECISE)
    outer_bias_total = jnp.sum(grad_prefix, axis=1)
    grad_inner = grad_hidden_prefix * (1.0 - hidden_prefix * hidden_prefix)
    inner_total = jnp.einsum("pd,pr->dr", prefix_table, grad_inner, precision=PRECISE)
    inner_bias_total = jnp.sum(grad_inner, axis=0)
    table_total = jnp.einsum("pr,dr->pd", grad_inner, inner_weight.astype(F32), precision=PRECISE)

    up_total, down_total = hidden_sum[:per], hidden_sum[per:].T
    joint_total = head_sum[: 3 * local].reshape(3, local, per).transpose(0, 2, 1)
    output_total = head_sum[3 * local :]
    return (
        share,
        tokens_gradient,
        gain_sums[0],
        gain_sums[1],
        joint_total,
        joint_bias_total,
        output_total,
        mixed_total[2],
        mixed_total[0],
        mixed_total[1],
        up_total,
        up_bias_total.reshape(hidden),
        down_total,
        mixed_total[3],
        table_total,
        inner_total,
        inner_bias_total,
        outer_total,
        outer_bias_total,
    )


def solution(mesh):
    placed = (
        P("batch", None),
        P("batch", None),
        P(),
        P(),
        P(None, None, "tensor"),
        P(None, "tensor"),
        P("tensor", None),
        P(),
        P(),
        P(),
        P(None, "tensor"),
        P("tensor"),
        P("tensor", None),
        P(),
        P(),
        P(),
        P(),
        P(None, None, "tensor"),
        P(None, "tensor"),
        P("batch", None),
    )
    return jax.shard_map(
        shards,
        mesh=mesh,
        in_specs=placed,
        out_specs=(
            P("batch", "tensor"),
            P("batch", "tensor"),
            P("tensor"),
            P("tensor"),
            P(None, "batch", "tensor"),
            P(None, "tensor"),
            P("tensor", "batch"),
            P("tensor"),
            P("tensor"),
            P("tensor"),
            P("batch", "tensor"),
            P("tensor"),
            P("tensor", "batch"),
            P("tensor"),
            P(),
            P(),
            P(),
            P("batch", None, "tensor"),
            P(None, "tensor"),
        ),
        check_vma=False,
    )
```

```python
import functools

import jax
import jax.numpy as jnp
from jax import lax
from jax.experimental import pallas as pl
from jax.experimental.pallas import tpu as pltpu
from jax.sharding import PartitionSpec as P

HD = 64
GROUP = 4
WIDE = GROUP * HD
QB = 256
CUT = 64
PAD = 16
TB = 256
EPSILON = 1e-05
PRECISE = lax.Precision.HIGHEST
NEGATIVE = -1e30
F32, BF16 = jnp.float32, jnp.bfloat16
NN = (((1,), (0,)), ((), ()))
NT = (((1,), (1,)), ((), ()))
TN = (((0,), (0,)), ((), ()))
shape_of = jax.ShapeDtypeStruct
BRIEF = pl.CostEstimate(flops=1024, bytes_accessed=1024, transcendentals=0)


def dot(a, b, dims=NN):
    return lax.dot_general(a, b, dims, preferred_element_type=F32)


def params(mib):
    return pltpu.CompilerParams(vmem_limit_bytes=mib * 2**20)


def resident(kernel, outs, scratch, name, mib, args, aliases={}):
    vm = pl.BlockSpec(memory_space=pltpu.VMEM)
    return pl.pallas_call(
        kernel,
        out_shape=outs,
        in_specs=[pl.BlockSpec(memory_space=pltpu.SMEM)] + [vm] * (len(args) - 1),
        out_specs=[vm] * len(outs),
        scratch_shapes=scratch,
        input_output_aliases=aliases,
        cost_estimate=BRIEF,
        compiler_params=params(mib),
        name=name,
    )(*args)


def normalize(values):
    centered = values - jnp.mean(values, axis=-1, keepdims=True)
    inverse = lax.rsqrt(jnp.mean(centered * centered, axis=-1, keepdims=True) + EPSILON)
    return centered * inverse, inverse


def heads_kernel(turn, member_ref, joint_ref, out_ref, own_ref, send_ref):
    for c in range(3):
        own_ref[c] = joint_ref[c].T
    own_ref[3] = out_ref[...]
    rows = own_ref.shape[1] // 8
    for p in range(2):
        member = member_ref[0] ^ (turn * p)
        start = pl.multiple_of(member * rows, rows)
        for c in range(4):
            send_ref[p, c * rows : (c + 1) * rows, :] = own_ref[c, pl.ds(start, rows), :].astype(F32)


def head_pieces(member, joint_weight, output_weight):
    _, width, local = joint_weight.shape
    vm = pl.BlockSpec(memory_space=pltpu.VMEM)
    return pl.pallas_call(
        functools.partial(heads_kernel, 6),
        out_shape=[shape_of((4, local, width), BF16), shape_of((2, local // 2, width), F32)],
        in_specs=[pl.BlockSpec(memory_space=pltpu.SMEM), vm, vm],
        out_specs=[vm, vm],
        cost_estimate=BRIEF,
        compiler_params=params(12),
        name="head_pieces",
    )(member, joint_weight, output_weight)


def hidden_kernel(member_ref, up_ref, down_ref, send_ref):
    rows = down_ref.shape[0]
    send_ref[0, 0:rows, :] = up_ref[...].T.astype(F32)
    send_ref[0, rows : 2 * rows, :] = down_ref[...].astype(F32)


def hidden_pieces(member, up_weight, down_weight):
    width, local = up_weight.shape
    rows = local // 8
    return pl.pallas_call(
        hidden_kernel,
        out_shape=shape_of((2, 2 * rows, width), F32),
        grid_spec=pltpu.PrefetchScalarGridSpec(
            num_scalar_prefetch=1,
            grid=(2,),
            in_specs=[
                pl.BlockSpec((width, rows), lambda p, m: (0, m[0] ^ (6 * p))),
                pl.BlockSpec((rows, width), lambda p, m: (m[0] ^ (6 * p), 0)),
            ],
            out_specs=pl.BlockSpec((1, 2 * rows, width), lambda p, m: (p, 0, 0)),
        ),
        cost_estimate=BRIEF,
        compiler_params=params(12),
        name="hidden_pieces",
    )(member, up_weight, down_weight)


def gather_kernel(places, *refs):
    sources, out_ref, sems = refs[: len(places)], refs[len(places)], refs[-1]
    copies, to = [], 0
    for (start, rows), ref in zip(places, sources):
        for at in range(0, rows, CUT):
            source, target = ref.at[pl.ds(start + at, CUT)], out_ref.at[pl.ds(to + at, CUT)]
            copies.append(pltpu.make_async_copy(source, target, sems.at[len(copies)]))
        to += rows
    for copy in copies:
        copy.start()
    for copy in copies:
        copy.wait()


def gather_rows(places, *arrays):
    anywhere = pl.BlockSpec(memory_space=pl.ANY)
    return pl.pallas_call(
        functools.partial(gather_kernel, places),
        in_specs=[anywhere] * len(arrays),
        out_specs=pl.BlockSpec(memory_space=pltpu.VMEM),
        out_shape=shape_of((sum(rows for _, rows in places), arrays[0].shape[1]), F32),
        scratch_shapes=[pltpu.SemaphoreType.DMA((sum(rows for _, rows in places) // CUT,))],
        cost_estimate=BRIEF,
        compiler_params=params(8),
        name="gather_rows",
    )(*arrays)


def reorder(values, member, dim=1):
    block = values.shape[dim] // 8
    place = lax.broadcasted_iota(jnp.int32, values.shape, dim) // block
    for bit in (1, 2, 4):
        up = pltpu.roll(values, block * bit, dim)
        down = pltpu.roll(values, values.shape[dim] - block * bit, dim)
        turned = jnp.where((place & bit) != 0, up, down)
        values = jnp.where((member & bit) != 0, turned, values)
    return values


def column_of(seg_row):
    wide = jnp.broadcast_to(seg_row.astype(F32), (128, seg_row.shape[1]))
    return wide.T[:, 0:1].astype(jnp.int32)


def extras(member, small_ref, others):
    small = small_ref[0:40, :]
    if others:
        small = reorder(small, member)
    return small[0:PAD].astype(BF16), small[PAD : 2 * PAD].astype(BF16), small[2 * PAD : 2 * PAD + 8]


def blocks_of(length):
    out = []
    for i in range(length // QB):
        first = max(0, (i * QB - length // 2 + 1) // QB) * QB
        last = (i + 1) * QB
        if first > 0 and last < length:
            first = 0
        out.append((i, first, last, (0, PAD + last) if first == 0 else (PAD + first, length + 2 * PAD)))
    return out


def strip_parts(block):
    _, first, last, (low, _) = block
    n = last - first
    return ((0, PAD), (PAD, PAD + n)) if low == 0 else ((n, n + PAD), (0, n))


def fill_prefix_mask(mask_ref, length, prefix_count):
    live = lax.broadcasted_iota(jnp.int32, (PAD, QB), 0) < prefix_count
    edge = jnp.where(live, 0.0, NEGATIVE)
    mask_ref[0:PAD, :] = edge
    mask_ref[PAD + length :, :] = edge


def fill_mask(mask_ref, seg_col, seg_row, block):
    i, first, last, _ = block
    keys = lax.broadcasted_iota(jnp.int32, (last - first, QB), 0) + first
    asks = lax.broadcasted_iota(jnp.int32, (last - first, QB), 1) + i * QB
    allowed = (seg_col[first:last] == seg_row[:, i * QB : last]) & (keys <= asks)
    mask_ref[PAD + first : PAD + last, :] = jnp.where(allowed, 0.0, NEGATIVE)


def fill_extended(ext_ref, prefix, values):
    length = values.shape[0]
    ext_ref[0:PAD, :] = prefix
    ext_ref[PAD : PAD + length, :] = values
    ext_ref[PAD + length :, :] = prefix


def head_lanes():
    return lax.broadcasted_iota(jnp.int32, (QB, WIDE), 1) // HD


def attend_scratch(length):
    return [
        pltpu.VMEM((length + 2 * PAD, QB), F32),
        pltpu.VMEM((length + 2 * PAD, WIDE), BF16),
        pltpu.VMEM((WIDE, length), BF16),
        pltpu.VMEM((2, length + PAD, QB), F32),
        pltpu.VMEM((GROUP, length), F32),
        pltpu.VMEM((GROUP, length), F32),
    ]


def attend_body(prefix_count, x_ref, w_ref, extra, segr_ref, q_ref, k_ref, v_ref, att_ref, lse_ref,
                mask_ref, ke_ref, vt_ref, s_ref, top_ref, sum_ref):
    length = x_ref.shape[0]
    pk, pv, bias = extra
    x = x_ref[...]
    q_ref[...] = ((dot(x, w_ref[0], NT) + bias[0:1]) * HD ** (-0.5)).astype(BF16)
    k = (dot(x, w_ref[1], NT) + bias[1:2]).astype(BF16)
    k_ref[...] = k
    fill_extended(ke_ref, pk, k)
    v = (dot(x, w_ref[2], NT) + bias[2:3]).astype(BF16)
    v_ref[...] = v
    vt_ref[...] = v.T
    pvt = pv.T
    seg_row = segr_ref[...]
    seg_col = column_of(seg_row)
    fill_prefix_mask(mask_ref, length, prefix_count)
    heads, zero = head_lanes(), jnp.zeros((), BF16)
    work = [(block, h) for block in blocks_of(length) for h in range(GROUP)]

    def ask(n):
        block, h = work[n]
        i, _, last, (low, high) = block
        if h == 0:
            fill_mask(mask_ref, seg_col, seg_row, block)
        asked = jnp.where(heads == h, q_ref[i * QB : last, :], zero)
        s_ref[n % 2, 0 : high - low, :] = dot(ke_ref[low:high, :], asked, NT) + mask_ref[low:high, :]

    ask(0)
    for n, (block, h) in enumerate(work):
        if n + 1 < len(work):
            ask(n + 1)
        i, first, last, (low, high) = block
        rows, span = slice(i * QB, last), slice(h * HD, (h + 1) * HD)
        (pa, pb), (ta, tb) = strip_parts(block)
        s = s_ref[n % 2, 0 : high - low, :]
        top = jnp.max(s, axis=0, keepdims=True)
        e = jnp.exp(s - top)
        total = jnp.sum(e, axis=0, keepdims=True)
        top_ref[h : h + 1, rows] = top
        sum_ref[h : h + 1, rows] = total
        e = e.astype(BF16)
        o = dot(vt_ref[span, first:last], e[ta:tb]) + dot(pvt[span, :], e[pa:pb])
        att_ref[span, rows] = (o * (1.0 / total)).astype(BF16)
    lse_ref[...] = top_ref[...] + jnp.log(sum_ref[...])


def attend_own_kernel(prefix_count, member_ref, tok_ref, gain_ref, shift_ref, w_ref, small_ref, segr_ref, bias_ref,
                      x_ref, q_ref, k_ref, v_ref, att_ref, lse_ref, out_ref, *scratch):
    length = tok_ref.shape[0]
    for t in range(0, length, TB):
        normed, _ = normalize(tok_ref[t : t + TB, :].astype(F32))
        x_ref[t : t + TB, :] = (normed * gain_ref[...] + shift_ref[...]).astype(BF16)
    attend_body(prefix_count, x_ref, w_ref, extras(member_ref[0], small_ref, False), segr_ref,
                q_ref, k_ref, v_ref, att_ref, lse_ref, *scratch)
    for t in range(0, length, TB):
        base = tok_ref[t : t + TB, :].astype(F32) + bias_ref[...]
        out_ref[t : t + TB, :] = base + dot(att_ref[:, t : t + TB], w_ref[3], TN)


def attend_others_kernel(prefix_count, carried, member_ref, x_ref, *refs):
    pieces, (small_ref, segr_ref, acc_ref) = refs[:8], refs[8:11]
    refs = refs[11 + carried :]
    w_ref, q_ref, k_ref, v_ref, att_ref, lse_ref, out_ref = refs[:7]
    half = HD // 2
    for j, ref in enumerate(pieces):
        for c in range(4):
            w_ref[c, j * half : (j + 1) * half, :] = ref[c * half : (c + 1) * half, :].astype(BF16)
    attend_body(prefix_count, x_ref, w_ref, extras(member_ref[0], small_ref, True), segr_ref,
                q_ref, k_ref, v_ref, att_ref, lse_ref, *refs[7:])

    @pl.when(pl.program_id(0) == 0)
    def _():
        out_ref[...] = acc_ref[...]

    for t in range(0, x_ref.shape[0], TB):
        out_ref[t : t + TB, :] += dot(att_ref[:, t : t + TB], w_ref[3], TN)


def attend_own(prefix_count, *args):
    length, width = args[1].shape
    return resident(
        functools.partial(attend_own_kernel, prefix_count),
        [shape_of((length, width), BF16)]
        + [shape_of((length, WIDE), BF16)] * 3
        + [shape_of((WIDE, length), BF16), shape_of((GROUP, length), F32), shape_of((length, width), F32)],
        attend_scratch(length),
        "attend_own",
        22,
        args,
    )


SCALARS = pl.BlockSpec(memory_space=pltpu.SMEM)


def once(values):
    return pl.BlockSpec(values.shape, lambda g: (0,) * len(values.shape), pipeline_mode=pl.Buffered(1))


def each(*block):
    return pl.BlockSpec((None,) + block, lambda g: (g,) + (0,) * len(block))


def rows_of(count, width):
    return pl.BlockSpec((count, width), lambda g: (g, 0))


def attend_others(prefix_count, first, count, total, member, x, pieces, small, seg, acc, carry=()):
    length, width = x.shape
    saved = [(4, WIDE, width), (length, WIDE), (length, WIDE), (length, WIDE), (WIDE, length), (GROUP, length)]
    piece = lambda at: pl.BlockSpec((128, width), lambda g: (g + at, 0))
    part = lambda block: pl.BlockSpec((None,) + block, lambda g: (g + first,) + (0,) * len(block))
    return pl.pallas_call(
        functools.partial(attend_others_kernel, prefix_count, len(carry)),
        grid=(count,),
        in_specs=[SCALARS, once(x)]
        + [piece(at) for _, at in pieces]
        + [pl.BlockSpec((48, WIDE), lambda g: (g + first, 0)), once(seg), once(acc)]
        + [pl.BlockSpec(memory_space=pl.ANY)] * len(carry),
        out_specs=[part(block) for block in saved] + [pl.BlockSpec((length, width), lambda g: (0, 0))],
        out_shape=[shape_of((total,) + block, BF16) for block in saved[:-1]]
        + [shape_of((total, GROUP, length), F32), shape_of((length, width), F32)],
        scratch_shapes=attend_scratch(length),
        input_output_aliases={13 + n: n for n in range(len(carry))},
        cost_estimate=BRIEF,
        compiler_params=params(50),
        name="attend_others",
    )(member, x, *[values for values, _ in pieces], small, seg, acc, *carry)


def back_scratch(length):
    low = lambda *shape: pltpu.VMEM(shape, BF16)
    return [
        pltpu.VMEM((length + 2 * PAD, QB), F32),
        low(length + 2 * PAD, WIDE),
        low(length + 2 * PAD, WIDE),
        low(WIDE, length),
        low(WIDE, length),
        low(WIDE, length),
        low(length, WIDE),
        pltpu.VMEM((2, length + PAD, QB), F32),
        pltpu.VMEM((2, length + PAD, QB), F32),
        pltpu.VMEM((GROUP, length), F32),
        pltpu.VMEM((2, WIDE, length), F32),
    ]


def back_body(prefix_count, extra, w_ref, q_ref, k_ref, v_ref, att_ref, lse_ref, segr_ref, low_ref, gjt_ref, gp_ref,
              mask_ref, ke_ref, ve_ref, kt_ref, qt_ref, dot_ref, do_ref, s_ref, dp_ref, delta_ref, acc_ref):
    length = q_ref.shape[0]
    pk, pv, _ = extra
    do = dot(low_ref[...], w_ref[3], NT).astype(BF16)
    do_ref[...] = do
    dot_ref[...] = do.T
    kt_ref[...] = k_ref[...].T
    qt_ref[...] = q_ref[...].T
    fill_extended(ke_ref, pk, k_ref[...])
    fill_extended(ve_ref, pv, v_ref[...])
    pkt = pk.T
    for h in range(GROUP):
        span = slice(h * HD, (h + 1) * HD)
        products = dot_ref[span, :].astype(F32) * att_ref[span, :].astype(F32)
        delta_ref[h : h + 1, :] = jnp.sum(products, axis=0, keepdims=True)
    seg_row = segr_ref[...]
    seg_col = column_of(seg_row)
    fill_prefix_mask(mask_ref, length, prefix_count)
    acc_ref[...] = jnp.zeros_like(acc_ref)
    if gp_ref is not None:
        gp_ref[...] = jnp.zeros_like(gp_ref)
    heads, zero = head_lanes(), jnp.zeros((), BF16)
    work = [(block, h) for block in blocks_of(length) for h in range(GROUP)]

    def ask(n):
        block, h = work[n]
        i, _, last, (low, high) = block
        if h == 0:
            fill_mask(mask_ref, seg_col, seg_row, block)
        rows = slice(i * QB, last)
        asked = jnp.where(heads == h, q_ref[rows, :], zero)
        grad = jnp.where(heads == h, do_ref[rows, :], zero)
        s_ref[n % 2, 0 : high - low, :] = dot(ke_ref[low:high, :], asked, NT) + mask_ref[low:high, :]
        dp_ref[n % 2, 0 : high - low, :] = dot(ve_ref[low:high, :], grad, NT)

    ask(0)
    for n, (block, h) in enumerate(work):
        if n + 1 < len(work):
            ask(n + 1)
        i, first, last, (low, high) = block
        rows, span = slice(i * QB, last), slice(h * HD, (h + 1) * HD)
        (pa, pb), (ta, tb) = strip_parts(block)
        p = jnp.exp(s_ref[n % 2, 0 : high - low, :] - lse_ref[h : h + 1, rows])
        ds = (p * (dp_ref[n % 2, 0 : high - low, :] - delta_ref[h : h + 1, rows])).astype(BF16)
        p = p.astype(BF16)
        dq = dot(kt_ref[span, first:last], ds[ta:tb]) + dot(pkt[span, :], ds[pa:pb])
        gjt_ref[span, rows] = dq.astype(BF16) * jnp.asarray(HD ** (-0.5), BF16)
        acc_ref[0, span, first:last] += dot(qt_ref[span, rows], ds[ta:tb], NT)
        acc_ref[1, span, first:last] += dot(dot_ref[span, rows], p[ta:tb], NT)
        if gp_ref is not None:
            gp_ref[0, span, :] += dot(qt_ref[span, rows], ds[pa:pb], NT)
            gp_ref[1, span, :] += dot(dot_ref[span, rows], p[pa:pb], NT)
    gjt_ref[WIDE : 2 * WIDE, :] = acc_ref[0].astype(BF16)
    gjt_ref[2 * WIDE : 3 * WIDE, :] = acc_ref[1].astype(BF16)


def take_own(out_ref, rows, values, index):
    width = out_ref.shape[1]
    for k in range(values.shape[1] // width):

        @pl.when(index == k)
        def _():
            out_ref[rows, :] = values[:, k * width : (k + 1) * width].astype(out_ref.dtype)


def norm_back(grad, normed, inverse, gain):
    scaled = grad * gain
    mean = jnp.mean(scaled, axis=-1, keepdims=True)
    return inverse * (scaled - mean - normed * jnp.mean(scaled * normed, axis=-1, keepdims=True))


def pack_sums(prefix_count, z, gp_ref, sums_ref, gjt_ref, ups_ref, outer_ref, pack_ref):
    pack_ref[...] = jnp.zeros_like(pack_ref)
    inner = 0.0
    for k in range(2):
        gp = gp_ref[k].T
        pack_ref[k * PAD : (k + 1) * PAD, :] = gp
        for _ in range(3):
            part = gp.astype(BF16)
            inner = inner + dot(part, outer_ref[:, k * WIDE : (k + 1) * WIDE], NT)
            gp = gp - part.astype(F32)
    for n in range(4):
        take_own(pack_ref, slice(2 * PAD + n, 2 * PAD + n + 1), sums_ref[n : n + 1, :], z)
    joint = dot(jnp.ones((8, gjt_ref.shape[1]), BF16), gjt_ref[...], NT)
    for k in range(3):
        pack_ref[2 * PAD + 4 + k : 2 * PAD + 5 + k, :] = joint[0:1, k * WIDE : (k + 1) * WIDE]
    for k in range(ups_ref.shape[1] // WIDE):
        pack_ref[2 * PAD + 8 + k : 2 * PAD + 9 + k, :] = ups_ref[:, k * WIDE : (k + 1) * WIDE]
    begin = 2 * PAD + 8 + ups_ref.shape[1] // WIDE
    for k in range(inner.shape[1] // WIDE):
        to = slice(begin + k * prefix_count, begin + (k + 1) * prefix_count)
        pack_ref[to, :] = inner[0:prefix_count, k * WIDE : (k + 1) * WIDE]


def back_own_kernel(prefix_count, places_ref, w_ref, q_ref, k_ref, v_ref, att_ref, lse_ref, small_ref, segr_ref,
                    low_ref, sums_ref, ups_ref, outer_ref, gjt_ref, pack_ref, ga_ref, gp_ref, *scratch):
    back_body(prefix_count, extras(places_ref[1], small_ref, False), w_ref, q_ref, k_ref, v_ref, att_ref, lse_ref,
              segr_ref, low_ref, gjt_ref, gp_ref, *scratch)
    w = w_ref[0:3].reshape(3 * WIDE, w_ref.shape[2])
    for t in range(0, low_ref.shape[0], TB):
        ga_ref[t : t + TB, :] = dot(gjt_ref[:, t : t + TB], w, TN)
    pack_sums(prefix_count, places_ref[0], gp_ref, sums_ref, gjt_ref, ups_ref, outer_ref, pack_ref)


def back_others_kernel(prefix_count, places_ref, w_ref, q_ref, k_ref, v_ref, att_ref, lse_ref, small_ref, segr_ref,
                       low_ref, gain_ref, from_ga, from_tok, from_part, out_ref, sums_ref, ga_ref, tok_ref, part_ref, sems, gjt_ref,
                       *scratch):
    length, step = low_ref.shape[0], pl.program_id(0)
    final = pl.num_programs(0) - 1
    pairs = ((from_ga, ga_ref), (from_tok, tok_ref), (from_part, part_ref))
    copies = [pltpu.make_async_copy(source, target, sems.at[n]) for n, (source, target) in enumerate(pairs)]

    @pl.when(step == 0)
    def _():
        for copy in copies:
            copy.start()

    back_body(prefix_count, extras(places_ref[1], small_ref, True), w_ref, q_ref, k_ref, v_ref, att_ref, lse_ref,
              segr_ref, low_ref, gjt_ref, None, *scratch)
    w = w_ref[0:3].reshape(3 * WIDE, w_ref.shape[2])

    @pl.when(step == 0)
    def _():
        for copy in copies:
            copy.wait()

    @pl.when(step < final)
    def _():
        for t in range(0, length, TB):
            ga_ref[t : t + TB, :] += dot(gjt_ref[:, t : t + TB], w, TN)

    @pl.when(step == final)
    def _():
        sums = [0.0, 0.0]
        for t in range(0, length, TB):
            rows = slice(t, t + TB)
            ga = ga_ref[rows, :] + dot(gjt_ref[:, rows], w, TN)
            normed, inverse = normalize(tok_ref[rows, :].astype(F32))
            grad = norm_back(ga, normed, inverse, gain_ref[...])
            width = out_ref.shape[1]
            for k in range(grad.shape[1] // width):

                @pl.when(places_ref[0] == k)
                def _():
                    out_ref[rows, :] = (part_ref[rows, :] + grad[:, k * width : (k + 1) * width]).astype(BF16)

            sums[0] = sums[0] + jnp.sum(ga * normed, axis=0, keepdims=True)
            sums[1] = sums[1] + jnp.sum(ga, axis=0, keepdims=True)
        sums_ref[...] = jnp.zeros_like(sums_ref)
        for n in range(2):
            take_own(sums_ref, slice(n, n + 1), sums[n], places_ref[0])


def back_own(prefix_count, *args):
    length, width = args[9].shape
    ups, outer = args[-2:]
    packed = 2 * PAD + 8 + ups.shape[1] // WIDE + outer.shape[0] // WIDE * prefix_count
    return resident(
        functools.partial(back_own_kernel, prefix_count),
        [
            shape_of((3 * WIDE, length), BF16),
            shape_of((-(-packed // 8) * 8, WIDE), F32),
            shape_of((length, width), F32),
        ],
        [pltpu.VMEM((2, WIDE, PAD), F32)] + back_scratch(length),
        "back_own",
        30,
        args,
    )


def back_others(prefix_count, places, saved, small, seg, low, ga, tokens, part, gain):
    length, width = low.shape
    return pl.pallas_call(
        functools.partial(back_others_kernel, prefix_count),
        grid=(saved[0].shape[0],),
        in_specs=[SCALARS]
        + [each(*values.shape[1:]) for values in saved]
        + [rows_of(48, WIDE)]
        + [once(values) for values in (seg, low, gain)]
        + [pl.BlockSpec(memory_space=pl.ANY)] * 3,
        out_specs=[pl.BlockSpec((length, WIDE), lambda g: (0, 0)), pl.BlockSpec((8, WIDE), lambda g: (0, 0))],
        out_shape=[shape_of((length, WIDE), BF16), shape_of((8, WIDE), F32)],
        scratch_shapes=[
            pltpu.VMEM((length, width), F32),
            pltpu.VMEM((length, width), BF16),
            pltpu.VMEM((length, WIDE), F32),
            pltpu.SemaphoreType.DMA((3,)),
            pltpu.VMEM((3 * WIDE, length), BF16),
        ]
        + back_scratch(length),
        cost_estimate=BRIEF,
        compiler_params=params(50),
        name="back_others",
    )(places, *saved, small, seg, low, gain, ga, tokens, part)


def gelu_pair(v):
    c = 0.7978845608028654
    square = v * v
    t = jnp.tanh(v * (c + (0.044715 * c) * square))
    half = 0.5 + 0.5 * t
    return v * half, half + (0.5 * v) * (1.0 - t * t) * (c + (3.0 * 0.044715 * c) * square)


def mix_rows(mid, cot, up_ref, up_dims, bias, down_ref, act_ref, gp_ref, rows, pre_ref, g_ref):
    hidden = down_ref.shape[0]
    chunks = [slice(c, c + TB) for c in range(0, hidden, TB)]

    def ask(n):
        up = up_ref[:, chunks[n]] if up_dims is NN else up_ref[chunks[n], :]
        pre_ref[n % 2] = dot(mid, up, up_dims) + bias[:, chunks[n]]
        g_ref[n % 2] = dot(cot, down_ref[chunks[n], :], NT)

    ask(0)
    for n, chunk in enumerate(chunks):
        if n + 1 < len(chunks):
            ask(n + 1)
        act, slope = gelu_pair(pre_ref[n % 2])
        act_ref[rows, chunk] = act.astype(BF16)
        gp_ref[rows, chunk] = (g_ref[n % 2] * slope).astype(BF16)


def mix_own_kernel(z_ref, res_ref, cot_ref, gain_ref, shift_ref, up_ref, bias_ref, down_ref, dbias_ref,
                   mid_ref, act_ref, gp_ref, share_ref, bsum_ref, gm_ref, pre_ref, g_ref):
    width = share_ref.shape[1]
    own = pl.ds(pl.multiple_of(z_ref[0] * width, width), width)
    every = slice(0, TB)
    normed, _ = normalize(res_ref[...])
    mid = (normed * gain_ref[...] + shift_ref[...]).astype(BF16)
    mid_ref[...] = mid
    mix_rows(mid, cot_ref[...], up_ref, NN, bias_ref[...], down_ref, act_ref, gp_ref, every, pre_ref, g_ref)
    share_ref[...] = res_ref[:, own] + dbias_ref[:, own] + dot(act_ref[...], down_ref[:, own])
    gp = gp_ref[...]
    gm_ref[...] = dot(gp, up_ref[...], NT)

    @pl.when(pl.program_id(0) == 0)
    def _():
        bsum_ref[...] = jnp.zeros_like(bsum_ref)

    bsum_ref[...] += jnp.sum(gp.astype(F32), axis=0, keepdims=True)


def mix_own(own_width, z, residual, cotangent, gain, shift, up, up_bias, down, down_bias):
    length, width = residual.shape
    hidden = up.shape[1]
    rows = lambda w: rows_of(TB, w)
    fixed = [once(values) for values in (gain, shift, up, up_bias, down, down_bias)]
    return pl.pallas_call(
        mix_own_kernel,
        grid=(length // TB,),
        in_specs=[SCALARS, rows(width), rows(width)] + fixed,
        out_specs=[rows(width), rows(hidden), rows(hidden), rows(own_width), pl.BlockSpec((1, hidden), lambda t: (0, 0)), rows(width)],
        out_shape=[
            shape_of((length, width), BF16),
            shape_of((length, hidden), BF16),
            shape_of((length, hidden), BF16),
            shape_of((length, own_width), F32),
            shape_of((1, hidden), F32),
            shape_of((length, width), F32),
        ],
        scratch_shapes=[pltpu.VMEM((2, TB, TB), F32)] * 2,
        cost_estimate=BRIEF,
        compiler_params=params(36),
        name="mix_own",
    )(z, residual, cotangent, gain, shift, up, up_bias, down, down_bias)


def mix_kernel(places, last, z_ref, mid_ref, cot_ref, small_ref, share_in, gm_in, *refs):
    pieces, per = len(places), 128
    if last:
        res_ref, gain_ref, *refs = refs
    sources, refs = refs[: 2 * pieces], refs[2 * pieces :]
    if last:
        share_ref, low_ref, own_ref, sums_ref, *refs = refs
    else:
        share_ref, gm_ref, *refs = refs
    up_ref, down_ref, part_ref, act_ref, gp_ref, pre_ref, g_ref = refs
    step = pl.program_id(0)
    width = share_ref.shape[1]
    own = pl.ds(pl.multiple_of(z_ref[0] * width, width), width)
    @pl.when(step == 0)
    def _():
        for j in range(pieces):
            up_ref[j * per : (j + 1) * per, :] = sources[2 * j][...].astype(BF16)
            down_ref[j * per : (j + 1) * per, :] = sources[2 * j + 1][...].astype(BF16)
        part_ref[...] = down_ref[:, own]
        if last:
            sums_ref[...] = jnp.zeros_like(sums_ref)

    def block():
        biases = {k: reorder(small_ref[48 * k + 40 : 48 * k + 48, 0:per], z_ref[1], 0) for k, _ in places}
        bias = jnp.concatenate([biases[k][j : j + 1] for k, j in places], axis=1)
        mix_rows(mid_ref[...], cot_ref[...], up_ref, NT, bias, down_ref, act_ref, gp_ref, slice(0, TB), pre_ref, g_ref)
        share_ref[...] = (share_in[...] + dot(act_ref[...], part_ref[...])).astype(share_ref.dtype)
        gm = gm_in[...] + dot(gp_ref[...], up_ref[...])
        if not last:
            gm_ref[...] = gm
            return
        normed, inverse = normalize(res_ref[...])
        cot = cot_ref[...].astype(F32)
        grad = cot + norm_back(gm, normed, inverse, gain_ref[...])
        low_ref[...] = grad.astype(BF16)
        take_own(own_ref, slice(0, TB), grad, z_ref[0])
        for n, values in enumerate((gm * normed, gm, grad, cot)):
            sums_ref[n : n + 1, :] += jnp.sum(values, axis=0, keepdims=True)

    block()


def mix(places, blocks, last, z, mid, cotangent, small, share, gm, *arrays):
    length, width = mid.shape
    hidden = 128 * len(places)
    own_width = share.shape[1]
    rows = lambda w: rows_of(TB, w)
    low = lambda *shape: pltpu.VMEM(shape, BF16)
    piece = lambda at: pl.BlockSpec((128, width), lambda t: (at, 0), pipeline_mode=pl.Buffered(1))
    outs = [(rows(own_width), shape_of((length, own_width), BF16 if last else F32))]
    if last:
        outs += [(rows(width), shape_of((length, width), BF16)), (rows(own_width), shape_of((length, own_width), F32))]
        outs += [(pl.BlockSpec((8, width), lambda t: (0, 0)), shape_of((8, width), F32))]
    else:
        outs += [(rows(width), shape_of((length, width), F32))]
    return pl.pallas_call(
        functools.partial(mix_kernel, places, last),
        grid=(length // TB,),
        in_specs=[SCALARS, rows(width), rows(width), once(small), rows(own_width), rows(width)]
        + ([rows(width), once(arrays[1])] if last else [])
        + [piece(at) for at in blocks],
        out_specs=[spec for spec, _ in outs],
        out_shape=[shape for _, shape in outs],
        scratch_shapes=[
            low(hidden, width),
            low(hidden, width),
            low(hidden, own_width),
            low(TB, hidden),
            low(TB, hidden),
        ]
        + [pltpu.VMEM((2, TB, TB), F32)] * 2,
        input_output_aliases={} if last else {4: 0, 5: 1},
        cost_estimate=BRIEF,
        compiler_params=params(40),
        name="mix_others",
    )(z, mid, cotangent, small, share, gm, *arrays)


def hidden_grad_kernel(mid_ref, cot_ref, gp_ref, act_ref, out_ref):
    parts, per = out_ref.shape[0], out_ref.shape[1] // 2
    for at, left, right in ((0, mid_ref, gp_ref), (per, cot_ref, act_ref)):
        grad = dot(left[...], right[...], TN)
        for a in range(parts):
            out_ref[a, at : at + per, :] = grad[a * per : (a + 1) * per]


def hidden_grad(parts, mid, cotangent, gp, act):
    length, width = mid.shape
    hidden = gp.shape[1]
    per = width // parts
    column = pl.BlockSpec((length, TB), lambda j: (0, j))
    return pl.pallas_call(
        hidden_grad_kernel,
        grid=(width // TB,),
        in_specs=[column, column, once(gp), once(act)],
        out_specs=pl.BlockSpec((TB // per, 2 * per, hidden), lambda j: (j, 0, 0)),
        out_shape=shape_of((parts, 2 * per, hidden), F32),
        cost_estimate=BRIEF,
        compiler_params=params(30),
        name="hidden_grad",
    )(mid, cotangent, gp, act)


def head_grad_kernel(places_ref, x_ref, low_ref, gjt_ref, att_ref, keep_ref, send_ref):
    wide, core, chip = gjt_ref.shape[0], places_ref[1] & 1, places_ref[1] >> 1
    for start, left, right in ((0, gjt_ref, x_ref), (wide, att_ref, low_ref)):
        for r in range(0, left.shape[0], TB):
            grad = dot(left[r : r + TB, :], right[...])
            for mine in range(2):

                @pl.when(core == mine)
                def _():
                    for j in range(8):
                        out_ref = keep_ref if j % 2 == mine else send_ref
                        out_ref[(j // 2) ^ chip, start + r : start + r + TB, :] = grad[:, 128 * j : 128 * (j + 1)]


def head_grad(*args):
    rows = args[3].shape[0] + args[4].shape[0]
    return resident(head_grad_kernel, [shape_of((4, rows, 128), F32)] * 2, [], "head_grad", 16, args)


def fold_kernel(places_ref, keep_ref, got_ref, far_x_ref, far_y_ref, stay_ref, near_ref):
    half = keep_ref.shape[1] // 2
    total = lambda s, rows: keep_ref[s, rows, :] + got_ref[s, rows, :]
    top, bottom = slice(0, half), slice(half, 2 * half)
    near_ref[...] = keep_ref[0] + got_ref[0]
    far_x_ref[0], far_x_ref[1] = total(1, top), total(3, top)
    far_y_ref[0], far_y_ref[1] = total(2, bottom), total(3, bottom)
    stay_ref[0], stay_ref[1] = total(2, top), total(1, bottom)


def fold(*args):
    _, rows, lanes = args[1].shape
    half = shape_of((2, rows // 2, lanes), F32)
    return resident(fold_kernel, [half, half, half, shape_of((rows, lanes), F32)], [], "fold", 12, args)


def shards(
    tokens, segment_ids, attention_gain, attention_shift, joint_weight, joint_bias, output_weight, output_bias,
    mixer_gain, mixer_shift, up_weight, up_bias, down_weight, down_bias, prefix_table, inner_weight, inner_bias,
    outer_weight, outer_bias, cotangent,
):
    length, width = tokens.shape
    local = joint_weight.shape[2]
    hidden = up_weight.shape[1]
    prefix_count = prefix_table.shape[0]
    batch_size, tensor_size = lax.axis_size("batch"), lax.axis_size("tensor")
    z = lax.axis_index("tensor").astype(jnp.int32)
    member = (lax.axis_index("batch") % 8).astype(jnp.int32)
    member_arr, places = member.reshape(1), jnp.stack([z, member])

    def own_columns(values):
        return lax.dynamic_slice_in_dim(values, z * local, local, values.ndim - 1)

    def along(values, k):
        return lax.ppermute(values, "tensor", [(i, i ^ k) for i in range(tensor_size)])

    def across(values, k):
        return lax.ppermute(values, "batch", [(i, i ^ k) for i in range(batch_size)])

    now = [member_arr]

    def after(values):
        return lax.optimization_barrier((values, *now))[0]

    def wait(*values):
        held = lax.optimization_barrier((*values, *now))
        now[:] = [held[0]]
        return held[0] if len(values) == 1 else held[: len(values)]

    def run(call, *args):
        outs = call(after(args[0]), *args[1:])
        now[:] = [outs[-1] if isinstance(outs, (list, tuple)) else outs]
        return outs

    row = lambda v: v.reshape(1, -1)
    stack = lambda *parts: jnp.concatenate(parts, axis=0)

    def gather(*parts):
        places = [(start, rows) for _, start, rows in parts]
        arrays = [values for values, _, _ in parts]
        return run(lambda *arrays: gather_rows(places, *arrays), *arrays)

    def rows(values, block, count=1):
        return values, block * 128, count * 128

    whole = lambda values: (values, 0, values.shape[0])

    own_heads, send_heads = run(head_pieces, member_arr, joint_weight, output_weight)
    a1, a2 = along(after(send_heads[0]), 1), along(after(send_heads[0]), 2)

    def prefixes(prefix_table, inner_weight):
        hidden_prefix = jnp.tanh(jnp.dot(prefix_table, inner_weight.astype(F32), precision=PRECISE) + inner_bias)
        pairs = jnp.einsum("pr,rke->kpe", hidden_prefix, outer_weight.astype(F32), precision=PRECISE)
        pairs = jnp.pad(pairs + outer_bias[:, None, :], ((0, 0), (0, PAD - prefix_count), (0, 0)))
        ups = jnp.pad(up_bias.reshape(8, hidden // 8), ((0, 0), (0, local - hidden // 8)))
        joints = jnp.pad(joint_bias, ((0, 5), (0, 0)))
        return hidden_prefix, stack(pairs.reshape(2 * PAD, local), joints, ups)

    hidden_prefix, small = run(prefixes, prefix_table, inner_weight)
    send_hidden = run(hidden_pieces, member_arr, up_weight, down_weight)
    smalls = [along(after(small), k) for k in (1, 2, 3)]
    a1, a2, *smalls = wait(a1, a2, *smalls)
    a12 = gather(whole(a1), whole(a2))
    x12, y12 = across(after(a12), 2), across(after(a12), 4)
    a3, a1d = along(after(send_heads[0]), 3), along(after(send_heads[1]), 1)
    c12 = across(after(a12), 1)
    x, *saved_own, residual = run(
        functools.partial(attend_own, prefix_count),
        member_arr, tokens, row(attention_gain), row(attention_shift), own_heads, small, segment_ids, row(output_bias),
    )
    extra = stack(*smalls)
    x12, y12, a3, a1d, c12 = wait(x12, y12, a3, a1d, c12)

    y3 = gather(whole(a3), rows(x12, 1))
    x3, y3 = across(after(a3), 2), across(after(y3), 4)
    f1, f2 = along(after(send_hidden[0]), 1), along(after(send_hidden[0]), 2)
    gb = gather(whole(x12), whole(y12), whole(a3), whole(a1d))
    cb = across(after(gb), 1)
    x3, y3, cb = wait(x3, y3, cb)
    a2d = run(lambda values: values[128:256], y3)
    ca2d = across(after(a2d), 1)
    a3d = across(after(y3[0:128]), 2)
    d12 = gather(whole(a1d), whole(a2d))
    ca2d = wait(ca2d)
    cd12 = gather(rows(cb, 5), whole(ca2d))
    *saved_others, residual = run(
        functools.partial(attend_others, prefix_count, 0, 2, 3),
        member_arr, x, [(a12, 0), (c12, 0), (x12, 0), (cb, 0), (y12, 0), (cb, 2), (d12, 0), (cd12, 0)], extra,
        segment_ids, residual,
    )
    a3d, f1, f2 = wait(a3d, f1, f2)

    f12 = gather(whole(f1), whole(f2))
    gc = gather(whole(x3), rows(y3, 0), whole(a3d), whole(f1), whole(f2))
    fx, fy = across(after(f12), 2), across(after(f12), 4)
    f3, f1d = along(after(send_hidden[0]), 3), along(after(send_hidden[1]), 1)
    cc = wait(across(after(gc), 1))
    *saved_others, residual = run(
        functools.partial(attend_others, prefix_count, 2, 1, 3),
        member_arr, x, [(a3, 0), (cb, 4), (x3, 0), (cc, 0), (y3, 0), (cc, 1), (a3d, 0), (cc, 2)], extra,
        segment_ids, residual, saved_others,
    )
    mid, act, gp, share, up_bias_sum, gm = run(
        functools.partial(mix_own, local),
        places, residual, cotangent, row(mixer_gain), row(mixer_shift), up_weight, row(up_bias), down_weight,
        row(down_bias),
    )
    hidden_part = run(functools.partial(hidden_grad, batch_size), mid, cotangent, gp, act)
    fx, fy, f3, f1d = wait(fx, fy, f3, f1d)

    x4 = gather(whole(f3), rows(fy, 3))
    y4 = gather(whole(f3), rows(fx, 2))
    x4, y4 = across(after(x4), 2), across(after(y4), 4)
    cfx, cfy, cf1d = [across(after(values), 1) for values in (fx, fy, f1d)]
    cfx, cfy, cf1d = wait(cfx, cfy, cf1d)

    def mix_more(pieces, share, gm, last=False):
        order = [(slot, j) for slot, j, _, _ in pieces]
        flat = [part for _, _, up, down in pieces for part in (up, down)]
        return run(
            functools.partial(mix, order, [at for _, at in flat], last),
            places, mid, cotangent, extra, share, gm, *([residual, row(mixer_gain)] if last else []),
            *[values for values, _ in flat],
        )

    def pair(values, at):
        return (values, at), (values, at + 1)

    def both(slot, number, mine, theirs):
        return [(slot, number, *pair(*mine)), (slot, number + 1, *pair(*theirs))]

    pieces = both(0, 0, (f12, 0), (cc, 3)) + both(0, 2, (fx, 0), (cfx, 0))
    share, gm = mix_more(pieces + both(0, 4, (fy, 0), (cfy, 0)) + both(0, 6, (f1d, 0), (cf1d, 0)), share, gm)
    pieces = both(1, 0, (f12, 2), (cc, 5)) + both(1, 2, (fx, 2), (cfx, 2))
    share, gm = mix_more(pieces + both(1, 4, (fy, 2), (cfy, 2)), share, gm)
    x4, y4 = wait(x4, y4)

    hidden_sum = lax.psum_scatter(after(hidden_part), "batch", scatter_dimension=0, tiled=False)
    x5, y5 = across(after(y4[128:256]), 2), across(after(x4[0:128]), 4)
    cx4, cy4, cf3 = wait(*[across(after(values), 1) for values in (x4, y4, f3)])
    pieces = [(1, 6, (y4, 2), (x4, 2)), (1, 7, (cy4, 2), (cx4, 2))] + both(2, 0, (f3, 0), (cf3, 0))
    share, gm = mix_more(pieces + both(2, 2, (x4, 0), (cx4, 0)) + both(2, 4, (y4, 0), (cy4, 0)), share, gm)
    x5, y5 = wait(x5, y5)

    cx5, cy5 = wait(across(after(x5), 1), across(after(y5), 1))
    pieces = [(2, 6, (y5, 0), (x5, 0)), (2, 7, (cy5, 0), (cx5, 0))]
    share, low, part, sums = mix_more(pieces, share, gm, True)
    gjt, totals, ga = run(
        functools.partial(back_own, prefix_count),
        places, own_heads, *saved_own, small, segment_ids, low, sums, up_bias_sum,
        outer_weight.reshape(outer_weight.shape[0], -1),
    )

    def spread(values, send, bits):
        if len(bits) == 1:
            return (send(after(values), bits[0]),)
        return tuple(send(after(values), k) for k in (bits[0], bits[1], bits[0] + bits[1]))

    def gather_sum(values, others):
        others = wait(*others) if len(others) > 1 else (wait(*others),)
        total = values + others[0]
        return total + (others[1] + others[2]) if len(others) == 3 else total

    def rounds_of(send, size):
        bits = [1 << b for b in range((size - 1).bit_length())]
        return [(send, bits[k : k + 2]) for k in range(0, len(bits), 2)]

    over_batch, over_tensor = rounds_of(across, batch_size), rounds_of(along, tensor_size)
    others = spread(totals, *over_batch[0])
    per = width // batch_size
    quick = batch_size == 8
    if quick:
        keep, send = run(head_grad, places, x, low, gjt, saved_own[3])
        far_x, far_y, stay, near = run(fold, places, keep, wait(across(after(send), 1)))
        far_x, far_y = across(after(far_x), 2), across(after(far_y), 4)
    tokens_gradient, gain_sums = run(
        functools.partial(back_others, prefix_count),
        places, saved_others, extra, segment_ids, low, ga, tokens, part, row(attention_gain),
    )
    totals = gather_sum(totals, others)
    if quick:
        far_x, far_y = wait(far_x, far_y)

        def halfway(stay, near, far_x, far_y):
            return stay[0] + far_x[1], stay[1] + far_y[1], near + stack(far_x[0], far_y[0])

        top, bottom, near = run(halfway, stay, near, far_x, far_y)
        top, bottom = across(after(top), 4), across(after(bottom), 2)
    turns = over_batch[1:] + over_tensor
    for n in range(max(len(turns), len(over_batch))):
        first = spread(totals, *turns[n]) if n < len(turns) else None
        second = spread(gain_sums, *over_batch[n]) if n < len(over_batch) else None
        if n == len(over_batch) - 1:
            batch_totals = totals
        if first is not None:
            totals = gather_sum(totals, first)
        if second is not None:
            gain_sums = gather_sum(gain_sums, second)
    if quick:
        top, bottom = wait(top, bottom)
        head_sum = near + stack(top, bottom)
    else:
        both_grads = stack(
            jnp.dot(gjt, x, preferred_element_type=F32), jnp.dot(saved_own[3], low, preferred_element_type=F32)
        )
        both_grads = both_grads.reshape(-1, batch_size, per).transpose(1, 0, 2)
        head_sum = lax.psum_scatter(both_grads, "batch", scatter_dimension=0, tiled=False)
    split = 2 * PAD + 8 + hidden // local
    halves = outer_weight.shape[0] // local
    inner = totals[split : split + halves * prefix_count].reshape(halves, prefix_count, local)

    grad_prefix = batch_totals[: 2 * PAD].reshape(2, PAD, local)[:, :prefix_count]
    mixed_total = batch_totals[2 * PAD : 2 * PAD + 4]
    joint_bias_total = batch_totals[2 * PAD + 4 : 2 * PAD + 7]
    up_bias_total = batch_totals[2 * PAD + 8 : split]
    grad_hidden_prefix = inner.transpose(1, 0, 2).reshape(prefix_count, -1)
    outer_rows = outer_weight.shape[0] // batch_size
    hidden_own = lax.dynamic_slice_in_dim(hidden_prefix, lax.axis_index("batch") * outer_rows, outer_rows, 1)
    outer_total = jnp.einsum("pr,kpe->rke", hidden_own, grad_prefix, precision=PRECISE)
    outer_bias_total = jnp.sum(grad_prefix, axis=1)
    grad_inner = grad_hidden_prefix * (1.0 - hidden_prefix * hidden_prefix)
    inner_total = jnp.einsum("pd,pr->dr", prefix_table, grad_inner, precision=PRECISE)
    inner_bias_total = jnp.sum(grad_inner, axis=0)
    table_total = jnp.einsum("pr,dr->pd", grad_inner, inner_weight.astype(F32), precision=PRECISE)

    up_total, down_total = hidden_sum[:per], hidden_sum[per:].T
    joint_total = head_sum[: 3 * local].reshape(3, local, per).transpose(0, 2, 1)
    output_total = head_sum[3 * local :]
    return (
        share,
        tokens_gradient,
        gain_sums[0],
        gain_sums[1],
        joint_total,
        joint_bias_total,
        output_total,
        mixed_total[2],
        mixed_total[0],
        mixed_total[1],
        up_total,
        up_bias_total.reshape(hidden),
        down_total,
        mixed_total[3],
        table_total,
        inner_total,
        inner_bias_total,
        outer_total,
        outer_bias_total,
    )


def solution(mesh):
    placed = (
        P("batch", None),
        P("batch", None),
        P(),
        P(),
        P(None, None, "tensor"),
        P(None, "tensor"),
        P("tensor", None),
        P(),
        P(),
        P(),
        P(None, "tensor"),
        P("tensor"),
        P("tensor", None),
        P(),
        P(),
        P(),
        P(),
        P(None, None, "tensor"),
        P(None, "tensor"),
        P("batch", None),
    )
    return jax.shard_map(
        shards,
        mesh=mesh,
        in_specs=placed,
        out_specs=(
            P("batch", "tensor"),
            P("batch", "tensor"),
            P("tensor"),
            P("tensor"),
            P(None, "batch", "tensor"),
            P(None, "tensor"),
            P("tensor", "batch"),
            P("tensor"),
            P("tensor"),
            P("tensor"),
            P("batch", "tensor"),
            P("tensor"),
            P("tensor", "batch"),
            P("tensor"),
            P(),
            P(),
            P(),
            P("batch", None, "tensor"),
            P(None, "tensor"),
        ),
        check_vma=False,
    )
```

```python
import functools

import jax
import jax.numpy as jnp
from jax import lax
from jax.experimental import pallas as pl
from jax.experimental.pallas import tpu as pltpu
from jax.sharding import PartitionSpec as P

HD = 64
GROUP = 4
WIDE = GROUP * HD
QB = 256
CUT = 64
PAD = 16
TB = 256
EPSILON = 1e-05
PRECISE = lax.Precision.HIGHEST
NEGATIVE = -1e30
F32, BF16 = jnp.float32, jnp.bfloat16
NN = (((1,), (0,)), ((), ()))
NT = (((1,), (1,)), ((), ()))
TN = (((0,), (0,)), ((), ()))
shape_of = jax.ShapeDtypeStruct
BRIEF = pl.CostEstimate(flops=1024, bytes_accessed=1024, transcendentals=0)


def dot(a, b, dims=NN):
    return lax.dot_general(a, b, dims, preferred_element_type=F32)


def params(mib):
    return pltpu.CompilerParams(vmem_limit_bytes=mib * 2**20)


def resident(kernel, outs, scratch, name, mib, args, aliases={}):
    vm = pl.BlockSpec(memory_space=pltpu.VMEM)
    return pl.pallas_call(
        kernel,
        out_shape=outs,
        in_specs=[pl.BlockSpec(memory_space=pltpu.SMEM)] + [vm] * (len(args) - 1),
        out_specs=[vm] * len(outs),
        scratch_shapes=scratch,
        input_output_aliases=aliases,
        cost_estimate=BRIEF,
        compiler_params=params(mib),
        name=name,
    )(*args)


def normalize(values):
    centered = values - jnp.mean(values, axis=-1, keepdims=True)
    inverse = lax.rsqrt(jnp.mean(centered * centered, axis=-1, keepdims=True) + EPSILON)
    return centered * inverse, inverse


def heads_kernel(turn, member_ref, joint_ref, out_ref, own_ref, send_ref):
    for c in range(3):
        own_ref[c] = joint_ref[c].T
    own_ref[3] = out_ref[...]
    rows = own_ref.shape[1] // 8
    for p in range(2):
        member = member_ref[0] ^ (turn * p)
        start = pl.multiple_of(member * rows, rows)
        for c in range(4):
            send_ref[p, c * rows : (c + 1) * rows, :] = own_ref[c, pl.ds(start, rows), :].astype(F32)


def head_pieces(member, joint_weight, output_weight):
    _, width, local = joint_weight.shape
    vm = pl.BlockSpec(memory_space=pltpu.VMEM)
    return pl.pallas_call(
        functools.partial(heads_kernel, 6),
        out_shape=[shape_of((4, local, width), BF16), shape_of((2, local // 2, width), F32)],
        in_specs=[pl.BlockSpec(memory_space=pltpu.SMEM), vm, vm],
        out_specs=[vm, vm],
        cost_estimate=BRIEF,
        compiler_params=params(12),
        name="head_pieces",
    )(member, joint_weight, output_weight)


def hidden_kernel(member_ref, up_ref, down_ref, send_ref):
    rows = down_ref.shape[0]
    send_ref[0, 0:rows, :] = up_ref[...].T.astype(F32)
    send_ref[0, rows : 2 * rows, :] = down_ref[...].astype(F32)


def hidden_pieces(member, up_weight, down_weight):
    width, local = up_weight.shape
    rows = local // 8
    return pl.pallas_call(
        hidden_kernel,
        out_shape=shape_of((2, 2 * rows, width), F32),
        grid_spec=pltpu.PrefetchScalarGridSpec(
            num_scalar_prefetch=1,
            grid=(2,),
            in_specs=[
                pl.BlockSpec((width, rows), lambda p, m: (0, m[0] ^ (6 * p))),
                pl.BlockSpec((rows, width), lambda p, m: (m[0] ^ (6 * p), 0)),
            ],
            out_specs=pl.BlockSpec((1, 2 * rows, width), lambda p, m: (p, 0, 0)),
        ),
        cost_estimate=BRIEF,
        compiler_params=params(12),
        name="hidden_pieces",
    )(member, up_weight, down_weight)


def gather_kernel(plan, *refs):
    count = sum(len(places) for places in plan)
    sources, outs, sems = list(refs[:count]), refs[count : count + len(plan)], refs[-1]
    copies = []
    for places, out_ref in zip(plan, outs):
        to = 0
        for start, rows in places:
            ref = sources.pop(0)
            for at in range(0, rows, CUT):
                source, target = ref.at[pl.ds(start + at, CUT)], out_ref.at[pl.ds(to + at, CUT)]
                copies.append(pltpu.make_async_copy(source, target, sems.at[len(copies)]))
            to += rows
    for copy in copies:
        copy.start()
    for copy in copies:
        copy.wait()


def gather_rows(plan, *arrays):
    sizes = [sum(rows for _, rows in places) for places in plan]
    return pl.pallas_call(
        functools.partial(gather_kernel, plan),
        in_specs=[pl.BlockSpec(memory_space=pl.ANY)] * len(arrays),
        out_specs=[pl.BlockSpec(memory_space=pltpu.VMEM)] * len(plan),
        out_shape=[shape_of((size, arrays[0].shape[1]), F32) for size in sizes],
        scratch_shapes=[pltpu.SemaphoreType.DMA((sum(sizes) // CUT,))],
        cost_estimate=BRIEF,
        compiler_params=params(8),
        name="gather_rows",
    )(*arrays)


def reorder(values, member, dim=1):
    block = values.shape[dim] // 8
    place = lax.broadcasted_iota(jnp.int32, values.shape, dim) // block
    for bit in (1, 2, 4):
        up = pltpu.roll(values, block * bit, dim)
        down = pltpu.roll(values, values.shape[dim] - block * bit, dim)
        turned = jnp.where((place & bit) != 0, up, down)
        values = jnp.where((member & bit) != 0, turned, values)
    return values


def column_of(seg_row):
    wide = jnp.broadcast_to(seg_row.astype(F32), (128, seg_row.shape[1]))
    return wide.T[:, 0:1].astype(jnp.int32)


def extras(member, small_ref, others):
    small = small_ref[0:40, :]
    if others:
        small = reorder(small, member)
    return small[0:PAD].astype(BF16), small[PAD : 2 * PAD].astype(BF16), small[2 * PAD : 2 * PAD + 8]


def blocks_of(length):
    out = []
    for i in range(length // QB):
        first = max(0, (i * QB - length // 2 + 1) // QB) * QB
        last = (i + 1) * QB
        if first > 0 and last < length:
            first = 0
        out.append((i, first, last, (0, PAD + last) if first == 0 else (PAD + first, length + 2 * PAD)))
    return out


def strip_parts(block):
    _, first, last, (low, _) = block
    n = last - first
    return ((0, PAD), (PAD, PAD + n)) if low == 0 else ((n, n + PAD), (0, n))


def fill_prefix_mask(mask_ref, length, prefix_count):
    live = lax.broadcasted_iota(jnp.int32, (PAD, QB), 0) < prefix_count
    edge = jnp.where(live, 0.0, NEGATIVE)
    mask_ref[0:PAD, :] = edge
    mask_ref[PAD + length :, :] = edge


def fill_mask(mask_ref, seg_col, seg_row, block):
    i, first, last, _ = block
    keys = lax.broadcasted_iota(jnp.int32, (last - first, QB), 0) + first
    asks = lax.broadcasted_iota(jnp.int32, (last - first, QB), 1) + i * QB
    allowed = (seg_col[first:last] == seg_row[:, i * QB : last]) & (keys <= asks)
    mask_ref[PAD + first : PAD + last, :] = jnp.where(allowed, 0.0, NEGATIVE)


def fill_extended(ext_ref, prefix, values):
    length = values.shape[0]
    ext_ref[0:PAD, :] = prefix
    ext_ref[PAD : PAD + length, :] = values
    ext_ref[PAD + length :, :] = prefix


def head_lanes():
    return lax.broadcasted_iota(jnp.int32, (QB, WIDE), 1) // HD


def attend_scratch(length):
    return [
        pltpu.VMEM((length + 2 * PAD, QB), F32),
        pltpu.VMEM((length + 2 * PAD, WIDE), BF16),
        pltpu.VMEM((WIDE, length), BF16),
        pltpu.VMEM((2, length + PAD, QB), F32),
        pltpu.VMEM((GROUP, length), F32),
        pltpu.VMEM((GROUP, length), F32),
    ]


def attend_body(prefix_count, x_ref, w_ref, extra, segr_ref, q_ref, k_ref, v_ref, att_ref, lse_ref,
                mask_ref, ke_ref, vt_ref, s_ref, top_ref, sum_ref):
    length = x_ref.shape[0]
    pk, pv, bias = extra
    x = x_ref[...]
    q_ref[...] = ((dot(x, w_ref[0], NT) + bias[0:1]) * HD ** (-0.5)).astype(BF16)
    k = (dot(x, w_ref[1], NT) + bias[1:2]).astype(BF16)
    k_ref[...] = k
    fill_extended(ke_ref, pk, k)
    v = (dot(x, w_ref[2], NT) + bias[2:3]).astype(BF16)
    v_ref[...] = v
    vt_ref[...] = v.T
    pvt = pv.T
    seg_row = segr_ref[...]
    seg_col = column_of(seg_row)
    fill_prefix_mask(mask_ref, length, prefix_count)
    heads, zero = head_lanes(), jnp.zeros((), BF16)
    work = [(block, h) for block in blocks_of(length) for h in range(GROUP)]

    def ask(n):
        block, h = work[n]
        i, _, last, (low, high) = block
        if h == 0:
            fill_mask(mask_ref, seg_col, seg_row, block)
        asked = jnp.where(heads == h, q_ref[i * QB : last, :], zero)
        s_ref[n % 2, 0 : high - low, :] = dot(ke_ref[low:high, :], asked, NT) + mask_ref[low:high, :]

    ask(0)
    for n, (block, h) in enumerate(work):
        if n + 1 < len(work):
            ask(n + 1)
        i, first, last, (low, high) = block
        rows, span = slice(i * QB, last), slice(h * HD, (h + 1) * HD)
        (pa, pb), (ta, tb) = strip_parts(block)
        s = s_ref[n % 2, 0 : high - low, :]
        top = jnp.max(s, axis=0, keepdims=True)
        e = jnp.exp(s - top)
        total = jnp.sum(e, axis=0, keepdims=True)
        top_ref[h : h + 1, rows] = top
        sum_ref[h : h + 1, rows] = total
        e = e.astype(BF16)
        o = dot(vt_ref[span, first:last], e[ta:tb]) + dot(pvt[span, :], e[pa:pb])
        att_ref[span, rows] = (o * (1.0 / total)).astype(BF16)
    lse_ref[...] = top_ref[...] + jnp.log(sum_ref[...])


def attend_own_kernel(prefix_count, member_ref, tok_ref, gain_ref, shift_ref, w_ref, small_ref, segr_ref, bias_ref,
                      x_ref, q_ref, k_ref, v_ref, att_ref, lse_ref, out_ref, *scratch):
    length = tok_ref.shape[0]
    for t in range(0, length, TB):
        normed, _ = normalize(tok_ref[t : t + TB, :].astype(F32))
        x_ref[t : t + TB, :] = (normed * gain_ref[...] + shift_ref[...]).astype(BF16)
    attend_body(prefix_count, x_ref, w_ref, extras(member_ref[0], small_ref, False), segr_ref,
                q_ref, k_ref, v_ref, att_ref, lse_ref, *scratch)
    for t in range(0, length, TB):
        base = tok_ref[t : t + TB, :].astype(F32) + bias_ref[...]
        out_ref[t : t + TB, :] = base + dot(att_ref[:, t : t + TB], w_ref[3], TN)


def attend_others_kernel(prefix_count, carried, member_ref, x_ref, *refs):
    pieces, (small_ref, segr_ref, acc_ref) = refs[:8], refs[8:11]
    refs = refs[11 + carried :]
    w_ref, q_ref, k_ref, v_ref, att_ref, lse_ref, out_ref = refs[:7]
    half = HD // 2
    for j, ref in enumerate(pieces):
        for c in range(4):
            w_ref[c, j * half : (j + 1) * half, :] = ref[c * half : (c + 1) * half, :].astype(BF16)
    attend_body(prefix_count, x_ref, w_ref, extras(member_ref[0], small_ref, True), segr_ref,
                q_ref, k_ref, v_ref, att_ref, lse_ref, *refs[7:])

    @pl.when(pl.program_id(0) == 0)
    def _():
        out_ref[...] = acc_ref[...]

    for t in range(0, x_ref.shape[0], TB):
        out_ref[t : t + TB, :] += dot(att_ref[:, t : t + TB], w_ref[3], TN)


def attend_own(prefix_count, *args):
    length, width = args[1].shape
    return resident(
        functools.partial(attend_own_kernel, prefix_count),
        [shape_of((length, width), BF16)]
        + [shape_of((length, WIDE), BF16)] * 3
        + [shape_of((WIDE, length), BF16), shape_of((GROUP, length), F32), shape_of((length, width), F32)],
        attend_scratch(length),
        "attend_own",
        22,
        args,
    )


SCALARS = pl.BlockSpec(memory_space=pltpu.SMEM)


def once(values):
    return pl.BlockSpec(values.shape, lambda g: (0,) * len(values.shape), pipeline_mode=pl.Buffered(1))


def each(*block):
    return pl.BlockSpec((None,) + block, lambda g: (g,) + (0,) * len(block))


def rows_of(count, width):
    return pl.BlockSpec((count, width), lambda g: (g, 0))


def attend_others(prefix_count, first, count, total, member, x, pieces, small, seg, acc, carry=()):
    length, width = x.shape
    saved = [(4, WIDE, width), (length, WIDE), (length, WIDE), (length, WIDE), (WIDE, length), (GROUP, length)]
    piece = lambda at: pl.BlockSpec((128, width), lambda g: (g + at, 0))
    part = lambda block: pl.BlockSpec((None,) + block, lambda g: (g + first,) + (0,) * len(block))
    return pl.pallas_call(
        functools.partial(attend_others_kernel, prefix_count, len(carry)),
        grid=(count,),
        in_specs=[SCALARS, once(x)]
        + [piece(at) for _, at in pieces]
        + [pl.BlockSpec((48, WIDE), lambda g: (g + first, 0)), once(seg), once(acc)]
        + [pl.BlockSpec(memory_space=pl.ANY)] * len(carry),
        out_specs=[part(block) for block in saved] + [pl.BlockSpec((length, width), lambda g: (0, 0))],
        out_shape=[shape_of((total,) + block, BF16) for block in saved[:-1]]
        + [shape_of((total, GROUP, length), F32), shape_of((length, width), F32)],
        scratch_shapes=attend_scratch(length),
        input_output_aliases={13 + n: n for n in range(len(carry))},
        cost_estimate=BRIEF,
        compiler_params=params(50),
        name="attend_others",
    )(member, x, *[values for values, _ in pieces], small, seg, acc, *carry)


def back_scratch(length):
    low = lambda *shape: pltpu.VMEM(shape, BF16)
    return [
        pltpu.VMEM((length + 2 * PAD, QB), F32),
        low(length + 2 * PAD, WIDE),
        low(length + 2 * PAD, WIDE),
        low(WIDE, length),
        low(WIDE, length),
        low(WIDE, length),
        low(length, WIDE),
        pltpu.VMEM((2, length + PAD, QB), F32),
        pltpu.VMEM((2, length + PAD, QB), F32),
        pltpu.VMEM((GROUP, length), F32),
        pltpu.VMEM((2, WIDE, length), F32),
    ]


def back_body(prefix_count, extra, w_ref, q_ref, k_ref, v_ref, att_ref, lse_ref, segr_ref, low_ref, gjt_ref, gp_ref,
              mask_ref, ke_ref, ve_ref, kt_ref, qt_ref, dot_ref, do_ref, s_ref, dp_ref, delta_ref, acc_ref):
    length = q_ref.shape[0]
    pk, pv, _ = extra
    do = dot(low_ref[...], w_ref[3], NT).astype(BF16)
    do_ref[...] = do
    dot_ref[...] = do.T
    kt_ref[...] = k_ref[...].T
    qt_ref[...] = q_ref[...].T
    fill_extended(ke_ref, pk, k_ref[...])
    fill_extended(ve_ref, pv, v_ref[...])
    pkt = pk.T
    for h in range(GROUP):
        span = slice(h * HD, (h + 1) * HD)
        products = dot_ref[span, :].astype(F32) * att_ref[span, :].astype(F32)
        delta_ref[h : h + 1, :] = jnp.sum(products, axis=0, keepdims=True)
    seg_row = segr_ref[...]
    seg_col = column_of(seg_row)
    fill_prefix_mask(mask_ref, length, prefix_count)
    acc_ref[...] = jnp.zeros_like(acc_ref)
    if gp_ref is not None:
        gp_ref[...] = jnp.zeros_like(gp_ref)
    heads, zero = head_lanes(), jnp.zeros((), BF16)
    work = [(block, h) for block in blocks_of(length) for h in range(GROUP)]

    def ask(n):
        block, h = work[n]
        i, _, last, (low, high) = block
        if h == 0:
            fill_mask(mask_ref, seg_col, seg_row, block)
        rows = slice(i * QB, last)
        asked = jnp.where(heads == h, q_ref[rows, :], zero)
        grad = jnp.where(heads == h, do_ref[rows, :], zero)
        s_ref[n % 2, 0 : high - low, :] = dot(ke_ref[low:high, :], asked, NT) + mask_ref[low:high, :]
        dp_ref[n % 2, 0 : high - low, :] = dot(ve_ref[low:high, :], grad, NT)

    ask(0)
    for n, (block, h) in enumerate(work):
        if n + 1 < len(work):
            ask(n + 1)
        i, first, last, (low, high) = block
        rows, span = slice(i * QB, last), slice(h * HD, (h + 1) * HD)
        (pa, pb), (ta, tb) = strip_parts(block)
        p = jnp.exp(s_ref[n % 2, 0 : high - low, :] - lse_ref[h : h + 1, rows])
        ds = (p * (dp_ref[n % 2, 0 : high - low, :] - delta_ref[h : h + 1, rows])).astype(BF16)
        p = p.astype(BF16)
        dq = dot(kt_ref[span, first:last], ds[ta:tb]) + dot(pkt[span, :], ds[pa:pb])
        gjt_ref[span, rows] = dq.astype(BF16) * jnp.asarray(HD ** (-0.5), BF16)
        acc_ref[0, span, first:last] += dot(qt_ref[span, rows], ds[ta:tb], NT)
        acc_ref[1, span, first:last] += dot(dot_ref[span, rows], p[ta:tb], NT)
        if gp_ref is not None:
            gp_ref[0, span, :] += dot(qt_ref[span, rows], ds[pa:pb], NT)
            gp_ref[1, span, :] += dot(dot_ref[span, rows], p[pa:pb], NT)
    gjt_ref[WIDE : 2 * WIDE, :] = acc_ref[0].astype(BF16)
    gjt_ref[2 * WIDE : 3 * WIDE, :] = acc_ref[1].astype(BF16)


def take_own(out_ref, rows, values, index):
    width = out_ref.shape[1]
    for k in range(values.shape[1] // width):

        @pl.when(index == k)
        def _():
            out_ref[rows, :] = values[:, k * width : (k + 1) * width].astype(out_ref.dtype)


def norm_back(grad, normed, inverse, gain):
    scaled = grad * gain
    mean = jnp.mean(scaled, axis=-1, keepdims=True)
    return inverse * (scaled - mean - normed * jnp.mean(scaled * normed, axis=-1, keepdims=True))


def pack_sums(prefix_count, z, gp_ref, sums_ref, gjt_ref, ups_ref, outer_ref, pack_ref):
    pack_ref[...] = jnp.zeros_like(pack_ref)
    inner = 0.0
    for k in range(2):
        gp = gp_ref[k].T
        pack_ref[k * PAD : (k + 1) * PAD, :] = gp
        for _ in range(3):
            part = gp.astype(BF16)
            inner = inner + dot(part, outer_ref[:, k * WIDE : (k + 1) * WIDE], NT)
            gp = gp - part.astype(F32)
    for n in range(4):
        take_own(pack_ref, slice(2 * PAD + n, 2 * PAD + n + 1), sums_ref[n : n + 1, :], z)
    joint = dot(jnp.ones((8, gjt_ref.shape[1]), BF16), gjt_ref[...], NT)
    for k in range(3):
        pack_ref[2 * PAD + 4 + k : 2 * PAD + 5 + k, :] = joint[0:1, k * WIDE : (k + 1) * WIDE]
    for k in range(ups_ref.shape[1] // WIDE):
        pack_ref[2 * PAD + 8 + k : 2 * PAD + 9 + k, :] = ups_ref[:, k * WIDE : (k + 1) * WIDE]
    begin = 2 * PAD + 8 + ups_ref.shape[1] // WIDE
    for k in range(inner.shape[1] // WIDE):
        to = slice(begin + k * prefix_count, begin + (k + 1) * prefix_count)
        pack_ref[to, :] = inner[0:prefix_count, k * WIDE : (k + 1) * WIDE]


def back_own_kernel(prefix_count, places_ref, w_ref, q_ref, k_ref, v_ref, att_ref, lse_ref, small_ref, segr_ref,
                    low_ref, sums_ref, ups_ref, outer_ref, gjt_ref, pack_ref, ga_ref, gp_ref, *scratch):
    back_body(prefix_count, extras(places_ref[1], small_ref, False), w_ref, q_ref, k_ref, v_ref, att_ref, lse_ref,
              segr_ref, low_ref, gjt_ref, gp_ref, *scratch)
    w = w_ref[0:3].reshape(3 * WIDE, w_ref.shape[2])
    for t in range(0, low_ref.shape[0], TB):
        ga_ref[t : t + TB, :] = dot(gjt_ref[:, t : t + TB], w, TN)
    pack_sums(prefix_count, places_ref[0], gp_ref, sums_ref, gjt_ref, ups_ref, outer_ref, pack_ref)


def back_others_kernel(prefix_count, places_ref, w_ref, q_ref, k_ref, v_ref, att_ref, lse_ref, small_ref, segr_ref,
                       low_ref, gain_ref, from_ga, from_tok, from_part, out_ref, sums_ref, ga_ref, tok_ref, part_ref, sems, gjt_ref,
                       *scratch):
    length, step = low_ref.shape[0], pl.program_id(0)
    final = pl.num_programs(0) - 1
    pairs = ((from_ga, ga_ref), (from_tok, tok_ref), (from_part, part_ref))
    copies = [pltpu.make_async_copy(source, target, sems.at[n]) for n, (source, target) in enumerate(pairs)]

    @pl.when(step == 0)
    def _():
        for copy in copies:
            copy.start()

    back_body(prefix_count, extras(places_ref[1], small_ref, True), w_ref, q_ref, k_ref, v_ref, att_ref, lse_ref,
              segr_ref, low_ref, gjt_ref, None, *scratch)
    w = w_ref[0:3].reshape(3 * WIDE, w_ref.shape[2])

    @pl.when(step == 0)
    def _():
        for copy in copies:
            copy.wait()

    @pl.when(step < final)
    def _():
        for t in range(0, length, TB):
            ga_ref[t : t + TB, :] += dot(gjt_ref[:, t : t + TB], w, TN)

    @pl.when(step == final)
    def _():
        sums = [0.0, 0.0]
        for t in range(0, length, TB):
            rows = slice(t, t + TB)
            ga = ga_ref[rows, :] + dot(gjt_ref[:, rows], w, TN)
            normed, inverse = normalize(tok_ref[rows, :].astype(F32))
            grad = norm_back(ga, normed, inverse, gain_ref[...])
            width = out_ref.shape[1]
            for k in range(grad.shape[1] // width):

                @pl.when(places_ref[0] == k)
                def _():
                    out_ref[rows, :] = (part_ref[rows, :] + grad[:, k * width : (k + 1) * width]).astype(BF16)

            sums[0] = sums[0] + jnp.sum(ga * normed, axis=0, keepdims=True)
            sums[1] = sums[1] + jnp.sum(ga, axis=0, keepdims=True)
        sums_ref[...] = jnp.zeros_like(sums_ref)
        for n in range(2):
            take_own(sums_ref, slice(n, n + 1), sums[n], places_ref[0])


def back_own(prefix_count, *args):
    length, width = args[9].shape
    ups, outer = args[-2:]
    packed = 2 * PAD + 8 + ups.shape[1] // WIDE + outer.shape[0] // WIDE * prefix_count
    return resident(
        functools.partial(back_own_kernel, prefix_count),
        [
            shape_of((3 * WIDE, length), BF16),
            shape_of((-(-packed // 8) * 8, WIDE), F32),
            shape_of((length, width), F32),
        ],
        [pltpu.VMEM((2, WIDE, PAD), F32)] + back_scratch(length),
        "back_own",
        30,
        args,
    )


def back_others(prefix_count, places, saved, small, seg, low, ga, tokens, part, gain):
    length, width = low.shape
    return pl.pallas_call(
        functools.partial(back_others_kernel, prefix_count),
        grid=(saved[0].shape[0],),
        in_specs=[SCALARS]
        + [each(*values.shape[1:]) for values in saved]
        + [rows_of(48, WIDE)]
        + [once(values) for values in (seg, low, gain)]
        + [pl.BlockSpec(memory_space=pl.ANY)] * 3,
        out_specs=[pl.BlockSpec((length, WIDE), lambda g: (0, 0)), pl.BlockSpec((8, WIDE), lambda g: (0, 0))],
        out_shape=[shape_of((length, WIDE), BF16), shape_of((8, WIDE), F32)],
        scratch_shapes=[
            pltpu.VMEM((length, width), F32),
            pltpu.VMEM((length, width), BF16),
            pltpu.VMEM((length, WIDE), F32),
            pltpu.SemaphoreType.DMA((3,)),
            pltpu.VMEM((3 * WIDE, length), BF16),
        ]
        + back_scratch(length),
        cost_estimate=BRIEF,
        compiler_params=params(50),
        name="back_others",
    )(places, *saved, small, seg, low, gain, ga, tokens, part)


def gelu_pair(v):
    c = 0.7978845608028654
    square = v * v
    t = jnp.tanh(v * (c + (0.044715 * c) * square))
    half = 0.5 + 0.5 * t
    return v * half, half + (0.5 * v) * (1.0 - t * t) * (c + (3.0 * 0.044715 * c) * square)


def mix_rows(mid, cot, up_ref, up_dims, bias, down_ref, act_ref, gp_ref, rows, pre_ref, g_ref):
    hidden = down_ref.shape[0]
    chunks = [slice(c, c + TB) for c in range(0, hidden, TB)]

    def ask(n):
        up = up_ref[:, chunks[n]] if up_dims is NN else up_ref[chunks[n], :]
        pre_ref[n % 2] = dot(mid, up, up_dims) + bias[:, chunks[n]]
        g_ref[n % 2] = dot(cot, down_ref[chunks[n], :], NT)

    ask(0)
    for n, chunk in enumerate(chunks):
        if n + 1 < len(chunks):
            ask(n + 1)
        act, slope = gelu_pair(pre_ref[n % 2])
        act_ref[rows, chunk] = act.astype(BF16)
        gp_ref[rows, chunk] = (g_ref[n % 2] * slope).astype(BF16)


def mix_own_kernel(z_ref, res_ref, cot_ref, gain_ref, shift_ref, up_ref, bias_ref, down_ref, dbias_ref,
                   mid_ref, act_ref, gp_ref, share_ref, bsum_ref, gm_ref, pre_ref, g_ref):
    width = share_ref.shape[1]
    own = pl.ds(pl.multiple_of(z_ref[0] * width, width), width)
    every = slice(0, TB)
    normed, _ = normalize(res_ref[...])
    mid = (normed * gain_ref[...] + shift_ref[...]).astype(BF16)
    mid_ref[...] = mid
    mix_rows(mid, cot_ref[...], up_ref, NN, bias_ref[...], down_ref, act_ref, gp_ref, every, pre_ref, g_ref)
    share_ref[...] = res_ref[:, own] + dbias_ref[:, own] + dot(act_ref[...], down_ref[:, own])
    gp = gp_ref[...]
    gm_ref[...] = dot(gp, up_ref[...], NT)

    @pl.when(pl.program_id(0) == 0)
    def _():
        bsum_ref[...] = jnp.zeros_like(bsum_ref)

    bsum_ref[...] += jnp.sum(gp.astype(F32), axis=0, keepdims=True)


def mix_own(own_width, z, residual, cotangent, gain, shift, up, up_bias, down, down_bias):
    length, width = residual.shape
    hidden = up.shape[1]
    rows = lambda w: rows_of(TB, w)
    fixed = [once(values) for values in (gain, shift, up, up_bias, down, down_bias)]
    return pl.pallas_call(
        mix_own_kernel,
        grid=(length // TB,),
        in_specs=[SCALARS, rows(width), rows(width)] + fixed,
        out_specs=[rows(width), rows(hidden), rows(hidden), rows(own_width), pl.BlockSpec((1, hidden), lambda t: (0, 0)), rows(width)],
        out_shape=[
            shape_of((length, width), BF16),
            shape_of((length, hidden), BF16),
            shape_of((length, hidden), BF16),
            shape_of((length, own_width), F32),
            shape_of((1, hidden), F32),
            shape_of((length, width), F32),
        ],
        scratch_shapes=[pltpu.VMEM((2, TB, TB), F32)] * 2,
        cost_estimate=BRIEF,
        compiler_params=params(36),
        name="mix_own",
    )(z, residual, cotangent, gain, shift, up, up_bias, down, down_bias)


def mix_kernel(places, last, z_ref, mid_ref, cot_ref, small_ref, share_in, gm_in, *refs):
    pieces, per = len(places), 128
    if last:
        res_ref, gain_ref, *refs = refs
    sources, refs = refs[: 2 * pieces], refs[2 * pieces :]
    if last:
        share_ref, low_ref, own_ref, sums_ref, *refs = refs
    else:
        share_ref, gm_ref, *refs = refs
    up_ref, down_ref, part_ref, act_ref, gp_ref, pre_ref, g_ref = refs
    step = pl.program_id(0)
    width = share_ref.shape[1]
    own = pl.ds(pl.multiple_of(z_ref[0] * width, width), width)
    @pl.when(step == 0)
    def _():
        for j in range(pieces):
            up_ref[j * per : (j + 1) * per, :] = sources[2 * j][...].astype(BF16)
            down_ref[j * per : (j + 1) * per, :] = sources[2 * j + 1][...].astype(BF16)
        part_ref[...] = down_ref[:, own]
        if last:
            sums_ref[...] = jnp.zeros_like(sums_ref)

    def block():
        biases = {k: reorder(small_ref[48 * k + 40 : 48 * k + 48, 0:per], z_ref[1], 0) for k, _ in places}
        bias = jnp.concatenate([biases[k][j : j + 1] for k, j in places], axis=1)
        mix_rows(mid_ref[...], cot_ref[...], up_ref, NT, bias, down_ref, act_ref, gp_ref, slice(0, TB), pre_ref, g_ref)
        share_ref[...] = (share_in[...] + dot(act_ref[...], part_ref[...])).astype(share_ref.dtype)
        gm = gm_in[...] + dot(gp_ref[...], up_ref[...])
        if not last:
            gm_ref[...] = gm
            return
        normed, inverse = normalize(res_ref[...])
        cot = cot_ref[...].astype(F32)
        grad = cot + norm_back(gm, normed, inverse, gain_ref[...])
        low_ref[...] = grad.astype(BF16)
        take_own(own_ref, slice(0, TB), grad, z_ref[0])
        for n, values in enumerate((gm * normed, gm, grad, cot)):
            sums_ref[n : n + 1, :] += jnp.sum(values, axis=0, keepdims=True)

    block()


def mix(places, blocks, last, z, mid, cotangent, small, share, gm, *arrays):
    length, width = mid.shape
    hidden = 128 * len(places)
    own_width = share.shape[1]
    rows = lambda w: rows_of(TB, w)
    low = lambda *shape: pltpu.VMEM(shape, BF16)
    piece = lambda at: pl.BlockSpec((128, width), lambda t: (at, 0), pipeline_mode=pl.Buffered(1))
    outs = [(rows(own_width), shape_of((length, own_width), BF16 if last else F32))]
    if last:
        outs += [(rows(width), shape_of((length, width), BF16)), (rows(own_width), shape_of((length, own_width), F32))]
        outs += [(pl.BlockSpec((8, width), lambda t: (0, 0)), shape_of((8, width), F32))]
    else:
        outs += [(rows(width), shape_of((length, width), F32))]
    return pl.pallas_call(
        functools.partial(mix_kernel, places, last),
        grid=(length // TB,),
        in_specs=[SCALARS, rows(width), rows(width), once(small), rows(own_width), rows(width)]
        + ([rows(width), once(arrays[1])] if last else [])
        + [piece(at) for at in blocks],
        out_specs=[spec for spec, _ in outs],
        out_shape=[shape for _, shape in outs],
        scratch_shapes=[
            low(hidden, width),
            low(hidden, width),
            low(hidden, own_width),
            low(TB, hidden),
            low(TB, hidden),
        ]
        + [pltpu.VMEM((2, TB, TB), F32)] * 2,
        input_output_aliases={} if last else {4: 0, 5: 1},
        cost_estimate=BRIEF,
        compiler_params=params(40),
        name="mix_others",
    )(z, mid, cotangent, small, share, gm, *arrays)


def hidden_grad_kernel(mid_ref, cot_ref, gp_ref, act_ref, out_ref):
    parts, per = out_ref.shape[0], out_ref.shape[1] // 2
    for at, left, right in ((0, mid_ref, gp_ref), (per, cot_ref, act_ref)):
        grad = dot(left[...], right[...], TN)
        for a in range(parts):
            out_ref[a, at : at + per, :] = grad[a * per : (a + 1) * per]


def hidden_grad(parts, mid, cotangent, gp, act):
    length, width = mid.shape
    hidden = gp.shape[1]
    per = width // parts
    column = pl.BlockSpec((length, TB), lambda j: (0, j))
    return pl.pallas_call(
        hidden_grad_kernel,
        grid=(width // TB,),
        in_specs=[column, column, once(gp), once(act)],
        out_specs=pl.BlockSpec((TB // per, 2 * per, hidden), lambda j: (j, 0, 0)),
        out_shape=shape_of((parts, 2 * per, hidden), F32),
        cost_estimate=BRIEF,
        compiler_params=params(30),
        name="hidden_grad",
    )(mid, cotangent, gp, act)


def head_grad_kernel(places_ref, x_ref, low_ref, gjt_ref, att_ref, keep_ref, send_ref):
    wide, core, chip = gjt_ref.shape[0], places_ref[1] & 1, places_ref[1] >> 1
    for start, left, right in ((0, gjt_ref, x_ref), (wide, att_ref, low_ref)):
        for r in range(0, left.shape[0], TB):
            grad = dot(left[r : r + TB, :], right[...])
            for mine in range(2):

                @pl.when(core == mine)
                def _():
                    for j in range(8):
                        out_ref = keep_ref if j % 2 == mine else send_ref
                        out_ref[(j // 2) ^ chip, start + r : start + r + TB, :] = grad[:, 128 * j : 128 * (j + 1)]


def head_grad(*args):
    rows = args[3].shape[0] + args[4].shape[0]
    return resident(head_grad_kernel, [shape_of((4, rows, 128), F32)] * 2, [], "head_grad", 16, args)


def fold_kernel(places_ref, keep_ref, got_ref, far_x_ref, far_y_ref, stay_ref, near_ref):
    half = keep_ref.shape[1] // 2
    total = lambda s, rows: keep_ref[s, rows, :] + got_ref[s, rows, :]
    top, bottom = slice(0, half), slice(half, 2 * half)
    near_ref[...] = keep_ref[0] + got_ref[0]
    far_x_ref[0], far_x_ref[1] = total(1, top), total(3, top)
    far_y_ref[0], far_y_ref[1] = total(2, bottom), total(3, bottom)
    stay_ref[0], stay_ref[1] = total(2, top), total(1, bottom)


def fold(*args):
    _, rows, lanes = args[1].shape
    half = shape_of((2, rows // 2, lanes), F32)
    return resident(fold_kernel, [half, half, half, shape_of((rows, lanes), F32)], [], "fold", 12, args)


def shards(
    tokens, segment_ids, attention_gain, attention_shift, joint_weight, joint_bias, output_weight, output_bias,
    mixer_gain, mixer_shift, up_weight, up_bias, down_weight, down_bias, prefix_table, inner_weight, inner_bias,
    outer_weight, outer_bias, cotangent,
):
    length, width = tokens.shape
    local = joint_weight.shape[2]
    hidden = up_weight.shape[1]
    prefix_count = prefix_table.shape[0]
    batch_size, tensor_size = lax.axis_size("batch"), lax.axis_size("tensor")
    z = lax.axis_index("tensor").astype(jnp.int32)
    member = (lax.axis_index("batch") % 8).astype(jnp.int32)
    member_arr, places = member.reshape(1), jnp.stack([z, member])

    def own_columns(values):
        return lax.dynamic_slice_in_dim(values, z * local, local, values.ndim - 1)

    def along(values, k):
        return lax.ppermute(values, "tensor", [(i, i ^ k) for i in range(tensor_size)])

    def across(values, k):
        return lax.ppermute(values, "batch", [(i, i ^ k) for i in range(batch_size)])

    now = [member_arr]

    def after(values):
        return lax.optimization_barrier((values, *now))[0]

    def wait(*values):
        held = lax.optimization_barrier((*values, *now))
        now[:] = [held[0]]
        return held[0] if len(values) == 1 else held[: len(values)]

    def run(call, *args):
        outs = call(after(args[0]), *args[1:])
        now[:] = [outs[-1] if isinstance(outs, (list, tuple)) else outs]
        return outs

    row = lambda v: v.reshape(1, -1)
    stack = lambda *parts: jnp.concatenate(parts, axis=0)

    def gather(*lists):
        plan = [[(start, rows) for _, start, rows in parts] for parts in lists]
        arrays = [values for parts in lists for values, _, _ in parts]
        outs = run(lambda *arrays: gather_rows(plan, *arrays), *arrays)
        return outs[0] if len(outs) == 1 else outs

    def rows(values, block, count=1):
        return values, block * 128, count * 128

    whole = lambda values: (values, 0, values.shape[0])

    own_heads, send_heads = run(head_pieces, member_arr, joint_weight, output_weight)
    a1, a2 = along(after(send_heads[0]), 1), along(after(send_heads[0]), 2)

    def prefixes(prefix_table, inner_weight):
        hidden_prefix = jnp.tanh(jnp.dot(prefix_table, inner_weight.astype(F32), precision=PRECISE) + inner_bias)
        pairs = jnp.einsum("pr,rke->kpe", hidden_prefix, outer_weight.astype(F32), precision=PRECISE)
        pairs = jnp.pad(pairs + outer_bias[:, None, :], ((0, 0), (0, PAD - prefix_count), (0, 0)))
        ups = jnp.pad(up_bias.reshape(8, hidden // 8), ((0, 0), (0, local - hidden // 8)))
        joints = jnp.pad(joint_bias, ((0, 5), (0, 0)))
        return hidden_prefix, stack(pairs.reshape(2 * PAD, local), joints, ups)

    hidden_prefix, small = run(prefixes, prefix_table, inner_weight)
    send_hidden = run(hidden_pieces, member_arr, up_weight, down_weight)
    smalls = [along(after(small), k) for k in (1, 2, 3)]
    a1, a2, *smalls = wait(a1, a2, *smalls)
    a12 = gather([whole(a1), whole(a2)])
    x12, y12 = across(after(a12), 2), across(after(a12), 4)
    a3, a1d = along(after(send_heads[0]), 3), along(after(send_heads[1]), 1)
    c12 = across(after(a12), 1)
    x, *saved_own, residual = run(
        functools.partial(attend_own, prefix_count),
        member_arr, tokens, row(attention_gain), row(attention_shift), own_heads, small, segment_ids, row(output_bias),
    )
    extra = stack(*smalls)
    x12, y12, a3, a1d, c12 = wait(x12, y12, a3, a1d, c12)

    y3 = gather([whole(a3), rows(x12, 1)])
    x3, y3 = across(after(a3), 2), across(after(y3), 4)
    f1, f2 = along(after(send_hidden[0]), 1), along(after(send_hidden[0]), 2)
    gb = gather([whole(x12), whole(y12), whole(a3), whole(a1d)])
    cb = across(after(gb), 1)
    x3, y3, cb = wait(x3, y3, cb)
    a2d = run(lambda values: values[128:256], y3)
    ca2d = across(after(a2d), 1)
    a3d = across(after(y3[0:128]), 2)
    d12 = gather([whole(a1d), whole(a2d)])
    ca2d = wait(ca2d)
    cd12 = gather([rows(cb, 5), whole(ca2d)])
    *saved_others, residual = run(
        functools.partial(attend_others, prefix_count, 0, 2, 3),
        member_arr, x, [(a12, 0), (c12, 0), (x12, 0), (cb, 0), (y12, 0), (cb, 2), (d12, 0), (cd12, 0)], extra,
        segment_ids, residual,
    )
    a3d, f1, f2 = wait(a3d, f1, f2)

    f12, gc = gather([whole(f1), whole(f2)], [whole(x3), rows(y3, 0), whole(a3d), whole(f1), whole(f2)])
    fx, fy = across(after(f12), 2), across(after(f12), 4)
    f3, f1d = along(after(send_hidden[0]), 3), along(after(send_hidden[1]), 1)
    cc = wait(across(after(gc), 1))
    *saved_others, residual = run(
        functools.partial(attend_others, prefix_count, 2, 1, 3),
        member_arr, x, [(a3, 0), (cb, 4), (x3, 0), (cc, 0), (y3, 0), (cc, 1), (a3d, 0), (cc, 2)], extra,
        segment_ids, residual, saved_others,
    )
    mid, act, gp, share, up_bias_sum, gm = run(
        functools.partial(mix_own, local),
        places, residual, cotangent, row(mixer_gain), row(mixer_shift), up_weight, row(up_bias), down_weight,
        row(down_bias),
    )
    hidden_part = run(functools.partial(hidden_grad, batch_size), mid, cotangent, gp, act)
    fx, fy, f3, f1d = wait(fx, fy, f3, f1d)

    x4, y4 = gather([whole(f3), rows(fy, 3)], [whole(f3), rows(fx, 2)])
    x4, y4 = across(after(x4), 2), across(after(y4), 4)
    cfx, cfy, cf1d = [across(after(values), 1) for values in (fx, fy, f1d)]
    cfx, cfy, cf1d = wait(cfx, cfy, cf1d)

    def mix_more(pieces, share, gm, last=False):
        order = [(slot, j) for slot, j, _, _ in pieces]
        flat = [part for _, _, up, down in pieces for part in (up, down)]
        return run(
            functools.partial(mix, order, [at for _, at in flat], last),
            places, mid, cotangent, extra, share, gm, *([residual, row(mixer_gain)] if last else []),
            *[values for values, _ in flat],
        )

    def pair(values, at):
        return (values, at), (values, at + 1)

    def both(slot, number, mine, theirs):
        return [(slot, number, *pair(*mine)), (slot, number + 1, *pair(*theirs))]

    pieces = both(0, 0, (f12, 0), (cc, 3)) + both(0, 2, (fx, 0), (cfx, 0))
    share, gm = mix_more(pieces + both(0, 4, (fy, 0), (cfy, 0)) + both(0, 6, (f1d, 0), (cf1d, 0)), share, gm)
    pieces = both(1, 0, (f12, 2), (cc, 5)) + both(1, 2, (fx, 2), (cfx, 2))
    share, gm = mix_more(pieces + both(1, 4, (fy, 2), (cfy, 2)), share, gm)
    x4, y4 = wait(x4, y4)

    hidden_sum = lax.psum_scatter(after(hidden_part), "batch", scatter_dimension=0, tiled=False)
    x5, y5 = across(after(y4[128:256]), 2), across(after(x4[0:128]), 4)
    cx4, cy4, cf3 = wait(*[across(after(values), 1) for values in (x4, y4, f3)])
    pieces = [(1, 6, (y4, 2), (x4, 2)), (1, 7, (cy4, 2), (cx4, 2))] + both(2, 0, (f3, 0), (cf3, 0))
    share, gm = mix_more(pieces + both(2, 2, (x4, 0), (cx4, 0)) + both(2, 4, (y4, 0), (cy4, 0)), share, gm)
    x5, y5 = wait(x5, y5)

    cx5, cy5 = wait(across(after(x5), 1), across(after(y5), 1))
    pieces = [(2, 6, (y5, 0), (x5, 0)), (2, 7, (cy5, 0), (cx5, 0))]
    share, low, part, sums = mix_more(pieces, share, gm, True)
    gjt, totals, ga = run(
        functools.partial(back_own, prefix_count),
        places, own_heads, *saved_own, small, segment_ids, low, sums, up_bias_sum,
        outer_weight.reshape(outer_weight.shape[0], -1),
    )

    def spread(values, send, bits):
        if len(bits) == 1:
            return (send(after(values), bits[0]),)
        return tuple(send(after(values), k) for k in (bits[0], bits[1], bits[0] + bits[1]))

    def gather_sum(values, others):
        others = wait(*others) if len(others) > 1 else (wait(*others),)
        total = values + others[0]
        return total + (others[1] + others[2]) if len(others) == 3 else total

    def rounds_of(send, size):
        bits = [1 << b for b in range((size - 1).bit_length())]
        return [(send, bits[k : k + 2]) for k in range(0, len(bits), 2)]

    over_batch, over_tensor = rounds_of(across, batch_size), rounds_of(along, tensor_size)
    others = spread(totals, *over_batch[0])
    per = width // batch_size
    quick = batch_size == 8
    if quick:
        keep, send = run(head_grad, places, x, low, gjt, saved_own[3])
        far_x, far_y, stay, near = run(fold, places, keep, wait(across(after(send), 1)))
        far_x, far_y = across(after(far_x), 2), across(after(far_y), 4)
    tokens_gradient, gain_sums = run(
        functools.partial(back_others, prefix_count),
        places, saved_others, extra, segment_ids, low, ga, tokens, part, row(attention_gain),
    )
    totals = gather_sum(totals, others)
    if quick:
        far_x, far_y = wait(far_x, far_y)

        def halfway(stay, near, far_x, far_y):
            return stay[0] + far_x[1], stay[1] + far_y[1], near + stack(far_x[0], far_y[0])

        top, bottom, near = run(halfway, stay, near, far_x, far_y)
        top, bottom = across(after(top), 4), across(after(bottom), 2)
    turns = over_batch[1:] + over_tensor
    for n in range(max(len(turns), len(over_batch))):
        first = spread(totals, *turns[n]) if n < len(turns) else None
        second = spread(gain_sums, *over_batch[n]) if n < len(over_batch) else None
        if n == len(over_batch) - 1:
            batch_totals = totals
        if first is not None:
            totals = gather_sum(totals, first)
        if second is not None:
            gain_sums = gather_sum(gain_sums, second)
    if quick:
        top, bottom = wait(top, bottom)
        head_sum = near + stack(top, bottom)
    else:
        both_grads = stack(
            jnp.dot(gjt, x, preferred_element_type=F32), jnp.dot(saved_own[3], low, preferred_element_type=F32)
        )
        both_grads = both_grads.reshape(-1, batch_size, per).transpose(1, 0, 2)
        head_sum = lax.psum_scatter(both_grads, "batch", scatter_dimension=0, tiled=False)
    split = 2 * PAD + 8 + hidden // local
    halves = outer_weight.shape[0] // local
    inner = totals[split : split + halves * prefix_count].reshape(halves, prefix_count, local)

    grad_prefix = batch_totals[: 2 * PAD].reshape(2, PAD, local)[:, :prefix_count]
    mixed_total = batch_totals[2 * PAD : 2 * PAD + 4]
    joint_bias_total = batch_totals[2 * PAD + 4 : 2 * PAD + 7]
    up_bias_total = batch_totals[2 * PAD + 8 : split]
    grad_hidden_prefix = inner.transpose(1, 0, 2).reshape(prefix_count, -1)
    outer_rows = outer_weight.shape[0] // batch_size
    hidden_own = lax.dynamic_slice_in_dim(hidden_prefix, lax.axis_index("batch") * outer_rows, outer_rows, 1)
    outer_total = jnp.einsum("pr,kpe->rke", hidden_own, grad_prefix, precision=PRECISE)
    outer_bias_total = jnp.sum(grad_prefix, axis=1)
    grad_inner = grad_hidden_prefix * (1.0 - hidden_prefix * hidden_prefix)
    inner_total = jnp.einsum("pd,pr->dr", prefix_table, grad_inner, precision=PRECISE)
    inner_bias_total = jnp.sum(grad_inner, axis=0)
    table_total = jnp.einsum("pr,dr->pd", grad_inner, inner_weight.astype(F32), precision=PRECISE)

    up_total, down_total = hidden_sum[:per], hidden_sum[per:].T
    joint_total = head_sum[: 3 * local].reshape(3, local, per).transpose(0, 2, 1)
    output_total = head_sum[3 * local :]
    return (
        share,
        tokens_gradient,
        gain_sums[0],
        gain_sums[1],
        joint_total,
        joint_bias_total,
        output_total,
        mixed_total[2],
        mixed_total[0],
        mixed_total[1],
        up_total,
        up_bias_total.reshape(hidden),
        down_total,
        mixed_total[3],
        table_total,
        inner_total,
        inner_bias_total,
        outer_total,
        outer_bias_total,
    )


def solution(mesh):
    placed = (
        P("batch", None),
        P("batch", None),
        P(),
        P(),
        P(None, None, "tensor"),
        P(None, "tensor"),
        P("tensor", None),
        P(),
        P(),
        P(),
        P(None, "tensor"),
        P("tensor"),
        P("tensor", None),
        P(),
        P(),
        P(),
        P(),
        P(None, None, "tensor"),
        P(None, "tensor"),
        P("batch", None),
    )
    return jax.shard_map(
        shards,
        mesh=mesh,
        in_specs=placed,
        out_specs=(
            P("batch", "tensor"),
            P("batch", "tensor"),
            P("tensor"),
            P("tensor"),
            P(None, "batch", "tensor"),
            P(None, "tensor"),
            P("tensor", "batch"),
            P("tensor"),
            P("tensor"),
            P("tensor"),
            P("batch", "tensor"),
            P("tensor"),
            P("tensor", "batch"),
            P("tensor"),
            P(),
            P(),
            P(),
            P("batch", None, "tensor"),
            P(None, "tensor"),
        ),
        check_vma=False,
    )
```
